32 devices in a mesh: dp: 4 (over y, x), section: 2 (over core), tensor: 4 (over z).
Axes of the slice: x: 2, y: 2, z: 4, core: 2. Of those that a mesh axis runs over, the one named last changes fastest.
Arguments:
- source: bfloat16 [4096, 4096], P(('dp', 'section', 'tensor')), parts along dimension 0, may hold values from -6 to 6
- enc_gain: float32 [4096], replicated, may hold values from 0.1 to 1.9
- w_gate: bfloat16 [4096, 8192], P(None, ('section', 'tensor')), may hold values from -0.09375 to 0.09375
- w_up: bfloat16 [4096, 8192], P(None, ('section', 'tensor')), may hold values from -0.09375 to 0.09375
- w_down: bfloat16 [8192, 4096], P(('section', 'tensor')), may hold values from -0.0625 to 0.0625
- enc_keep: int32 [4096, 1024], P(('dp', 'section', 'tensor')), parts along dimension 0, may hold values from 0 to 4095
- final_gain: float32 [4096], replicated, may hold values from 0.1 to 1.9
- target: bfloat16 [512, 4096], P(('dp', 'section', 'tensor')), parts along dimension 0, may hold values from -6 to 6
- self_gain: float32 [4096], replicated, may hold values from 0.1 to 1.9
- self_qkv: bfloat16 [4096, 3, 1024], P('section', None, 'tensor'), as said below
- self_out: bfloat16 [1024, 4096], P('tensor', 'section'), may hold values from -0.1875 to 0.1875
- cross_gain: float32 [4096], replicated, may hold values from 0.1 to 1.9
- cross_q: bfloat16 [4096, 1024], P('section', 'tensor'), as said below
- cross_kv: bfloat16 [4096, 2, 1024], P('section', None, 'tensor'), as said below
- cross_out: bfloat16 [1024, 4096], P('tensor', 'section'), may hold values from -0.1875 to 0.1875
- dec_keep: int32 [512, 1024], P(('dp', 'section', 'tensor')), parts along dimension 0, may hold values from 0 to 4095
Outputs:
- enc_out: bfloat16 [4096, 4096], P(('dp', 'section', 'tensor')), parts along dimension 0
- dec_out: bfloat16 [512, 4096], P(('dp', 'section', 'tensor')), parts along dimension 0
The draws below stay inside these ranges and needn't reach their ends.
There are 4 independent parts, one for each index of `dp`. The reference program is written for one: setup_inputs(seed, part) draws one part's arguments, and reference() takes and returns one part's arrays. A program takes and returns all parts, laid end to end along the dimension named above; an argument that names none is the same for every part. Nothing has to cross between parts.
Inputs may be any that keep to these rules, and one draw needn't show every extreme that they name: `self_qkv`: query weights of self-attention; independent of the keys' weights in the shown draw. `cross_q`: query weights of cross-attention. `cross_kv`: key and value weights of cross-attention.
All inputs are finite; a program needn't handle non-finite values.
Results may differ from the reference program's by a relative error of at most 0.035.
Values may be sent and summed in bfloat16 or wider, within the bound.
No kernel may reach another device: no remote copies, remote signals or barrier semaphores. Data moves between devices by JAX's collectives and lax.ppermute only.
A program may use at most 192 MiB of HBM per device.

```python
import jax
import jax.numpy as jnp
from jax import lax

D = 4096
HD = 256
FF = 8192
HEADS = 4
HK = 1024
SRC = 1024
TGT = 128
N_SECTION = 2
N_TENSOR = 4


def shared_keys(key):
    return jax.random.normal(key, (D, HK), jnp.float32) * D ** (-0.5)


def draw_self_qkv(key, part):
    key = jax.random.fold_in(key, 21)
    first, second, third = jax.random.split(key, 3)
    scale = D ** (-0.5)
    keys = jax.random.normal(second, (D, HK), jnp.float32) * scale
    values = jax.random.normal(third, (D, HK), jnp.float32) * scale
    queries = jax.random.normal(first, (D, HK), jnp.float32) * scale
    return jnp.stack([queries, keys, values], axis=1).astype(jnp.bfloat16)


def draw_cross_kv(key, part):
    keys = shared_keys(key)
    key = jax.random.fold_in(key, 22)
    values = jax.random.normal(key, (D, HK), jnp.float32) * D ** (-0.5)
    return jnp.stack([keys, values], axis=1).astype(jnp.bfloat16)


def draw_cross_q(key, part):
    key = jax.random.fold_in(key, 23)
    first = jax.random.fold_in(key, 0)
    fresh = jax.random.normal(first, (D, HK), jnp.float32) * (2.5 * D ** (-0.5))
    queries = fresh
    return queries.astype(jnp.bfloat16)


def set_ends(array, rng, low, high):
    index_at = [jax.random.randint(jax.random.fold_in(rng, axis), (), 0, length) for axis, length in enumerate(array.shape)]
    main_axis = array.shape.index(max(array.shape))
    beside = index_at[:main_axis] + [(index_at[main_axis] + 1) % array.shape[main_axis]] + index_at[main_axis + 1:]
    return array.at[tuple(index_at)].set(low).at[tuple(beside)].set(high)


def levels(own_key, extent, pieces, low, largest):
    level, own = 1.0, jax.random.fold_in(own_key, 6)
    for dim, blocks in pieces:
        draws = jnp.exp(jax.random.uniform(jax.random.fold_in(own, dim), (blocks,), jnp.float32, low / len(pieces), largest / len(pieces)))
        level = level * jnp.repeat(draws, extent[dim] // blocks).reshape([-1 if axis == dim else 1 for axis in range(len(extent))])
    return level


def scatter_about(own_key, shape, scale, most, cuts=(), held_as=jnp.bfloat16):
    entries = jax.random.normal(own_key, shape, jnp.float32) * scale
    if len(cuts) > 0:
        entries = levels(own_key, shape, cuts, -0.22, 0.18) * entries
    return jnp.clip(entries, min=-most, max=most).astype(held_as)


def setup_inputs(seed: int = 0, part: int = 0) -> dict:
    splits = jax.random.split(jax.random.key(seed), 17)
    part_splits = jax.random.split(jax.random.fold_in(splits[16], part), 17)
    source = scatter_about(part_splits[0], (SRC, D), 1.0, 6.0, ((0, 8),))
    enc_gain = jnp.clip(1.0 + 0.18 * jax.random.normal(splits[1], (D,), jnp.float32), 0.1, 1.9)
    w_gate = scatter_about(splits[2], (D, FF), D ** -0.5, 0.09375, ((1, 8),))
    w_up = scatter_about(splits[3], (D, FF), D ** -0.5, 0.09375, ((1, 8),))
    w_down = scatter_about(splits[4], (FF, D), FF ** -0.5, 0.0625, ((0, 8),))
    enc_keep = set_ends(jax.random.randint(part_splits[5], (SRC, D // 4), 0, 4096), jax.random.fold_in(part_splits[5], 1), 0, 4095).astype(jnp.int32)
    final_gain = jnp.clip(1.0 + 0.18 * jax.random.normal(splits[6], (D,), jnp.float32), 0.1, 1.9)
    target = scatter_about(part_splits[7], (TGT, D), 1.0, 6.0, ((0, 8),))
    self_gain = jnp.clip(1.0 + 0.18 * jax.random.normal(splits[8], (D,), jnp.float32), 0.1, 1.9)
    self_qkv = draw_self_qkv(jax.random.fold_in(splits[16], 71), part)
    self_out = scatter_about(splits[10], (HK, D), HK ** -0.5, 0.1875, ((0, 4), (1, 2)))
    cross_gain = jnp.clip(1.0 + 0.18 * jax.random.normal(splits[11], (D,), jnp.float32), 0.1, 1.9)
    cross_q = draw_cross_q(jax.random.fold_in(splits[16], 71), part)
    cross_kv = draw_cross_kv(jax.random.fold_in(splits[16], 71), part)
    cross_out = scatter_about(splits[14], (HK, D), HK ** -0.5, 0.1875, ((0, 4), (1, 2)))
    dec_keep = set_ends(jax.random.randint(part_splits[15], (TGT, D // 4), 0, 4096), jax.random.fold_in(part_splits[15], 1), 0, 4095).astype(jnp.int32)
    return {"source": source, "enc_gain": enc_gain, "w_gate": w_gate, "w_up": w_up, "w_down": w_down, "enc_keep": enc_keep, "final_gain": final_gain, "target": target, "self_gain": self_gain, "self_qkv": self_qkv, "self_out": self_out, "cross_gain": cross_gain, "cross_q": cross_q, "cross_kv": cross_kv, "cross_out": cross_out, "dec_keep": dec_keep}


def norm_rows(x, gain):
    values = x.astype(jnp.float32)
    power = lax.optimization_barrier(jnp.mean(values * values, axis=-1, keepdims=True))
    return values * lax.rsqrt(power + 1e-06) * gain

def keep_factor(words):
    shifts = jnp.arange(4, dtype=jnp.int32) * 3
    bits = jnp.right_shift(words[:, None, :], shifts[None, :, None]) & 7
    kept = jnp.where(bits == 7, 0.0, 8.0 / 7.0).astype(jnp.float32)
    return kept.reshape(words.shape[0], 4 * words.shape[1])

def attend(query, keys, values, allowed):
    rows = query.shape[0]
    count = keys.shape[0]
    qh = query.reshape(rows, HEADS, HD).astype(jnp.float32)
    kh = keys.reshape(count, HEADS, HD).astype(jnp.float32)
    vh = values.reshape(count, HEADS, HD).astype(jnp.float32)
    scores = jnp.einsum('rhd,khd->hrk', qh, kh) / jnp.sqrt(jnp.float32(HD))
    if allowed is not None:
        scores = jnp.where(allowed[None], scores, jnp.float32(-1e+30))
    top = lax.optimization_barrier(jnp.max(scores, axis=-1, keepdims=True))
    expo = jnp.exp(scores - top)
    probs = (expo / lax.optimization_barrier(jnp.sum(expo, axis=-1, keepdims=True))).astype(jnp.bfloat16)
    context = jnp.einsum('hrk,khd->rhd', probs.astype(jnp.float32), vh)
    return context.reshape(rows, HEADS * HD).astype(jnp.bfloat16)

def block_sum(left, right, groups):
    width = left.shape[1] // groups

    def add_block(total, index):
        piece = lax.dynamic_slice_in_dim(left, index * width, width, 1)
        rows = lax.dynamic_slice_in_dim(right, index * width, width, 0)
        term = jnp.dot(piece, rows, preferred_element_type=jnp.float32).astype(jnp.bfloat16)
        term = lax.optimization_barrier(term)
        return (total + term.astype(jnp.float32), None)
    start = jnp.zeros((left.shape[0], right.shape[1]), jnp.float32)
    total, unused = lax.scan(add_block, start, jnp.arange(groups, dtype=jnp.int32))
    return total

def reference(source, enc_gain, w_gate, w_up, w_down, enc_keep, final_gain, target, self_gain, self_qkv, self_out, cross_gain, cross_q, cross_kv, cross_out, dec_keep):
    normed = norm_rows(source, enc_gain).astype(jnp.bfloat16)
    gate = jnp.dot(normed, w_gate, preferred_element_type=jnp.float32)
    up = jnp.dot(normed, w_up, preferred_element_type=jnp.float32)
    hidden = (jax.nn.gelu(gate, approximate=True) * up).astype(jnp.bfloat16)
    ffn = block_sum(hidden, w_down, N_SECTION * N_TENSOR)
    enc_out = (source.astype(jnp.float32) + keep_factor(enc_keep) * ffn).astype(jnp.bfloat16)
    memory = norm_rows(enc_out, final_gain).astype(jnp.bfloat16)
    selfin = norm_rows(target, self_gain).astype(jnp.bfloat16)
    qkv = jnp.dot(selfin, self_qkv.reshape(D, 3 * HK), preferred_element_type=jnp.float32).astype(jnp.bfloat16)
    qkv = qkv.reshape(TGT, 3, HK)
    positions = jnp.arange(TGT, dtype=jnp.int32)
    causal = positions[None, :] <= positions[:, None]
    selfctx = attend(qkv[:, 0], qkv[:, 1], qkv[:, 2], causal)
    selfsum = block_sum(selfctx, self_out, N_TENSOR)
    mid = (target.astype(jnp.float32) + selfsum).astype(jnp.bfloat16)
    crossin = norm_rows(mid, cross_gain).astype(jnp.bfloat16)
    cq = jnp.dot(crossin, cross_q, preferred_element_type=jnp.float32).astype(jnp.bfloat16)
    ckv = jnp.dot(memory, cross_kv.reshape(D, 2 * HK), preferred_element_type=jnp.float32).astype(jnp.bfloat16)
    ckv = ckv.reshape(SRC, 2, HK)
    crossctx = attend(cq, ckv[:, 0], ckv[:, 1], None)
    crosssum = block_sum(crossctx, cross_out, N_TENSOR)
    dec_out = (mid.astype(jnp.float32) + keep_factor(dec_keep) * crosssum).astype(jnp.bfloat16)
    return (enc_out, dec_out)
```

```python
import functools

import jax
import jax.numpy as jnp
from jax import lax
from jax.experimental import pallas as pl
from jax.experimental.pallas import tpu as pltpu
from jax.sharding import PartitionSpec as P

HD = 256
F32 = jnp.float32
BF16 = jnp.bfloat16
CHUNKS = 2
STATS = 5


def norm_rows(x, gain):
    values = x.astype(F32)
    power = jnp.mean(values * values, axis=-1, keepdims=True)
    return values * lax.rsqrt(power + 1e-06) * gain


def keep_factor(words):
    shifts = jnp.arange(4, dtype=jnp.int32) * 3
    bits = jnp.right_shift(words[:, None, :], shifts[None, :, None]) & 7
    kept = jnp.where(bits == 7, 0.0, 8.0 / 7.0).astype(F32)
    return kept.reshape(words.shape[0], 4 * words.shape[1])


def swap_section(value):
    return lax.ppermute(value, "section", [(0, 1), (1, 0)])


def from_slots(value, count):
    return [value] + [
        lax.ppermute(value, "tensor", [(i, (i - o) % count) for i in range(count)]) for o in range(1, count)
    ]


def half_columns(value, index):
    return lax.dynamic_slice_in_dim(value, index * (value.shape[1] // 2), value.shape[1] // 2, 1)


def gather_half(rows, section, count):
    own = half_columns(rows, section)
    other = swap_section(half_columns(rows, 1 - section))
    pair = jnp.where(section == 0, jnp.concatenate([own, other], 0), jnp.concatenate([other, own], 0))
    return jnp.concatenate(from_slots(pair, count), 0)


def both_halves(partial):
    return partial + swap_section(partial)


def ffn_part(x, w_gate, w_up, w_down, section, tensor, count):
    gate = jnp.dot(x, w_gate, preferred_element_type=F32)
    up = jnp.dot(x, w_up, preferred_element_type=F32)
    hidden = (jax.nn.gelu(gate, approximate=True) * up).astype(BF16)
    rows = hidden.shape[0] // 2
    block = rows // count
    theirs = lax.dynamic_slice_in_dim(hidden, (1 - section) * rows, rows, 0)
    got = swap_section(jnp.dot(theirs, w_down, preferred_element_type=F32).astype(BF16))
    ours = lax.dynamic_slice_in_dim(hidden, section * rows, rows, 0)
    mine = jnp.dot(ours, w_down, preferred_element_type=F32).astype(BF16)

    def part(slot):
        at = lax.rem(tensor + slot, count) * block
        return lax.dynamic_slice_in_dim(mine, at, block, 0).astype(F32) + lax.dynamic_slice_in_dim(
            got, at, block, 0
        ).astype(F32)

    above, below = None, None
    for step in range(1, count):
        send_up, send_down = part(count - step), part(step)
        if step > 1:
            send_up = send_up + above.astype(F32)
            send_down = send_down + below.astype(F32)
        above = lax.ppermute(send_up.astype(BF16), "tensor", [(i, i + 1) for i in range(step)])
        below = lax.ppermute(
            send_down.astype(BF16), "tensor", [(i, i - 1) for i in range(count - step, count)]
        )
    return part(0) + above.astype(F32) + below.astype(F32)


def attend_kernel(steps, mem_ref, w_ref, cq_ref, out_ref, keys, values):
    head, step = pl.program_id(0), pl.program_id(1)
    depth = w_ref.shape[4]
    total_k = jnp.zeros(keys.shape, F32)
    total_v = jnp.zeros(values.shape, F32)
    for g in range(w_ref.shape[0]):
        x = mem_ref[:, g * depth : (g + 1) * depth]
        total_k += jnp.dot(x, w_ref[g, 0, 0, 0], preferred_element_type=F32)
        total_v += jnp.dot(x, w_ref[g, 0, 0, 1], preferred_element_type=F32)

    @pl.when(step == 0)
    def _():
        keys[...] = total_k
        values[...] = total_v

    @pl.when(step > 0)
    def _():
        keys[...] += total_k
        values[...] += total_v

    @pl.when(step == steps - 1)
    def _():
        k, v = keys[...].astype(BF16), values[...].astype(BF16)
        scores = lax.dot_general(cq_ref[0], k, (((1,), (1,)), ((), ())), preferred_element_type=F32)
        scores = scores * (1.0 / 16.0)
        top = jnp.max(scores, axis=-1, keepdims=True)
        expo = jnp.exp(scores - top)
        total = jnp.sum(expo, axis=-1, keepdims=True)
        context = jnp.dot(expo.astype(BF16), v, preferred_element_type=F32)
        out_ref[:, pl.ds(pl.multiple_of(head * HD, HD), HD)] = context.astype(BF16)
        lanes = lax.broadcasted_iota(jnp.int32, (scores.shape[0], 128), 1) - head * STATS
        base = out_ref.shape[1] - 128
        high = top.astype(BF16).astype(F32)
        rest = top - high
        middle = rest.astype(BF16).astype(F32)
        low = rest - middle
        sum_high = total.astype(BF16).astype(F32)
        sum_low = total - sum_high
        stats = jnp.where(head == 0, jnp.zeros(lanes.shape, F32), out_ref[:, base:].astype(F32))
        for index, piece in enumerate((high, middle, low, sum_high, sum_low)):
            stats = jnp.where(lanes == index, piece, stats)
        out_ref[:, base:] = stats.astype(BF16)


def attend_own_keys(memory, weights, queries):
    dp, sections, heads, two, depth, width = weights.shape
    rows, features = memory.shape
    count = queries.shape[1]
    return pl.pallas_call(
        functools.partial(attend_kernel, sections),
        grid=(heads, sections),
        in_specs=[
            pl.BlockSpec((rows, features // sections), lambda h, s: (0, s)),
            pl.BlockSpec((dp, 1, 1, two, depth, width), lambda h, s: (0, s, h, 0, 0, 0)),
            pl.BlockSpec((1, count, width), lambda h, s: (h, 0, 0)),
        ],
        out_specs=pl.BlockSpec((count, heads * width + 128), lambda h, s: (0, 0)),
        out_shape=jax.ShapeDtypeStruct((count, heads * width + 128), BF16),
        scratch_shapes=[pltpu.VMEM((rows, width), F32), pltpu.VMEM((rows, width), F32)],
        compiler_params=pltpu.CompilerParams(vmem_limit_bytes=32 * 2**20),
        cost_estimate=pl.CostEstimate(
            flops=4 * rows * features * heads * width, bytes_accessed=2 * weights.size, transcendentals=0
        ),
        name="attend_own_keys",
    )(memory, weights, queries)


def finish(parts, weights, mid, words):
    dp, sections, heads, width, tile = weights.shape
    rows, features = mid.shape
    sources = parts.shape[0]
    per_word = words.shape[1] // tile

    def kernel(parts_ref, w_ref, mid_ref, words_ref, out_ref, context):
        finish_body(heads, words.shape[1], parts_ref, w_ref, mid_ref, words_ref, out_ref, context)

    return pl.pallas_call(
        kernel,
        grid=(sections, dp),
        in_specs=[
            pl.BlockSpec(parts.shape, lambda s, g: (0, 0, 0)),
            pl.BlockSpec((1, 1, heads, width, tile), lambda s, g: (g, s, 0, 0, 0)),
            pl.BlockSpec((rows, tile), lambda s, g: (0, s * dp + g)),
            pl.BlockSpec((rows, tile), lambda s, g: (0, lax.rem(s * dp + g, per_word))),
        ],
        out_specs=pl.BlockSpec((rows, tile), lambda s, g: (0, s * dp + g)),
        out_shape=jax.ShapeDtypeStruct((rows, features), BF16),
        scratch_shapes=[pltpu.VMEM((rows, heads * width), BF16)],
        compiler_params=pltpu.CompilerParams(vmem_limit_bytes=32 * 2**20),
        cost_estimate=pl.CostEstimate(
            flops=2 * rows * features * heads * width, bytes_accessed=2 * weights.size, transcendentals=0
        ),
        name="finish",
    )(parts, weights, mid, words)


def finish_body(heads, words_width, parts_ref, w_ref, mid_ref, words_ref, out_ref, context):
    tile = out_ref.shape[1]
    index = pl.program_id(0) * pl.num_programs(1) + pl.program_id(1)

    @pl.when(index == 0)
    def _():
        base = heads * HD
        stat = parts_ref[:, :, base:].astype(F32)
        for head in range(heads):
            at = head * STATS
            top = stat[:, :, at : at + 1] + stat[:, :, at + 1 : at + 2] + stat[:, :, at + 2 : at + 3]
            total = stat[:, :, at + 3 : at + 4] + stat[:, :, at + 4 : at + 5]
            most = jnp.max(top, axis=0, keepdims=True)
            weight = jnp.exp(top - most)
            whole = jnp.sum(weight * total, axis=0)
            part = parts_ref[:, :, head * HD : (head + 1) * HD].astype(F32)
            context[:, head * HD : (head + 1) * HD] = (jnp.sum(part * weight, axis=0) / whole).astype(BF16)

    w = w_ref[0, 0].reshape(heads * HD, tile)
    total = jnp.dot(context[...], w, preferred_element_type=F32)
    shift = 3 * (index // (words_width // tile))
    bits = lax.shift_right_logical(words_ref[...], jnp.broadcast_to(shift, words_ref.shape)) & 7
    kept = jnp.where(bits == 7, 0.0, 8.0 / 7.0).astype(F32)
    out_ref[...] = (mid_ref[...].astype(F32) + kept * total).astype(BF16)


def per_device(
    source,
    enc_gain,
    w_gate,
    w_up,
    w_down,
    enc_keep,
    final_gain,
    target,
    self_gain,
    self_qkv,
    self_out,
    cross_gain,
    cross_q,
    cross_kv,
    cross_out,
    dec_keep,
):
    count, groups = lax.axis_size("tensor"), lax.axis_size("dp")
    section, tensor, group = lax.axis_index("section"), lax.axis_index("tensor"), lax.axis_index("dp")
    devices = 2 * count

    normed = norm_rows(source, enc_gain).astype(BF16)
    block = normed.shape[0] // CHUNKS
    gathered = [
        lax.all_gather(normed[c * block : (c + 1) * block], ("section", "tensor"), axis=0, tiled=True)
        for c in range(CHUNKS)
    ]

    depth = cross_kv.shape[0] // groups
    kv_share = lax.dynamic_slice_in_dim(jnp.transpose(cross_kv, (1, 0, 2)), group * depth, depth, 1)
    kv_all = lax.all_gather(kv_share, ("dp", "section", "tensor"), axis=0, tiled=False)
    kv_all = kv_all.reshape((groups, 2, count) + kv_share.shape)
    tile = cross_out.shape[1] // groups
    out_share = lax.dynamic_slice_in_dim(cross_out, group * tile, tile, 1)
    out_all = lax.all_gather(out_share, ("dp", "section", "tensor"), axis=0, tiled=False)
    out_all = out_all.reshape((groups, 2, count) + out_share.shape)

    rows = target.shape[0]
    selfin = norm_rows(target, self_gain).astype(BF16)
    x = gather_half(selfin, section, count)
    qkv_w = jnp.transpose(self_qkv, (1, 0, 2))
    q, k, v = [jnp.dot(x, qkv_w[i], preferred_element_type=F32) for i in range(3)]
    q, k, v = [y.astype(BF16) for y in both_halves(jnp.stack([q, k, v]))]
    slot_chip = lax.rem(tensor + jnp.arange(count, dtype=jnp.int32), count)
    positions = (
        (jnp.arange(2, dtype=jnp.int32)[None, :] * count + slot_chip[:, None])[:, :, None] * rows
        + jnp.arange(rows, dtype=jnp.int32)
    ).reshape(-1)
    scores = lax.dot_general(q, k, (((1,), (1,)), ((), ())), preferred_element_type=F32) * (1.0 / 16.0)
    scores = jnp.where(positions[None, :] <= positions[:, None], scores, F32(-1e30))
    expo = jnp.exp(scores - jnp.max(scores, axis=-1, keepdims=True))
    probs = (expo / jnp.sum(expo, axis=-1, keepdims=True)).astype(BF16)
    context = jnp.dot(probs, v, preferred_element_type=F32).astype(BF16)
    product = jnp.dot(context, self_out, preferred_element_type=F32).astype(BF16)
    product = product.reshape(count, 2 * rows, product.shape[1])
    total = product[0].astype(F32)
    for o in range(1, count):
        total = total + lax.ppermute(
            product[o], "tensor", [(i, (i + o) % count) for i in range(count)]
        ).astype(F32)
    own = lax.dynamic_slice_in_dim(total, section * rows, rows, 0)
    other = swap_section(lax.dynamic_slice_in_dim(total, (1 - section) * rows, rows, 0))
    selfsum = jnp.where(section == 0, jnp.concatenate([own, other], 1), jnp.concatenate([other, own], 1))
    mid = (target.astype(F32) + selfsum).astype(BF16)

    crossin = norm_rows(mid, cross_gain).astype(BF16)
    x = gather_half(crossin, section, count)
    cq = both_halves(jnp.dot(x, cross_q, preferred_element_type=F32)).astype(BF16)
    cq = jnp.roll(cq.reshape(count, 2, rows, HD), tensor, axis=0)
    cq = jnp.transpose(cq, (1, 0, 2, 3)).reshape(devices * rows, HD)
    queries = jnp.roll(jnp.stack(from_slots(cq, count)), tensor, axis=0)

    ffn = jnp.concatenate(
        [ffn_part(x, w_gate, w_up, w_down, section, tensor, count) for x in gathered], 0
    )
    enc_out = (source.astype(F32) + keep_factor(enc_keep) * ffn).astype(BF16)
    memory = norm_rows(enc_out, final_gain).astype(BF16)

    parts = attend_own_keys(memory, kv_all, queries)
    parts = parts.reshape(devices, rows, parts.shape[1])
    parts = lax.all_to_all(parts, ("section", "tensor"), split_axis=0, concat_axis=0, tiled=True)
    dec_out = finish(parts, out_all, mid, dec_keep)
    return (enc_out, dec_out)


def solution(mesh):
    return jax.shard_map(
        per_device,
        mesh=mesh,
        in_specs=(
            P(("dp", "section", "tensor"), None),
            P(),
            P(None, ("section", "tensor")),
            P(None, ("section", "tensor")),
            P(("section", "tensor"), None),
            P(("dp", "section", "tensor"), None),
            P(),
            P(("dp", "section", "tensor"), None),
            P(),
            P("section", None, "tensor"),
            P("tensor", "section"),
            P(),
            P("section", "tensor"),
            P("section", None, "tensor"),
            P("tensor", "section"),
            P(("dp", "section", "tensor"), None),
        ),
        out_specs=(P(("dp", "section", "tensor"), None), P(("dp", "section", "tensor"), None)),
        check_vma=False,
    )
```

```python
import functools

import jax
import jax.numpy as jnp
from jax import lax
from jax.experimental import pallas as pl
from jax.experimental.pallas import tpu as pltpu
from jax.sharding import PartitionSpec as P

HD = 256
F32 = jnp.float32
BF16 = jnp.bfloat16
CHUNKS = 2
STATS = 5


def norm_rows(x, gain):
    values = x.astype(F32)
    power = jnp.mean(values * values, axis=-1, keepdims=True)
    return values * lax.rsqrt(power + 1e-06) * gain


def keep_factor(words):
    shifts = jnp.arange(4, dtype=jnp.int32) * 3
    bits = jnp.right_shift(words[:, None, :], shifts[None, :, None]) & 7
    kept = jnp.where(bits == 7, 0.0, 8.0 / 7.0).astype(F32)
    return kept.reshape(words.shape[0], 4 * words.shape[1])


def swap(value, axis, distance):
    return lax.ppermute(value, axis, [(i, i ^ distance) for i in range(lax.axis_size(axis))])


def near_bits(axis):
    bits, bit = [], 1
    while bit < lax.axis_size(axis):
        bits.append(bit)
        bit *= 2
    return bits


def slot_order(bits):
    order = [0]
    for bit in bits:
        order = order + [m ^ bit for m in order]
    return order


def gather_swaps(value, axis, bits):
    for bit in bits:
        value = jnp.concatenate([value, swap(value, axis, bit)], 0)
    return value


def sum_swaps(value, axis, bits, sent):
    for bit in bits[::-1]:
        half = value.shape[0] // 2
        value = value[:half] + swap(value[half:].astype(sent), axis, bit).astype(F32)
    return value


def half_columns(value, index):
    return lax.dynamic_slice_in_dim(value, index * (value.shape[1] // 2), value.shape[1] // 2, 1)


def gather_half(rows, section, bits):
    own = half_columns(rows, section)
    other = swap(half_columns(rows, 1 - section), "section", 1)
    pair = jnp.where(section == 0, jnp.concatenate([own, other], 0), jnp.concatenate([other, own], 0))
    return gather_swaps(pair, "tensor", bits)


def both_halves(partial):
    return partial + swap(partial, "section", 1)


def gelu(x):
    return 0.5 * x * (1.0 + jnp.tanh(0.7978845608028654 * (x + 0.044715 * x * x * x)))


def ffn_kernel(hidden_steps, xa_ref, xb_ref, gate_ref, up_ref, down_ref, ya_ref, yb_ref, hidden):
    step = pl.program_id(0)
    rows = xa_ref.shape[0]
    width = gate_ref.shape[1]

    @pl.when(step < hidden_steps)
    def _():
        for i, x_ref in enumerate((xa_ref, xb_ref)):
            gate = jnp.dot(x_ref[...], gate_ref[...], preferred_element_type=F32)
            up = jnp.dot(x_ref[...], up_ref[...], preferred_element_type=F32)
            hidden[step, i * rows : (i + 1) * rows, :] = (gelu(gate) * up).astype(BF16)

    @pl.when(step >= hidden_steps)
    def _():
        total = jnp.zeros((2 * rows, ya_ref.shape[1]), F32)
        for k in range(hidden.shape[0]):
            total += jnp.dot(
                hidden[k], down_ref[k * width : (k + 1) * width, :], preferred_element_type=F32
            )
        ya_ref[...] = total[:rows].astype(BF16)
        yb_ref[...] = total[rows:].astype(BF16)


def ffn(xa, xb, w_gate, w_up, w_down):
    rows, features = xa.shape
    units = w_gate.shape[1]
    width = min(256, units)
    tile = 512
    first, last = units // width, features // tile
    return pl.pallas_call(
        functools.partial(ffn_kernel, first),
        grid=(first + last,),
        in_specs=[
            pl.BlockSpec((rows, features), lambda i: (0, 0)),
            pl.BlockSpec((rows, features), lambda i: (0, 0)),
            pl.BlockSpec((features, width), lambda i: (0, jnp.minimum(i, first - 1))),
            pl.BlockSpec((features, width), lambda i: (0, jnp.minimum(i, first - 1))),
            pl.BlockSpec((units, tile), lambda i: (0, jnp.maximum(i - first, 0))),
        ],
        out_specs=[pl.BlockSpec((rows, tile), lambda i: (0, jnp.maximum(i - first, 0)))] * 2,
        out_shape=[jax.ShapeDtypeStruct((rows, features), BF16)] * 2,
        scratch_shapes=[pltpu.VMEM((first, 2 * rows, width), BF16)],
        compiler_params=pltpu.CompilerParams(vmem_limit_bytes=48 * 2**20),
        cost_estimate=pl.CostEstimate(
            flops=12 * rows * features * units, bytes_accessed=6 * features * units, transcendentals=0
        ),
        name="ffn",
    )(xa, xb, w_gate, w_up, w_down)


def attend_kernel(
    heads, table, ids, mem_ref, a0_ref, a1_ref, b0_ref, b1_ref, cq_ref, out_ref
):
    slot = pl.program_id(0)
    head = ids[slot]
    groups, depth = a0_ref.shape[0], a0_ref.shape[3]

    def attend(own_ref, other_ref, row):
        keys = jnp.zeros((mem_ref.shape[0], HD), F32)
        values = jnp.zeros((mem_ref.shape[0], HD), F32)
        for place, ref in enumerate((own_ref, other_ref)):
            for i in range(groups):
                at = pl.multiple_of(table[row + place, i] * depth, depth)
                x = mem_ref[:, pl.ds(at, depth)]
                keys += jnp.dot(x, ref[i, 0, 0], preferred_element_type=F32)
                values += jnp.dot(x, ref[i, 0, 1], preferred_element_type=F32)
        k, v = keys.astype(BF16), values.astype(BF16)
        scores = lax.dot_general(cq_ref[0], k, (((1,), (1,)), ((), ())), preferred_element_type=F32)
        scores = scores * (1.0 / 16.0)
        top = jnp.max(scores, axis=-1, keepdims=True)
        expo = jnp.exp(scores - top)
        total = jnp.sum(expo, axis=-1, keepdims=True)
        context = jnp.dot(expo.astype(BF16), v, preferred_element_type=F32)
        out_ref[:, pl.ds(pl.multiple_of(head * HD, HD), HD)] = context.astype(BF16)
        lanes = lax.broadcasted_iota(jnp.int32, (scores.shape[0], 128), 1) - head * STATS
        base = heads * HD
        high = top.astype(BF16).astype(F32)
        rest = top - high
        middle = rest.astype(BF16).astype(F32)
        low = rest - middle
        sum_high = total.astype(BF16).astype(F32)
        sum_low = total - sum_high
        stats = jnp.where(slot == 0, jnp.zeros(lanes.shape, F32), out_ref[:, base:].astype(F32))
        for index, piece in enumerate((high, middle, low, sum_high, sum_low)):
            stats = jnp.where(lanes == index, piece, stats)
        out_ref[:, base:] = stats.astype(BF16)

    @pl.when(slot < heads // 2)
    def _():
        attend(a0_ref, a1_ref, 0)

    @pl.when(slot >= heads // 2)
    def _():
        attend(b0_ref, b1_ref, 2)


def attend_own_keys(memory, weights, queries, table, ids):
    rows, features = memory.shape
    heads, count, width = queries.shape
    groups, half, _, depth, _ = weights[0].shape
    block = (groups, 1, 2, depth, width)
    first = pl.BlockSpec(block, lambda h, t, n: (0, jnp.minimum(h, half - 1), 0, 0, 0))
    second = pl.BlockSpec(block, lambda h, t, n: (0, jnp.maximum(h - half, 0), 0, 0, 0))
    return pl.pallas_call(
        functools.partial(attend_kernel, heads),
        grid_spec=pltpu.PrefetchScalarGridSpec(
            num_scalar_prefetch=2,
            grid=(heads,),
            in_specs=[
                pl.BlockSpec((rows, features), lambda h, t, n: (0, 0)),
                first,
                first,
                second,
                second,
                pl.BlockSpec((1, count, width), lambda h, t, n: (h, 0, 0)),
            ],
            out_specs=pl.BlockSpec((count, heads * width + 128), lambda h, t, n: (0, 0)),
        ),
        out_shape=jax.ShapeDtypeStruct((count, heads * width + 128), BF16),
        compiler_params=pltpu.CompilerParams(vmem_limit_bytes=40 * 2**20),
        cost_estimate=pl.CostEstimate(
            flops=4 * rows * features * heads * width,
            bytes_accessed=4 * features * heads * width,
            transcendentals=0,
        ),
        name="attend_own_keys",
    )(table, ids, memory, *weights, queries)


def finish_kernel(
    heads, words_width, table, ids, parts_ref, a0_ref, a1_ref, b0_ref, b1_ref, mid_ref, words_ref, out_ref, context
):
    place, step = pl.program_id(0), pl.program_id(1)
    tile = out_ref.shape[1]
    index = table[place, step]

    @pl.when((place == 0) & (step == 0))
    def _():
        stat = parts_ref[:, :, heads * HD :].astype(F32)
        lanes = lax.broadcasted_iota(jnp.int32, stat.shape, 2)
        for slot in range(heads):
            head = ids[slot]
            pick = [
                jnp.sum(jnp.where(lanes == head * STATS + j, stat, 0.0), axis=-1, keepdims=True)
                for j in range(STATS)
            ]
            top = pick[0] + pick[1] + pick[2]
            weight = jnp.exp(top - jnp.max(top, axis=0, keepdims=True))
            whole = jnp.sum(weight * (pick[3] + pick[4]), axis=0)
            part = parts_ref[:, :, pl.ds(pl.multiple_of(head * HD, HD), HD)].astype(F32)
            context[:, slot * HD : (slot + 1) * HD] = (jnp.sum(part * weight, axis=0) / whole).astype(BF16)

    def columns(a_ref, b_ref):
        half = heads * HD // 2
        for u in range(tile // HD):
            cut = slice(u * HD, (u + 1) * HD)
            wa = a_ref[0, :, 0, cut, :].reshape(half, HD)
            wb = b_ref[0, :, 0, cut, :].reshape(half, HD)
            total = jnp.dot(context[:, :half], wa, preferred_element_type=F32)
            total += jnp.dot(context[:, half:], wb, preferred_element_type=F32)
            words = words_ref[:, cut]
            shift = 3 * (index // (words_width // tile))
            bits = lax.shift_right_logical(words, jnp.broadcast_to(shift, words.shape)) & 7
            kept = jnp.where(bits == 7, 0.0, 8.0 / 7.0).astype(F32)
            out_ref[:, cut] = (mid_ref[:, cut].astype(F32) + kept * total).astype(BF16)

    @pl.when(place == 0)
    def _():
        columns(a0_ref, b0_ref)

    @pl.when(place == 1)
    def _():
        columns(a1_ref, b1_ref)


def finish(parts, weights, mid, words, table, ids):
    groups, half, _, depth, width = weights[0].shape
    heads = 2 * half
    rows, features = mid.shape
    per_word = words.shape[1] // depth
    block = (1, half, 1, depth, width)
    bits = []
    while 1 << len(bits) < groups:
        bits.append(len(bits))
    top = len(bits) - 1

    def reverse(i):
        out = 0
        for b in bits:
            out = out + ((i >> b) & 1) * (1 << (top - b))
        return out

    def a_own(p, i, t, n):
        return (jnp.where(p == 0, i, groups - 1), 0, 2, 0, 0)

    def a_other(p, i, t, n):
        return (jnp.where(p == 0, 0, i), 0, 2, 0, 0)

    def b_own(p, i, t, n):
        return (reverse(jnp.where(p == 0, i, groups - 1)), 0, 2, 0, 0)

    def b_other(p, i, t, n):
        return (reverse(jnp.where(p == 0, 0, i)), 0, 2, 0, 0)

    return pl.pallas_call(
        functools.partial(finish_kernel, heads, words.shape[1]),
        grid_spec=pltpu.PrefetchScalarGridSpec(
            num_scalar_prefetch=2,
            grid=(2, groups),
            in_specs=[
                pl.BlockSpec(parts.shape, lambda p, i, t, n: (0, 0, 0)),
                pl.BlockSpec(block, a_own),
                pl.BlockSpec(block, a_other),
                pl.BlockSpec(block, b_own),
                pl.BlockSpec(block, b_other),
                pl.BlockSpec((rows, depth), lambda p, i, t, n: (0, t[p, i])),
                pl.BlockSpec((rows, depth), lambda p, i, t, n: (0, lax.rem(t[p, i], per_word))),
            ],
            out_specs=pl.BlockSpec((rows, depth), lambda p, i, t, n: (0, t[p, i])),
            scratch_shapes=[pltpu.VMEM((rows, heads * width), BF16)],
        ),
        out_shape=jax.ShapeDtypeStruct((rows, features), BF16),
        compiler_params=pltpu.CompilerParams(vmem_limit_bytes=32 * 2**20),
        cost_estimate=pl.CostEstimate(
            flops=2 * rows * features * heads * width,
            bytes_accessed=2 * features * heads * width,
            transcendentals=0,
        ),
        name="finish",
    )(table, ids, parts, *weights, mid, words)


def per_device(
    source,
    enc_gain,
    w_gate,
    w_up,
    w_down,
    enc_keep,
    final_gain,
    target,
    self_gain,
    self_qkv,
    self_out,
    cross_gain,
    cross_q,
    cross_kv,
    cross_out,
    dec_keep,
):
    count, groups = lax.axis_size("tensor"), lax.axis_size("dp")
    section, tensor, group = lax.axis_index("section"), lax.axis_index("tensor"), lax.axis_index("dp")
    devices = 2 * count
    bits = near_bits("tensor")[::-1]
    order = slot_order(bits)
    rows = target.shape[0]
    after = lax.optimization_barrier

    normed = norm_rows(source, enc_gain).astype(BF16)
    block = normed.shape[0] // CHUNKS
    near = [gather_swaps(normed[c * block : (c + 1) * block], "tensor", bits) for c in range(CHUNKS)]
    far = [swap(x, "section", 1) for x in near]

    selfin = norm_rows(target, self_gain).astype(BF16)
    x = gather_half(selfin, section, bits)
    qkv_w = jnp.transpose(self_qkv, (1, 0, 2))
    q, k, v = [jnp.dot(x, qkv_w[i], preferred_element_type=F32) for i in range(3)]
    q, k, v = [y.astype(BF16) for y in both_halves(jnp.stack([q, k, v]))]
    slot_chip = jnp.stack([tensor ^ m for m in order])
    positions = (
        (jnp.arange(2, dtype=jnp.int32)[None, :] * count + slot_chip[:, None])[:, :, None] * rows
        + jnp.arange(rows, dtype=jnp.int32)
    ).reshape(-1)
    scores = lax.dot_general(q, k, (((1,), (1,)), ((), ())), preferred_element_type=F32) * (1.0 / 16.0)
    scores = jnp.where(positions[None, :] <= positions[:, None], scores, F32(-1e30))
    expo = jnp.exp(scores - jnp.max(scores, axis=-1, keepdims=True))
    probs = (expo / jnp.sum(expo, axis=-1, keepdims=True)).astype(BF16)
    context = jnp.dot(probs, v, preferred_element_type=F32).astype(BF16)
    product = jnp.dot(context, self_out, preferred_element_type=F32).astype(BF16).astype(F32)
    total = sum_swaps(product, "tensor", bits, BF16)
    own = lax.dynamic_slice_in_dim(total, section * rows, rows, 0)
    other = swap(lax.dynamic_slice_in_dim(total, (1 - section) * rows, rows, 0), "section", 1)
    selfsum = jnp.where(section == 0, jnp.concatenate([own, other], 1), jnp.concatenate([other, own], 1))
    mid = (target.astype(F32) + selfsum).astype(BF16)

    shares = [ffn(near[0], far[0], w_gate, w_up, w_down)]

    depth = cross_kv.shape[0] // groups
    kv_share = lax.dynamic_slice_in_dim(jnp.transpose(cross_kv, (1, 0, 2)), group * depth, depth, 1)
    out_share = lax.dynamic_slice_in_dim(cross_out, group * depth, depth, 1)
    out_share = jnp.transpose(out_share.reshape(HD, depth // HD, HD), (1, 0, 2)).reshape(1, depth, HD)
    share = jnp.concatenate([kv_share, out_share], 0)[None]
    share, near[0] = after((share, near[0]))
    share = gather_swaps(share, "tensor", bits)
    dp_bits = near_bits("dp")
    weights, table = [], []
    for piece, way in ((share[: count // 2], dp_bits), (share[count // 2 :], dp_bits[::-1])):
        own = gather_swaps(piece[None], "dp", way)
        weights += [own, swap(own, "section", 1)]
        at = jnp.stack([group ^ m for m in slot_order(way)])
        table += [section * groups + at, (1 - section) * groups + at]
    table = jnp.stack(table).astype(jnp.int32)
    ids = slot_chip.astype(jnp.int32)

    mid, first = after((mid, shares[0][0]))
    shares[0] = (first, shares[0][1])
    crossin = norm_rows(mid, cross_gain).astype(BF16)
    x = gather_half(crossin, section, bits)
    cq = both_halves(jnp.dot(x, cross_q, preferred_element_type=F32)).astype(BF16)
    cq = cq.reshape(count, 2, rows, HD)
    place = [order.index(m) for m in range(count)]
    back = jnp.asarray(place, jnp.int32)
    cq = jnp.stack(
        [lax.dynamic_index_in_dim(cq, back[tensor ^ c], 0, keepdims=False) for c in range(count)]
    )
    cq = jnp.transpose(cq, (1, 0, 2, 3)).reshape(devices * rows, HD)
    queries = gather_swaps(cq[None], "tensor", bits)

    for c in range(1, CHUNKS):
        shares.append(ffn(near[c], far[c], w_gate, w_up, w_down))
    total = [
        sum_swaps(ya.astype(F32) + swap(yb, "section", 1).astype(F32), "tensor", bits, BF16)
        for ya, yb in shares
    ]
    enc_out = (source.astype(F32) + keep_factor(enc_keep) * jnp.concatenate(total, 0)).astype(BF16)
    memory = norm_rows(enc_out, final_gain).astype(BF16)

    parts = attend_own_keys(memory, weights, queries, table, ids)
    parts = parts.reshape(devices, rows, parts.shape[1])
    parts = lax.all_to_all(parts, ("section", "tensor"), split_axis=0, concat_axis=0, tiled=True)
    dec_out = finish(parts, weights, mid, dec_keep, table, ids)
    return (enc_out, dec_out)


def solution(mesh):
    return jax.shard_map(
        per_device,
        mesh=mesh,
        in_specs=(
            P(("dp", "section", "tensor"), None),
            P(),
            P(None, ("section", "tensor")),
            P(None, ("section", "tensor")),
            P(("section", "tensor"), None),
            P(("dp", "section", "tensor"), None),
            P(),
            P(("dp", "section", "tensor"), None),
            P(),
            P("section", None, "tensor"),
            P("tensor", "section"),
            P(),
            P("section", "tensor"),
            P("section", None, "tensor"),
            P("tensor", "section"),
            P(("dp", "section", "tensor"), None),
        ),
        out_specs=(P(("dp", "section", "tensor"), None), P(("dp", "section", "tensor"), None)),
        check_vma=False,
    )
```

```python
import functools

import jax
import jax.numpy as jnp
from jax import lax
from jax.experimental import pallas as pl
from jax.experimental.pallas import tpu as pltpu
from jax.sharding import PartitionSpec as P

HD = 256
F32 = jnp.float32
BF16 = jnp.bfloat16
CHUNKS = 2


def norm_rows(x, gain):
    values = x.astype(F32)
    power = jnp.mean(values * values, axis=-1, keepdims=True)
    return values * lax.rsqrt(power + 1e-06) * gain


def keep_factor(words):
    shifts = jnp.arange(4, dtype=jnp.int32) * 3
    bits = jnp.right_shift(words[:, None, :], shifts[None, :, None]) & 7
    kept = jnp.where(bits == 7, 0.0, 8.0 / 7.0).astype(F32)
    return kept.reshape(words.shape[0], 4 * words.shape[1])


def swap(value, axis, distance):
    return lax.ppermute(value, axis, [(i, i ^ distance) for i in range(lax.axis_size(axis))])


def from_slots(value):
    count = lax.axis_size("tensor")
    return [value] + [
        lax.ppermute(value, "tensor", [(i, (i - o) % count) for i in range(count)]) for o in range(1, count)
    ]


def line_slots(value):
    count, tensor = lax.axis_size("tensor"), lax.axis_index("tensor")
    above, below = [value], [value]
    for step in range(1, count):
        above.append(lax.ppermute(above[-1], "tensor", [(i, i + 1) for i in range(step - 1, count - 1)]))
        below.append(lax.ppermute(below[-1], "tensor", [(i, i - 1) for i in range(1, count - step + 1)]))
    return [value] + [jnp.where(tensor + o < count, below[o], above[count - o]) for o in range(1, count)]


def line_sum(mine, got):
    count = lax.axis_size("tensor")
    block = mine.shape[0] // count

    def part(slot):
        at = slice(slot * block, (slot + 1) * block)
        return mine[at].astype(F32) + got[at].astype(F32)

    above, below = None, None
    for step in range(1, count):
        send_up, send_down = part(count - step), part(step)
        if step > 1:
            send_up = send_up + above.astype(F32)
            send_down = send_down + below.astype(F32)
        above = lax.ppermute(send_up.astype(BF16), "tensor", [(i, i + 1) for i in range(step)])
        below = lax.ppermute(
            send_down.astype(BF16), "tensor", [(i, i - 1) for i in range(count - step, count)]
        )
    return part(0) + above.astype(F32) + below.astype(F32)


def slots_sum(product):
    count = lax.axis_size("tensor")
    product = product.reshape(count, product.shape[0] // count, product.shape[1])
    total = product[0].astype(F32)
    for o in range(1, count):
        total = total + lax.ppermute(
            product[o], "tensor", [(i, (i + o) % count) for i in range(count)]
        ).astype(F32)
    return total


def half_columns(value, index):
    return lax.dynamic_slice_in_dim(value, index * (value.shape[1] // 2), value.shape[1] // 2, 1)


def in_order(own, other, section, axis):
    return jnp.where(
        section == 0, jnp.concatenate([own, other], axis), jnp.concatenate([other, own], axis)
    )


def gather_half(rows, section):
    own = half_columns(rows, section)
    other = swap(half_columns(rows, 1 - section), "section", 1)
    return jnp.concatenate(from_slots(in_order(own, other, section, 0)), 0)


def whole_rows(total, section):
    rows = total.shape[0] // 2
    own = lax.dynamic_slice_in_dim(total, section * rows, rows, 0)
    other = swap(lax.dynamic_slice_in_dim(total, (1 - section) * rows, rows, 0), "section", 1)
    return in_order(own, other, section, 1)


def both_halves(partial):
    return partial + swap(partial, "section", 1)


def gelu(x):
    return 0.5 * x * (1.0 + jnp.tanh(0.7978845608028654 * (x + 0.044715 * x * x * x)))


def ffn_kernel(hidden_steps, xa_ref, xb_ref, gate_ref, up_ref, down_ref, ya_ref, yb_ref, x, hidden):
    step = pl.program_id(0)
    rows = xa_ref.shape[0]
    width = gate_ref.shape[1]

    @pl.when(step == 0)
    def _():
        x[:rows, :] = xa_ref[...]
        x[rows:, :] = xb_ref[...]

    @pl.when(step < hidden_steps)
    def _():
        gate = jnp.dot(x[...], gate_ref[...], preferred_element_type=F32)
        up = jnp.dot(x[...], up_ref[...], preferred_element_type=F32)
        hidden[step] = (gelu(gate) * up).astype(BF16)

    @pl.when(step >= hidden_steps)
    def _():
        total = jnp.zeros((2 * rows, ya_ref.shape[1]), F32)
        for k in range(hidden.shape[0]):
            total += jnp.dot(
                hidden[k], down_ref[k * width : (k + 1) * width, :], preferred_element_type=F32
            )
        ya_ref[...] = total[:rows].astype(BF16)
        yb_ref[...] = total[rows:].astype(BF16)


def ffn(xa, xb, w_gate, w_up, w_down):
    rows, features = xa.shape
    units = w_gate.shape[1]
    width = min(256, units)
    tile = 512
    first, last = units // width, features // tile
    return pl.pallas_call(
        functools.partial(ffn_kernel, first),
        grid=(first + last,),
        in_specs=[
            pl.BlockSpec((rows, features), lambda i: (0, 0)),
            pl.BlockSpec((rows, features), lambda i: (0, 0)),
            pl.BlockSpec((features, width), lambda i: (0, jnp.minimum(i, first - 1))),
            pl.BlockSpec((features, width), lambda i: (0, jnp.minimum(i, first - 1))),
            pl.BlockSpec((units, tile), lambda i: (0, jnp.maximum(i - first, 0))),
        ],
        out_specs=[pl.BlockSpec((rows, tile), lambda i: (0, jnp.maximum(i - first, 0)))] * 2,
        out_shape=[jax.ShapeDtypeStruct((rows, features), BF16)] * 2,
        scratch_shapes=[
            pltpu.VMEM((2 * rows, features), BF16),
            pltpu.VMEM((first, 2 * rows, width), BF16),
        ],
        compiler_params=pltpu.CompilerParams(vmem_limit_bytes=48 * 2**20),
        cost_estimate=pl.CostEstimate(
            flops=12 * rows * features * units, bytes_accessed=6 * features * units, transcendentals=0
        ),
        name="ffn",
    )(xa, xb, w_gate, w_up, w_down)


def per_device(
    source,
    enc_gain,
    w_gate,
    w_up,
    w_down,
    enc_keep,
    final_gain,
    target,
    self_gain,
    self_qkv,
    self_out,
    cross_gain,
    cross_q,
    cross_kv,
    cross_out,
    dec_keep,
):
    section = lax.axis_index("section")
    count, tensor = lax.axis_size("tensor"), lax.axis_index("tensor")
    rows = target.shape[0]
    after = lax.optimization_barrier

    selfin = norm_rows(target, self_gain).astype(BF16)
    selfin = gather_half(selfin, section)

    normed = norm_rows(source, enc_gain).astype(BF16)
    block = normed.shape[0] // CHUNKS
    near = [
        jnp.concatenate(line_slots(normed[c * block : (c + 1) * block]), 0) for c in range(CHUNKS)
    ]
    far = [swap(x, "section", 1) for x in near]
    kv = jnp.transpose(cross_kv, (1, 0, 2))
    kv = in_order(kv, swap(kv, "section", 1), section, 1)

    qkv_w = jnp.transpose(self_qkv, (1, 0, 2))
    q, k, v = [jnp.dot(selfin, qkv_w[i], preferred_element_type=F32) for i in range(3)]
    q, k, v = [y.astype(BF16) for y in both_halves(jnp.stack([q, k, v]))]
    slot_chip = lax.rem(tensor + jnp.arange(count, dtype=jnp.int32), count)
    positions = (
        (jnp.arange(2, dtype=jnp.int32)[None, :] * count + slot_chip[:, None])[:, :, None] * rows
        + jnp.arange(rows, dtype=jnp.int32)
    ).reshape(-1)
    scores = lax.dot_general(q, k, (((1,), (1,)), ((), ())), preferred_element_type=F32) * (1.0 / 16.0)
    scores = jnp.where(positions[None, :] <= positions[:, None], scores, F32(-1e30))
    expo = jnp.exp(scores - jnp.max(scores, axis=-1, keepdims=True))
    probs = (expo / jnp.sum(expo, axis=-1, keepdims=True)).astype(BF16)
    context = jnp.dot(probs, v, preferred_element_type=F32).astype(BF16)
    product = jnp.dot(context, self_out, preferred_element_type=F32).astype(BF16)
    total = slots_sum(product)

    shares = [ffn(near[0], far[0], w_gate, w_up, w_down)]
    total, first = after((total, shares[0][0]))
    shares[0] = (first, shares[0][1])
    mid = (target.astype(F32) + whole_rows(total, section)).astype(BF16)
    crossin = gather_half(norm_rows(mid, cross_gain).astype(BF16), section)
    for c in range(1, CHUNKS):
        shares.append(ffn(near[c], far[c], w_gate, w_up, w_down))
    crossin, last = after((crossin, shares[-1][0]))
    shares[-1] = (last, shares[-1][1])
    cq = both_halves(jnp.dot(crossin, cross_q, preferred_element_type=F32)).astype(BF16)

    outs, keys, values = [], [], []
    for c, (ya, yb) in enumerate(shares):
        at = slice(c * block, (c + 1) * block)
        total = line_sum(ya, swap(yb, "section", 1))
        out = (source[at].astype(F32) + keep_factor(enc_keep[at]) * total).astype(BF16)
        outs.append(out)
        memory = norm_rows(out, final_gain).astype(BF16)
        memory = jnp.concatenate(line_slots(memory), 0)
        keys.append(jnp.dot(memory, kv[0], preferred_element_type=F32).astype(BF16))
        values.append(jnp.dot(memory, kv[1], preferred_element_type=F32).astype(BF16))
    enc_out = jnp.concatenate(outs, 0)
    keys, values = jnp.concatenate(keys, 0), jnp.concatenate(values, 0)

    scores = lax.dot_general(cq, keys, (((1,), (1,)), ((), ())), preferred_element_type=F32) * (1.0 / 16.0)
    top = jnp.max(scores, axis=-1, keepdims=True)
    expo = jnp.exp(scores - top)
    whole = jnp.sum(expo, axis=-1, keepdims=True)
    context = jnp.dot(expo.astype(BF16), values, preferred_element_type=F32)
    ours = jnp.concatenate(
        [context, jnp.broadcast_to(top, (top.shape[0], 128)), jnp.broadcast_to(whole, (top.shape[0], 128))], 1
    )
    theirs = swap(ours, "section", 1)
    their_top, their_whole = theirs[:, HD : HD + 1], theirs[:, HD + 128 : HD + 129]
    most = jnp.maximum(top, their_top)
    mine, other = jnp.exp(top - most), jnp.exp(their_top - most)
    context = (context * mine + theirs[:, :HD] * other) / (whole * mine + their_whole * other)
    product = jnp.dot(context.astype(BF16), cross_out, preferred_element_type=F32).astype(BF16)
    crosssum = whole_rows(slots_sum(product), section)
    dec_out = (mid.astype(F32) + keep_factor(dec_keep) * crosssum).astype(BF16)
    return (enc_out, dec_out)


def solution(mesh):
    return jax.shard_map(
        per_device,
        mesh=mesh,
        in_specs=(
            P(("dp", "section", "tensor"), None),
            P(),
            P(None, ("section", "tensor")),
            P(None, ("section", "tensor")),
            P(("section", "tensor"), None),
            P(("dp", "section", "tensor"), None),
            P(),
            P(("dp", "section", "tensor"), None),
            P(),
            P("section", None, "tensor"),
            P("tensor", "section"),
            P(),
            P("section", "tensor"),
            P("section", None, "tensor"),
            P("tensor", "section"),
            P(("dp", "section", "tensor"), None),
        ),
        out_specs=(P(("dp", "section", "tensor"), None), P(("dp", "section", "tensor"), None)),
        check_vma=False,
    )
```

```python
import functools

import jax
import jax.numpy as jnp
from jax import lax
from jax.experimental import pallas as pl
from jax.experimental.pallas import tpu as pltpu
from jax.sharding import PartitionSpec as P

HD = 256
F32 = jnp.float32
BF16 = jnp.bfloat16
STATS = 5


def norm_rows(x, gain):
    values = x.astype(F32)
    power = jnp.mean(values * values, axis=-1, keepdims=True)
    return values * lax.rsqrt(power + 1e-06) * gain


def keep_factor(words):
    shifts = jnp.arange(4, dtype=jnp.int32) * 3
    bits = jnp.right_shift(words[:, None, :], shifts[None, :, None]) & 7
    kept = jnp.where(bits == 7, 0.0, 8.0 / 7.0).astype(F32)
    return kept.reshape(words.shape[0], 4 * words.shape[1])


def swap(value, axis, distance):
    return lax.ppermute(value, axis, [(i, i ^ distance) for i in range(lax.axis_size(axis))])


def from_slots(value):
    count = lax.axis_size("tensor")
    return [value] + [
        lax.ppermute(value, "tensor", [(i, (i - o) % count) for i in range(count)]) for o in range(1, count)
    ]


def gated(value, *others):
    return lax.optimization_barrier((value,) + others)[0]


def line_step(above, below, step):
    count = lax.axis_size("tensor")
    return (
        lax.ppermute(above, "tensor", [(i, i + 1) for i in range(step - 1, count - 1)]),
        lax.ppermute(below, "tensor", [(i, i - 1) for i in range(1, count - step + 1)]),
    )


def line_rows(above, below):
    count, tensor = lax.axis_size("tensor"), lax.axis_index("tensor")
    return jnp.concatenate(
        [above[0]] + [jnp.where(tensor + o < count, below[o], above[count - o]) for o in range(1, count)], 0
    )


def slot_sum(mine, got, slot):
    block = mine.shape[0] // lax.axis_size("tensor")
    at = slice(slot * block, (slot + 1) * block)
    return mine[at].astype(F32) + got[at].astype(F32)


def sum_sends(mine, got, came, step):
    up, down = slot_sum(mine, got, lax.axis_size("tensor") - step), slot_sum(mine, got, step)
    if came is not None:
        up, down = up + came[0].astype(F32), down + came[1].astype(F32)
    return up.astype(BF16), down.astype(BF16)


def sum_step(sends, step):
    count = lax.axis_size("tensor")
    above = lax.ppermute(sends[0], "tensor", [(i, i + 1) for i in range(step)])
    below = lax.ppermute(sends[1], "tensor", [(i, i - 1) for i in range(count - step, count)])
    return lax.optimization_barrier((above, below))


def slots_sum(product):
    count = lax.axis_size("tensor")
    product = product.reshape(count, product.shape[0] // count, product.shape[1])
    total = product[0].astype(F32)
    for o in range(1, count):
        total = total + lax.ppermute(
            product[o], "tensor", [(i, (i + o) % count) for i in range(count)]
        ).astype(F32)
    return total


def half_columns(value, index):
    return lax.dynamic_slice_in_dim(value, index * (value.shape[1] // 2), value.shape[1] // 2, 1)


def in_order(own, other, section, axis):
    return jnp.where(
        section == 0, jnp.concatenate([own, other], axis), jnp.concatenate([other, own], axis)
    )


def gather_half(rows, section):
    own = half_columns(rows, section)
    other = swap(half_columns(rows, 1 - section), "section", 1)
    return jnp.concatenate(from_slots(in_order(own, other, section, 0)), 0)


def whole_rows(total, section):
    rows = total.shape[0] // 2
    own = lax.dynamic_slice_in_dim(total, section * rows, rows, 0)
    other = swap(lax.dynamic_slice_in_dim(total, (1 - section) * rows, rows, 0), "section", 1)
    return in_order(own, other, section, 1)


def both_halves(partial):
    return partial + swap(partial, "section", 1)


def gelu(x):
    return 0.5 * x * (1.0 + jnp.tanh(0.7978845608028654 * (x + 0.044715 * x * x * x)))


def ffn_kernel(hidden_steps, xa_ref, xb_ref, gate_ref, up_ref, down_ref, ya_ref, yb_ref, x, hidden):
    step = pl.program_id(0)
    rows = xa_ref.shape[0]
    width = gate_ref.shape[1]

    @pl.when(step == 0)
    def _():
        x[:rows, :] = xa_ref[...]
        x[rows:, :] = xb_ref[...]

    @pl.when(step < hidden_steps)
    def _():
        gate = jnp.dot(x[...], gate_ref[...], preferred_element_type=F32)
        up = jnp.dot(x[...], up_ref[...], preferred_element_type=F32)
        hidden[step] = (gelu(gate) * up).astype(BF16)

    @pl.when(step >= hidden_steps)
    def _():
        total = jnp.zeros((2 * rows, ya_ref.shape[1]), F32)
        for k in range(hidden.shape[0]):
            total += jnp.dot(
                hidden[k], down_ref[k * width : (k + 1) * width, :], preferred_element_type=F32
            )
        ya_ref[...] = total[:rows].astype(BF16)
        yb_ref[...] = total[rows:].astype(BF16)


def ffn(xa, xb, w_gate, w_up, w_down):
    rows, features = xa.shape
    units = w_gate.shape[1]
    width = min(256, units)
    tile = 512
    first, last = units // width, features // tile
    return pl.pallas_call(
        functools.partial(ffn_kernel, first),
        grid=(first + last,),
        in_specs=[
            pl.BlockSpec((rows, features), lambda i: (0, 0)),
            pl.BlockSpec((rows, features), lambda i: (0, 0)),
            pl.BlockSpec((features, width), lambda i: (0, jnp.minimum(i, first - 1))),
            pl.BlockSpec((features, width), lambda i: (0, jnp.minimum(i, first - 1))),
            pl.BlockSpec((units, tile), lambda i: (0, jnp.maximum(i - first, 0))),
        ],
        out_specs=[pl.BlockSpec((rows, tile), lambda i: (0, jnp.maximum(i - first, 0)))] * 2,
        out_shape=[jax.ShapeDtypeStruct((rows, features), BF16)] * 2,
        scratch_shapes=[
            pltpu.VMEM((2 * rows, features), BF16),
            pltpu.VMEM((first, 2 * rows, width), BF16),
        ],
        compiler_params=pltpu.CompilerParams(vmem_limit_bytes=48 * 2**20),
        cost_estimate=pl.CostEstimate(
            flops=12 * rows * features * units, bytes_accessed=6 * features * units, transcendentals=0
        ),
        name="ffn",
    )(xa, xb, w_gate, w_up, w_down)


def attend_kernel(
    heads, table, ids, mem_ref, a0_ref, a1_ref, b0_ref, b1_ref, cq_ref, out_ref
):
    slot = pl.program_id(0)
    head = ids[slot]
    groups, depth = a0_ref.shape[0], a0_ref.shape[3]

    def attend(own_ref, other_ref):
        keys = jnp.zeros((mem_ref.shape[0], HD), F32)
        values = jnp.zeros((mem_ref.shape[0], HD), F32)
        for place, ref in enumerate((own_ref, other_ref)):
            for i in range(groups):
                at = pl.multiple_of(table[place, i] * depth, depth)
                x = mem_ref[:, pl.ds(at, depth)]
                keys += jnp.dot(x, ref[i, 0, 0], preferred_element_type=F32)
                values += jnp.dot(x, ref[i, 0, 1], preferred_element_type=F32)
        k, v = keys.astype(BF16), values.astype(BF16)
        scores = lax.dot_general(cq_ref[0], k, (((1,), (1,)), ((), ())), preferred_element_type=F32)
        scores = scores * (1.0 / 16.0)
        top = jnp.max(scores, axis=-1, keepdims=True)
        expo = jnp.exp(scores - top)
        total = jnp.sum(expo, axis=-1, keepdims=True)
        context = jnp.dot(expo.astype(BF16), v, preferred_element_type=F32)
        out_ref[:, pl.ds(pl.multiple_of(head * HD, HD), HD)] = context.astype(BF16)
        lanes = lax.broadcasted_iota(jnp.int32, (scores.shape[0], 128), 1) - head * STATS
        base = heads * HD
        high = top.astype(BF16).astype(F32)
        rest = top - high
        middle = rest.astype(BF16).astype(F32)
        low = rest - middle
        sum_high = total.astype(BF16).astype(F32)
        sum_low = total - sum_high
        stats = jnp.where(slot == 0, jnp.zeros(lanes.shape, F32), out_ref[:, base:].astype(F32))
        for index, piece in enumerate((high, middle, low, sum_high, sum_low)):
            stats = jnp.where(lanes == index, piece, stats)
        out_ref[:, base:] = stats.astype(BF16)

    @pl.when(slot < heads // 2)
    def _():
        attend(a0_ref, a1_ref)

    @pl.when(slot >= heads // 2)
    def _():
        attend(b0_ref, b1_ref)


def attend_own_keys(memory, weights, queries, table, ids):
    rows, features = memory.shape
    heads, count, width = queries.shape
    groups, half, _, depth, _ = weights[0].shape
    block = (groups, 1, 2, depth, width)
    first = pl.BlockSpec(block, lambda h, t, n: (0, jnp.minimum(h, half - 1), 0, 0, 0))
    second = pl.BlockSpec(block, lambda h, t, n: (0, jnp.maximum(h - half, 0), 0, 0, 0))
    return pl.pallas_call(
        functools.partial(attend_kernel, heads),
        grid_spec=pltpu.PrefetchScalarGridSpec(
            num_scalar_prefetch=2,
            grid=(heads,),
            in_specs=[
                pl.BlockSpec((rows, features), lambda h, t, n: (0, 0)),
                first,
                first,
                second,
                second,
                pl.BlockSpec((1, count, width), lambda h, t, n: (h, 0, 0)),
            ],
            out_specs=pl.BlockSpec((count, heads * width + 128), lambda h, t, n: (0, 0)),
        ),
        out_shape=jax.ShapeDtypeStruct((count, heads * width + 128), BF16),
        compiler_params=pltpu.CompilerParams(vmem_limit_bytes=40 * 2**20),
        cost_estimate=pl.CostEstimate(
            flops=4 * rows * features * heads * width,
            bytes_accessed=4 * features * heads * width,
            transcendentals=0,
        ),
        name="attend_own_keys",
    )(table, ids, memory, *weights, queries)


def finish_kernel(
    heads, words_width, table, ids, parts_ref, a0_ref, a1_ref, b0_ref, b1_ref, mid_ref, words_ref, out_ref, context
):
    place, step = pl.program_id(0), pl.program_id(1)
    tile = out_ref.shape[1]
    index = table[place, step]

    @pl.when((place == 0) & (step == 0))
    def _():
        stat = parts_ref[:, :, heads * HD :].astype(F32)
        lanes = lax.broadcasted_iota(jnp.int32, stat.shape, 2)
        for slot in range(heads):
            head = ids[slot]
            pick = [
                jnp.sum(jnp.where(lanes == head * STATS + j, stat, 0.0), axis=-1, keepdims=True)
                for j in range(STATS)
            ]
            top = pick[0] + pick[1] + pick[2]
            weight = jnp.exp(top - jnp.max(top, axis=0, keepdims=True))
            whole = jnp.sum(weight * (pick[3] + pick[4]), axis=0)
            part = parts_ref[:, :, pl.ds(pl.multiple_of(head * HD, HD), HD)].astype(F32)
            context[:, slot * HD : (slot + 1) * HD] = (jnp.sum(part * weight, axis=0) / whole).astype(BF16)

    def columns(a_ref, b_ref):
        half = heads * HD // 2
        for u in range(tile // HD):
            cut = slice(u * HD, (u + 1) * HD)
            wa = a_ref[0, :, 0, cut, :].reshape(half, HD)
            wb = b_ref[0, :, 0, cut, :].reshape(half, HD)
            total = jnp.dot(context[:, :half], wa, preferred_element_type=F32)
            total += jnp.dot(context[:, half:], wb, preferred_element_type=F32)
            words = words_ref[:, cut]
            shift = 3 * (index // (words_width // tile))
            bits = lax.shift_right_logical(words, jnp.broadcast_to(shift, words.shape)) & 7
            kept = jnp.where(bits == 7, 0.0, 8.0 / 7.0).astype(F32)
            out_ref[:, cut] = (mid_ref[:, cut].astype(F32) + kept * total).astype(BF16)

    @pl.when(place == 0)
    def _():
        columns(a0_ref, b0_ref)

    @pl.when(place == 1)
    def _():
        columns(a1_ref, b1_ref)


def finish(parts, weights, mid, words, table, ids):
    groups, half, _, depth, width = weights[0].shape
    heads = 2 * half
    rows, features = mid.shape
    per_word = words.shape[1] // depth
    block = (1, half, 1, depth, width)
    def own_block(p, i, t, n):
        return (jnp.where(p == 0, i, groups - 1), 0, 2, 0, 0)

    def other_block(p, i, t, n):
        return (jnp.where(p == 0, 0, i), 0, 2, 0, 0)

    return pl.pallas_call(
        functools.partial(finish_kernel, heads, words.shape[1]),
        grid_spec=pltpu.PrefetchScalarGridSpec(
            num_scalar_prefetch=2,
            grid=(2, groups),
            in_specs=[
                pl.BlockSpec(parts.shape, lambda p, i, t, n: (0, 0, 0)),
                pl.BlockSpec(block, own_block),
                pl.BlockSpec(block, other_block),
                pl.BlockSpec(block, own_block),
                pl.BlockSpec(block, other_block),
                pl.BlockSpec((rows, depth), lambda p, i, t, n: (0, t[p, i])),
                pl.BlockSpec((rows, depth), lambda p, i, t, n: (0, lax.rem(t[p, i], per_word))),
            ],
            out_specs=pl.BlockSpec((rows, depth), lambda p, i, t, n: (0, t[p, i])),
            scratch_shapes=[pltpu.VMEM((rows, heads * width), BF16)],
        ),
        out_shape=jax.ShapeDtypeStruct((rows, features), BF16),
        compiler_params=pltpu.CompilerParams(vmem_limit_bytes=32 * 2**20),
        cost_estimate=pl.CostEstimate(
            flops=2 * rows * features * heads * width,
            bytes_accessed=2 * features * heads * width,
            transcendentals=0,
        ),
        name="finish",
    )(table, ids, parts, *weights, mid, words)


def per_device(
    source,
    enc_gain,
    w_gate,
    w_up,
    w_down,
    enc_keep,
    final_gain,
    target,
    self_gain,
    self_qkv,
    self_out,
    cross_gain,
    cross_q,
    cross_kv,
    cross_out,
    dec_keep,
):
    section, group = lax.axis_index("section"), lax.axis_index("dp")
    count, tensor = lax.axis_size("tensor"), lax.axis_index("tensor")
    groups = lax.axis_size("dp")
    rows = target.shape[0]
    devices = 2 * count

    normed = norm_rows(source, enc_gain).astype(BF16)
    block = normed.shape[0] // 2
    above, below = [[normed[:block]], [normed[block:]]], [[normed[:block]], [normed[block:]]]

    def pass_on(c):
        one, two = line_step(above[c][-1], below[c][-1], len(above[c]))
        above[c].append(one)
        below[c].append(two)

    for step in range(1, count):
        pass_on(0)
        if step == count - 2:
            second = gated(normed[block:], above[0][-1], below[0][-1])
            above[1], below[1] = [second], [second]
            pass_on(1)
    near = line_rows(above[0], below[0])
    far = swap(near, "section", 1)
    near = gated(near, above[1][-1], below[1][-1])
    if count > 2:
        pass_on(1)

    selfin = gather_half(gated(norm_rows(target, self_gain).astype(BF16), above[0][-2], below[0][-2]), section)

    mine, theirs = ffn(near, far, w_gate, w_up, w_down)
    while len(above[1]) < count:
        pass_on(1)
    near = line_rows(above[1], below[1])
    far = swap(near, "section", 1)

    depth = cross_kv.shape[0] // groups
    kv_share = lax.dynamic_slice_in_dim(jnp.transpose(cross_kv, (1, 0, 2)), group * depth, depth, 1)
    out_share = lax.dynamic_slice_in_dim(cross_out, group * depth, depth, 1)
    out_share = jnp.transpose(out_share.reshape(HD, depth // HD, HD), (1, 0, 2)).reshape(1, depth, HD)
    share = gated(jnp.concatenate([kv_share, out_share], 0), above[1][-2], below[1][-2])
    slots = from_slots(share)
    weights = []
    for pieces in (slots[: count // 2], slots[count // 2 :]):
        own = lax.all_gather(jnp.stack(pieces), "dp", axis=0, tiled=False)
        weights += [own, swap(own, "section", 1)]
    table = jnp.stack([section * groups, (1 - section) * groups])[:, None] + jnp.arange(groups, dtype=jnp.int32)
    slot_chip = lax.rem(tensor + jnp.arange(count, dtype=jnp.int32), count)

    selfin = gated(selfin, mine)
    qkv_w = jnp.transpose(self_qkv, (1, 0, 2))
    q, k, v = [jnp.dot(selfin, qkv_w[i], preferred_element_type=F32) for i in range(3)]
    q, k, v = [y.astype(BF16) for y in both_halves(jnp.stack([q, k, v]))]
    positions = (
        (jnp.arange(2, dtype=jnp.int32)[None, :] * count + slot_chip[:, None])[:, :, None] * rows
        + jnp.arange(rows, dtype=jnp.int32)
    ).reshape(-1)
    scores = lax.dot_general(q, k, (((1,), (1,)), ((), ())), preferred_element_type=F32) * (1.0 / 16.0)
    scores = jnp.where(positions[None, :] <= positions[:, None], scores, F32(-1e30))
    expo = jnp.exp(scores - jnp.max(scores, axis=-1, keepdims=True))
    probs = (expo / jnp.sum(expo, axis=-1, keepdims=True)).astype(BF16)
    context = jnp.dot(probs, v, preferred_element_type=F32).astype(BF16)
    product = jnp.dot(context, self_out, preferred_element_type=F32).astype(BF16)
    total = slots_sum(product)

    got = swap(theirs, "section", 1)
    came = sum_step(sum_sends(mine, got, None, 1), 1)
    sends = sum_sends(mine, got, came, 2)
    near = gated(near, *sends)
    came = sum_step(sends, 2)
    mine_b, theirs_b = ffn(near, far, w_gate, w_up, w_down)
    for step in range(3, count):
        came = sum_step(sum_sends(mine, got, came, step), step)
    ffn_a = slot_sum(mine, got, 0) + came[0].astype(F32) + came[1].astype(F32)

    total = gated(total, mine_b)
    mid = (target.astype(F32) + whole_rows(total, section)).astype(BF16)
    crossin = gather_half(norm_rows(mid, cross_gain).astype(BF16), section)

    got_b = swap(theirs_b, "section", 1)
    came_b = sum_step(sum_sends(mine_b, got_b, None, 1), 1)
    crossin = gated(crossin, *came_b)
    for step in range(2, count):
        came_b = sum_step(sum_sends(mine_b, got_b, came_b, step), step)
    cq = both_halves(jnp.dot(crossin, cross_q, preferred_element_type=F32)).astype(BF16)
    cq = jnp.roll(cq.reshape(count, 2, rows, HD), tensor, axis=0)
    cq = jnp.transpose(cq, (1, 0, 2, 3)).reshape(devices * rows, HD)
    queries = jnp.stack(from_slots(cq))
    ffn_b = slot_sum(mine_b, got_b, 0) + came_b[0].astype(F32) + came_b[1].astype(F32)

    total = jnp.concatenate([ffn_a, ffn_b], 0)
    enc_out = (source.astype(F32) + keep_factor(enc_keep) * total).astype(BF16)
    memory = norm_rows(enc_out, final_gain).astype(BF16)

    parts = attend_own_keys(memory, weights, queries, table, slot_chip)
    parts = parts.reshape(devices, rows, parts.shape[1])
    parts = lax.all_to_all(parts, ("section", "tensor"), split_axis=0, concat_axis=0, tiled=True)
    dec_out = finish(parts, weights, mid, dec_keep, table, slot_chip)
    return (enc_out, dec_out)


def solution(mesh):
    return jax.shard_map(
        per_device,
        mesh=mesh,
        in_specs=(
            P(("dp", "section", "tensor"), None),
            P(),
            P(None, ("section", "tensor")),
            P(None, ("section", "tensor")),
            P(("section", "tensor"), None),
            P(("dp", "section", "tensor"), None),
            P(),
            P(("dp", "section", "tensor"), None),
            P(),
            P("section", None, "tensor"),
            P("tensor", "section"),
            P(),
            P("section", "tensor"),
            P("section", None, "tensor"),
            P("tensor", "section"),
            P(("dp", "section", "tensor"), None),
        ),
        out_specs=(P(("dp", "section", "tensor"), None), P(("dp", "section", "tensor"), None)),
        check_vma=False,
    )
```

```python
import functools

import jax
import jax.numpy as jnp
from jax import lax
from jax.experimental import pallas as pl
from jax.experimental.pallas import tpu as pltpu
from jax.sharding import PartitionSpec as P

HD = 256
F32 = jnp.float32
BF16 = jnp.bfloat16


def norm_rows(x, gain):
    values = x.astype(F32)
    power = jnp.mean(values * values, axis=-1, keepdims=True)
    return values * lax.rsqrt(power + 1e-06) * gain


def keep_factor(words):
    shifts = jnp.arange(4, dtype=jnp.int32) * 3
    bits = jnp.right_shift(words[:, None, :], shifts[None, :, None]) & 7
    kept = jnp.where(bits == 7, 0.0, 8.0 / 7.0).astype(F32)
    return kept.reshape(words.shape[0], 4 * words.shape[1])


def swap(value, axis, distance):
    return lax.ppermute(value, axis, [(i, i ^ distance) for i in range(lax.axis_size(axis))])


def from_slots(value):
    count = lax.axis_size("tensor")
    return [value] + [
        lax.ppermute(value, "tensor", [(i, (i - o) % count) for i in range(count)]) for o in range(1, count)
    ]


def gated(value, *others):
    return lax.optimization_barrier((value,) + others)[0]


def slot_sum(mine, got, slot):
    block = mine.shape[0] // lax.axis_size("tensor")
    at = slice(slot * block, (slot + 1) * block)
    return mine[at].astype(F32) + got[at].astype(F32)


def sum_sends(mine, got, came, step):
    up, down = slot_sum(mine, got, lax.axis_size("tensor") - step), slot_sum(mine, got, step)
    if came is not None:
        up, down = up + came[0].astype(F32), down + came[1].astype(F32)
    return up.astype(BF16), down.astype(BF16)


def sum_step(sends, step):
    count = lax.axis_size("tensor")
    above = lax.ppermute(sends[0], "tensor", [(i, i + 1) for i in range(step)])
    below = lax.ppermute(sends[1], "tensor", [(i, i - 1) for i in range(count - step, count)])
    return lax.optimization_barrier((above, below))


def slots_sum(product):
    count = lax.axis_size("tensor")
    product = product.reshape(count, product.shape[0] // count, product.shape[1])
    total = product[0].astype(F32)
    for o in range(1, count):
        total = total + lax.ppermute(
            product[o], "tensor", [(i, (i + o) % count) for i in range(count)]
        ).astype(F32)
    return total


def half_columns(value, index):
    return lax.dynamic_slice_in_dim(value, index * (value.shape[1] // 2), value.shape[1] // 2, 1)


def in_order(own, other, section, axis):
    return jnp.where(
        section == 0, jnp.concatenate([own, other], axis), jnp.concatenate([other, own], axis)
    )


def gather_half(rows, section):
    own = half_columns(rows, section)
    other = swap(half_columns(rows, 1 - section), "section", 1)
    return jnp.concatenate(from_slots(in_order(own, other, section, 0)), 0)


def whole_rows(total, section):
    rows = total.shape[0] // 2
    own = lax.dynamic_slice_in_dim(total, section * rows, rows, 0)
    other = swap(lax.dynamic_slice_in_dim(total, (1 - section) * rows, rows, 0), "section", 1)
    return in_order(own, other, section, 1)


def both_halves(partial):
    return partial + swap(partial, "section", 1)


def gelu(x):
    return 0.5 * x * (1.0 + jnp.tanh(0.7978845608028654 * (x + 0.044715 * x * x * x)))


def ffn_kernel(hidden_steps, order, x_ref, gate_ref, up_ref, down_ref, ya_ref, yb_ref, x, hidden):
    step = pl.program_id(0)
    rows = ya_ref.shape[0]
    width = gate_ref.shape[1]
    blocks = order.shape[0]
    block = 2 * rows // blocks

    @pl.when(step == 0)
    def _():
        for slot in range(blocks):
            at = pl.multiple_of(order[slot] * block, block)
            x[slot * block : (slot + 1) * block, :] = x_ref[pl.ds(at, block), :]

    @pl.when(step < hidden_steps)
    def _():
        gate = jnp.dot(x[...], gate_ref[...], preferred_element_type=F32)
        up = jnp.dot(x[...], up_ref[...], preferred_element_type=F32)
        hidden[step] = (gelu(gate) * up).astype(BF16)

    @pl.when(step >= hidden_steps)
    def _():
        total = jnp.zeros((2 * rows, ya_ref.shape[1]), F32)
        for k in range(hidden.shape[0]):
            total += jnp.dot(
                hidden[k], down_ref[k * width : (k + 1) * width, :], preferred_element_type=F32
            )
        ya_ref[...] = total[:rows].astype(BF16)
        yb_ref[...] = total[rows:].astype(BF16)


def ffn(x, order, w_gate, w_up, w_down):
    rows, features = x.shape
    units = w_gate.shape[1]
    width = min(256, units)
    tile = 512
    first, last = units // width, features // tile
    return pl.pallas_call(
        functools.partial(ffn_kernel, first),
        grid_spec=pltpu.PrefetchScalarGridSpec(
            num_scalar_prefetch=1,
            grid=(first + last,),
            in_specs=[
                pl.BlockSpec((rows, features), lambda i, t: (0, 0), pipeline_mode=pl.Buffered(1)),
                pl.BlockSpec((features, width), lambda i, t: (0, jnp.minimum(i, first - 1))),
                pl.BlockSpec((features, width), lambda i, t: (0, jnp.minimum(i, first - 1))),
                pl.BlockSpec((units, tile), lambda i, t: (0, jnp.maximum(i - first, 0))),
            ],
            out_specs=[pl.BlockSpec((rows // 2, tile), lambda i, t: (0, jnp.maximum(i - first, 0)))] * 2,
            scratch_shapes=[
                pltpu.VMEM((rows, features), BF16),
                pltpu.VMEM((first, rows, width), BF16),
            ],
        ),
        out_shape=[jax.ShapeDtypeStruct((rows // 2, features), BF16)] * 2,
        compiler_params=pltpu.CompilerParams(vmem_limit_bytes=48 * 2**20),
        cost_estimate=pl.CostEstimate(
            flops=6 * rows * features * units, bytes_accessed=6 * features * units, transcendentals=0
        ),
        name="ffn",
    )(order, x, w_gate, w_up, w_down)


def per_device(
    source,
    enc_gain,
    w_gate,
    w_up,
    w_down,
    enc_keep,
    final_gain,
    target,
    self_gain,
    self_qkv,
    self_out,
    cross_gain,
    cross_q,
    cross_kv,
    cross_out,
    dec_keep,
):
    section = lax.axis_index("section")
    count, tensor = lax.axis_size("tensor"), lax.axis_index("tensor")
    rows = target.shape[0]
    slot_chip = lax.rem(tensor + jnp.arange(count, dtype=jnp.int32), count)
    order = jnp.concatenate([section * count + slot_chip, (1 - section) * count + slot_chip])

    selfin = gather_half(norm_rows(target, self_gain).astype(BF16), section)

    normed = norm_rows(source, enc_gain).astype(BF16)
    block = normed.shape[0] // 2
    near = [
        lax.all_gather(normed[c * block : (c + 1) * block], ("section", "tensor"), axis=0, tiled=True)
        for c in range(2)
    ]
    kv = jnp.transpose(cross_kv, (1, 0, 2))
    kv = in_order(kv, swap(kv, "section", 1), section, 1)

    qkv_w = jnp.transpose(self_qkv, (1, 0, 2))
    q, k, v = [jnp.dot(selfin, qkv_w[i], preferred_element_type=F32) for i in range(3)]
    q, k, v = [y.astype(BF16) for y in both_halves(jnp.stack([q, k, v]))]
    positions = (
        (jnp.arange(2, dtype=jnp.int32)[None, :] * count + slot_chip[:, None])[:, :, None] * rows
        + jnp.arange(rows, dtype=jnp.int32)
    ).reshape(-1)
    scores = lax.dot_general(q, k, (((1,), (1,)), ((), ())), preferred_element_type=F32) * (1.0 / 16.0)
    scores = jnp.where(positions[None, :] <= positions[:, None], scores, F32(-1e30))
    expo = jnp.exp(scores - jnp.max(scores, axis=-1, keepdims=True))
    probs = (expo / jnp.sum(expo, axis=-1, keepdims=True)).astype(BF16)
    context = jnp.dot(probs, v, preferred_element_type=F32).astype(BF16)
    product = jnp.dot(context, self_out, preferred_element_type=F32).astype(BF16)
    total = slots_sum(product)

    mine, theirs = ffn(near[0], order, w_gate, w_up, w_down)
    got = swap(theirs, "section", 1)
    came = sum_step(sum_sends(mine, got, None, 1), 1)
    total = gated(total, *came)
    mid = (target.astype(F32) + whole_rows(total, section)).astype(BF16)
    crossin = gather_half(norm_rows(mid, cross_gain).astype(BF16), section)
    for step in range(2, count - 1):
        came = sum_step(sum_sends(mine, got, came, step), step)
    sends = sum_sends(mine, got, came, count - 1)
    came = sum_step(sends, count - 1)
    mine_b, theirs_b = ffn(gated(near[1], *sends), order, w_gate, w_up, w_down)

    def finish_rows(c, mine, got, came):
        at = slice(c * block, (c + 1) * block)
        total = slot_sum(mine, got, 0) + came[0].astype(F32) + came[1].astype(F32)
        out = (source[at].astype(F32) + keep_factor(enc_keep[at]) * total).astype(BF16)
        memory = norm_rows(out, final_gain).astype(BF16)
        return out, memory

    def to_heads(memory):
        return lax.all_gather(memory, "tensor", axis=0, tiled=True)

    def keys_values(memory):
        return [jnp.dot(memory, kv[i], preferred_element_type=F32).astype(BF16) for i in range(2)]

    out_a, memory_a = finish_rows(0, mine, got, came)
    memory_a, mine_b = lax.optimization_barrier((memory_a, mine_b))
    memory_a = to_heads(memory_a)
    got = swap(theirs_b, "section", 1)
    came = sum_step(sum_sends(mine_b, got, None, 1), 1)
    crossin = gated(crossin, *came)
    cq = both_halves(jnp.dot(crossin, cross_q, preferred_element_type=F32)).astype(BF16)
    for step in range(2, count):
        came = sum_step(sum_sends(mine_b, got, came, step), step)
    out_b, memory_b = finish_rows(1, mine_b, got, came)
    memory_b = to_heads(memory_b)
    memory_a = gated(memory_a, out_b)
    keys_a, values_a = keys_values(memory_a)
    keys_b, values_b = keys_values(memory_b)
    enc_out = jnp.concatenate([out_a, out_b], 0)
    keys, values = jnp.concatenate([keys_a, keys_b], 0), jnp.concatenate([values_a, values_b], 0)

    scores = lax.dot_general(cq, keys, (((1,), (1,)), ((), ())), preferred_element_type=F32) * (1.0 / 16.0)
    top = jnp.max(scores, axis=-1, keepdims=True)
    expo = jnp.exp(scores - top)
    whole = jnp.sum(expo, axis=-1, keepdims=True)
    context = jnp.dot(expo.astype(BF16), values, preferred_element_type=F32)
    ours = jnp.concatenate(
        [context, jnp.broadcast_to(top, (top.shape[0], 128)), jnp.broadcast_to(whole, (top.shape[0], 128))], 1
    )
    theirs = swap(ours, "section", 1)
    their_top, their_whole = theirs[:, HD : HD + 1], theirs[:, HD + 128 : HD + 129]
    most = jnp.maximum(top, their_top)
    mine, other = jnp.exp(top - most), jnp.exp(their_top - most)
    context = (context * mine + theirs[:, :HD] * other) / (whole * mine + their_whole * other)
    product = jnp.dot(context.astype(BF16), cross_out, preferred_element_type=F32).astype(BF16)
    crosssum = whole_rows(slots_sum(product), section)
    dec_out = (mid.astype(F32) + keep_factor(dec_keep) * crosssum).astype(BF16)
    return (enc_out, dec_out)


def solution(mesh):
    return jax.shard_map(
        per_device,
        mesh=mesh,
        in_specs=(
            P(("dp", "section", "tensor"), None),
            P(),
            P(None, ("section", "tensor")),
            P(None, ("section", "tensor")),
            P(("section", "tensor"), None),
            P(("dp", "section", "tensor"), None),
            P(),
            P(("dp", "section", "tensor"), None),
            P(),
            P("section", None, "tensor"),
            P("tensor", "section"),
            P(),
            P("section", "tensor"),
            P("section", None, "tensor"),
            P("tensor", "section"),
            P(("dp", "section", "tensor"), None),
        ),
        out_specs=(P(("dp", "section", "tensor"), None), P(("dp", "section", "tensor"), None)),
        check_vma=False,
    )
```

```python
import functools

import jax
import jax.numpy as jnp
from jax import lax
from jax.experimental import pallas as pl
from jax.experimental.pallas import tpu as pltpu
from jax.sharding import PartitionSpec as P

HD = 256
F32 = jnp.float32
BF16 = jnp.bfloat16


def norm_rows(x, gain):
    values = x.astype(F32)
    power = jnp.mean(values * values, axis=-1, keepdims=True)
    return values * lax.rsqrt(power + 1e-06) * gain


def keep_factor(words):
    shifts = jnp.arange(4, dtype=jnp.int32) * 3
    bits = jnp.right_shift(words[:, None, :], shifts[None, :, None]) & 7
    kept = jnp.where(bits == 7, 0.0, 8.0 / 7.0).astype(F32)
    return kept.reshape(words.shape[0], 4 * words.shape[1])


def swap(value, axis, distance):
    return lax.ppermute(value, axis, [(i, i ^ distance) for i in range(lax.axis_size(axis))])


def from_slots(value):
    count = lax.axis_size("tensor")
    return [value] + [
        lax.ppermute(value, "tensor", [(i, (i - o) % count) for i in range(count)]) for o in range(1, count)
    ]


def gated(value, *others):
    return lax.optimization_barrier((value,) + others)[0]


def slot_sum(mine, got, slot):
    block = mine.shape[0] // lax.axis_size("tensor")
    at = slice(slot * block, (slot + 1) * block)
    return mine[at].astype(F32) + got[at].astype(F32)


def sum_sends(mine, got, came, step):
    up, down = slot_sum(mine, got, lax.axis_size("tensor") - step), slot_sum(mine, got, step)
    if came is not None:
        up, down = up + came[0].astype(F32), down + came[1].astype(F32)
    return up.astype(BF16), down.astype(BF16)


def sum_step(sends, step):
    count = lax.axis_size("tensor")
    above = lax.ppermute(sends[0], "tensor", [(i, i + 1) for i in range(step)])
    below = lax.ppermute(sends[1], "tensor", [(i, i - 1) for i in range(count - step, count)])
    return lax.optimization_barrier((above, below))


def slots_sum(product):
    count = lax.axis_size("tensor")
    product = product.reshape(count, product.shape[0] // count, product.shape[1])
    total = product[0].astype(F32)
    for o in range(1, count):
        total = total + lax.ppermute(
            product[o], "tensor", [(i, (i + o) % count) for i in range(count)]
        ).astype(F32)
    return total


def half_columns(value, index):
    return lax.dynamic_slice_in_dim(value, index * (value.shape[1] // 2), value.shape[1] // 2, 1)


def in_order(own, other, section, axis):
    return jnp.where(
        section == 0, jnp.concatenate([own, other], axis), jnp.concatenate([other, own], axis)
    )


def gather_half(rows, section):
    own = half_columns(rows, section)
    other = swap(half_columns(rows, 1 - section), "section", 1)
    return jnp.concatenate(from_slots(in_order(own, other, section, 0)), 0)


def whole_rows(total, section):
    rows = total.shape[0] // 2
    own = lax.dynamic_slice_in_dim(total, section * rows, rows, 0)
    other = swap(lax.dynamic_slice_in_dim(total, (1 - section) * rows, rows, 0), "section", 1)
    return in_order(own, other, section, 1)


def both_halves(partial):
    return partial + swap(partial, "section", 1)


def gelu(x):
    return 0.5 * x * (1.0 + jnp.tanh(0.7978845608028654 * (x + 0.044715 * x * x * x)))


def ffn_kernel(ins, order, x_ref, gate_ref, up_ref, down_ref, ya_ref, yb_ref, x, gate, up, hidden):
    step = pl.program_id(0)
    blocks, block, _ = x_ref.shape
    depth = gate_ref.shape[0]

    @pl.when(step == 0)
    def _():
        for slot in range(blocks):
            rows = x_ref[order[slot]]
            for k in range(ins):
                x[k, slot * block : (slot + 1) * block, :] = rows[:, k * depth : (k + 1) * depth]

    @pl.when(step < ins)
    def _():
        part = x[step]
        one = jnp.dot(part, gate_ref[...], preferred_element_type=F32)
        two = jnp.dot(part, up_ref[...], preferred_element_type=F32)

        @pl.when(step == 0)
        def _():
            gate[...] = one
            up[...] = two

        @pl.when(step > 0)
        def _():
            gate[...] += one
            up[...] += two

    @pl.when(step == ins)
    def _():
        hidden[...] = (gelu(gate[...]) * up[...]).astype(BF16)

    @pl.when(step >= ins)
    def _():
        total = jnp.dot(hidden[...], down_ref[...], preferred_element_type=F32).astype(BF16)
        half = total.shape[0] // 2
        ya_ref[...] = total[:half]
        yb_ref[...] = total[half:]


def ffn(x, order, piece, pieces, w_gate, w_up, w_down):
    rows, features = x.shape
    units = w_gate.shape[1]
    depth, tile = 512, 1024
    ins, outs = features // depth, features // tile
    blocks = order.shape[0]
    block = rows // blocks // pieces
    rows = rows // pieces
    return pl.pallas_call(
        functools.partial(ffn_kernel, ins),
        grid_spec=pltpu.PrefetchScalarGridSpec(
            num_scalar_prefetch=1,
            grid=(ins + outs,),
            in_specs=[
                pl.BlockSpec((blocks, block, features), lambda i, t: (0, piece, 0), pipeline_mode=pl.Buffered(1)),
                pl.BlockSpec((depth, units), lambda i, t: (jnp.minimum(i, ins - 1), 0)),
                pl.BlockSpec((depth, units), lambda i, t: (jnp.minimum(i, ins - 1), 0)),
                pl.BlockSpec((units, tile), lambda i, t: (0, jnp.maximum(i - ins, 0))),
            ],
            out_specs=[pl.BlockSpec((rows // 2, tile), lambda i, t: (0, jnp.maximum(i - ins, 0)))] * 2,
            scratch_shapes=[
                pltpu.VMEM((ins, rows, depth), BF16),
                pltpu.VMEM((rows, units), F32),
                pltpu.VMEM((rows, units), F32),
                pltpu.VMEM((rows, units), BF16),
            ],
        ),
        out_shape=[jax.ShapeDtypeStruct((rows // 2, features), BF16)] * 2,
        compiler_params=pltpu.CompilerParams(vmem_limit_bytes=40 * 2**20),
        cost_estimate=pl.CostEstimate(
            flops=6 * rows * features * units, bytes_accessed=6 * features * units, transcendentals=0
        ),
        name="ffn",
    )(order, x.reshape(blocks, -1, features), w_gate, w_up, w_down)


def per_device(
    source,
    enc_gain,
    w_gate,
    w_up,
    w_down,
    enc_keep,
    final_gain,
    target,
    self_gain,
    self_qkv,
    self_out,
    cross_gain,
    cross_q,
    cross_kv,
    cross_out,
    dec_keep,
):
    section = lax.axis_index("section")
    count, tensor = lax.axis_size("tensor"), lax.axis_index("tensor")
    rows = target.shape[0]
    slot_chip = lax.rem(tensor + jnp.arange(count, dtype=jnp.int32), count)
    order = jnp.concatenate([section * count + slot_chip, (1 - section) * count + slot_chip])

    selfin = gather_half(norm_rows(target, self_gain).astype(BF16), section)

    normed = norm_rows(source, enc_gain).astype(BF16)
    block = normed.shape[0] // 2
    near = [
        lax.all_gather(normed[c * block : (c + 1) * block], ("section", "tensor"), axis=0, tiled=True)
        for c in range(2)
    ]
    kv = jnp.transpose(cross_kv, (1, 0, 2))
    kv = in_order(kv, swap(kv, "section", 1), section, 1)

    qkv_w = jnp.transpose(self_qkv, (1, 0, 2))
    q, k, v = [jnp.dot(selfin, qkv_w[i], preferred_element_type=F32) for i in range(3)]
    q, k, v = [y.astype(BF16) for y in both_halves(jnp.stack([q, k, v]))]
    positions = (
        (jnp.arange(2, dtype=jnp.int32)[None, :] * count + slot_chip[:, None])[:, :, None] * rows
        + jnp.arange(rows, dtype=jnp.int32)
    ).reshape(-1)
    scores = lax.dot_general(q, k, (((1,), (1,)), ((), ())), preferred_element_type=F32) * (1.0 / 16.0)
    scores = jnp.where(positions[None, :] <= positions[:, None], scores, F32(-1e30))
    expo = jnp.exp(scores - jnp.max(scores, axis=-1, keepdims=True))
    probs = (expo / jnp.sum(expo, axis=-1, keepdims=True)).astype(BF16)
    context = jnp.dot(probs, v, preferred_element_type=F32).astype(BF16)
    product = jnp.dot(context, self_out, preferred_element_type=F32).astype(BF16)
    total = slots_sum(product)

    def begin(rows, mine, theirs):
        got = swap(theirs, "section", 1)
        return dict(rows=rows, mine=mine, got=got, came=None)

    def sends(state, step):
        return sum_sends(state["mine"], state["got"], state["came"], step)

    def finish_rows(state):
        at, came = state["rows"], state["came"]
        total = slot_sum(state["mine"], state["got"], 0) + came[0].astype(F32) + came[1].astype(F32)
        out = (source[at].astype(F32) + keep_factor(enc_keep[at]) * total).astype(BF16)
        return out, norm_rows(out, final_gain).astype(BF16)

    def to_heads(memory):
        return lax.all_gather(memory, "tensor", axis=0, tiled=True)

    def keys_values(memory):
        return [jnp.dot(memory, kv[i], preferred_element_type=F32).astype(BF16) for i in range(2)]

    weights = (w_gate, w_up, w_down)
    quarter = block // 2
    a = begin(slice(0, block), *ffn(gated(near[0], product), order, 0, 1, *weights))
    for step in range(1, count - 1):
        a["came"] = sum_step(sends(a, step), step)
        if step == 1:
            total = gated(total, *a["came"])
            mid = (target.astype(F32) + whole_rows(total, section)).astype(BF16)
            crossin = gather_half(norm_rows(mid, cross_gain).astype(BF16), section)
    last = sends(a, count - 1)
    x = gated(near[1], *last)
    b = begin(slice(block, block + quarter), *ffn(x, order, 0, 2, *weights))
    a["came"] = sum_step(last, count - 1)
    out_a, memory_a = finish_rows(a)

    first = sends(b, 1)
    x, memory_a = lax.optimization_barrier((x, memory_a) + first)[:2]
    memory_a = to_heads(memory_a)
    b["came"] = sum_step(first, 1)
    c = begin(slice(block + quarter, 2 * block), *ffn(x, order, 1, 2, *weights))
    for step in range(2, count):
        b["came"] = sum_step(sends(b, step), step)
        if step == 2:
            first = lax.optimization_barrier(sends(c, 1) + b["came"])[:2]
            c["came"] = sum_step(first, 1)
            crossin = gated(crossin, *c["came"])
            cq = both_halves(jnp.dot(crossin, cross_q, preferred_element_type=F32)).astype(BF16)
    out_b, memory_b = finish_rows(b)
    second = lax.optimization_barrier(sends(c, 2) + (memory_b,))
    memory_b = to_heads(second[2])
    c["came"] = sum_step(second[:2], 2)
    for step in range(3, count):
        c["came"] = sum_step(sends(c, step), step)
    out_c, memory_c = finish_rows(c)
    memory_a, memory_c = lax.optimization_barrier((memory_a, memory_c))
    memory_c = to_heads(memory_c)
    memories = [keys_values(m) for m in (memory_a, memory_b, memory_c)]
    enc_out = jnp.concatenate([out_a, out_b, out_c], 0)
    keys, values = [jnp.concatenate([m[i] for m in memories], 0) for i in range(2)]

    scores = lax.dot_general(cq, keys, (((1,), (1,)), ((), ())), preferred_element_type=F32) * (1.0 / 16.0)
    top = jnp.max(scores, axis=-1, keepdims=True)
    expo = jnp.exp(scores - top)
    whole = jnp.sum(expo, axis=-1, keepdims=True)
    context = jnp.dot(expo.astype(BF16), values, preferred_element_type=F32)
    ours = jnp.concatenate(
        [context, jnp.broadcast_to(top, (top.shape[0], 128)), jnp.broadcast_to(whole, (top.shape[0], 128))], 1
    )
    theirs = swap(ours, "section", 1)
    their_top, their_whole = theirs[:, HD : HD + 1], theirs[:, HD + 128 : HD + 129]
    most = jnp.maximum(top, their_top)
    mine, other = jnp.exp(top - most), jnp.exp(their_top - most)
    context = (context * mine + theirs[:, :HD] * other) / (whole * mine + their_whole * other)
    product = jnp.dot(context.astype(BF16), cross_out, preferred_element_type=F32).astype(BF16)
    crosssum = whole_rows(slots_sum(product), section)
    dec_out = (mid.astype(F32) + keep_factor(dec_keep) * crosssum).astype(BF16)
    return (enc_out, dec_out)


def solution(mesh):
    return jax.shard_map(
        per_device,
        mesh=mesh,
        in_specs=(
            P(("dp", "section", "tensor"), None),
            P(),
            P(None, ("section", "tensor")),
            P(None, ("section", "tensor")),
            P(("section", "tensor"), None),
            P(("dp", "section", "tensor"), None),
            P(),
            P(("dp", "section", "tensor"), None),
            P(),
            P("section", None, "tensor"),
            P("tensor", "section"),
            P(),
            P("section", "tensor"),
            P("section", None, "tensor"),
            P("tensor", "section"),
            P(("dp", "section", "tensor"), None),
        ),
        out_specs=(P(("dp", "section", "tensor"), None), P(("dp", "section", "tensor"), None)),
        check_vma=False,
    )
```

```python
import functools

import jax
import jax.numpy as jnp
from jax import lax
from jax.experimental import pallas as pl
from jax.experimental.pallas import tpu as pltpu
from jax.sharding import PartitionSpec as P

HD = 256
F32 = jnp.float32
BF16 = jnp.bfloat16


def norm_rows(x, gain):
    values = x.astype(F32)
    power = jnp.mean(values * values, axis=-1, keepdims=True)
    return values * lax.rsqrt(power + 1e-06) * gain


def keep_factor(words):
    shifts = jnp.arange(4, dtype=jnp.int32) * 3
    bits = jnp.right_shift(words[:, None, :], shifts[None, :, None]) & 7
    kept = jnp.where(bits == 7, 0.0, 8.0 / 7.0).astype(F32)
    return kept.reshape(words.shape[0], 4 * words.shape[1])


def swap(value, axis, distance):
    return lax.ppermute(value, axis, [(i, i ^ distance) for i in range(lax.axis_size(axis))])


def from_slots(value):
    count = lax.axis_size("tensor")
    return [value] + [
        lax.ppermute(value, "tensor", [(i, (i - o) % count) for i in range(count)]) for o in range(1, count)
    ]


def gated(value, *others):
    return lax.optimization_barrier((value,) + others)[0]


def slot_sum(mine, got, slot):
    block = mine.shape[0] // lax.axis_size("tensor")
    at = slice(slot * block, (slot + 1) * block)
    return mine[at].astype(F32) + got[at].astype(F32)


def sum_sends(mine, got, came, step):
    up, down = slot_sum(mine, got, lax.axis_size("tensor") - step), slot_sum(mine, got, step)
    if came is not None:
        up, down = up + came[0].astype(F32), down + came[1].astype(F32)
    return up.astype(BF16), down.astype(BF16)


def sum_step(sends, step):
    count = lax.axis_size("tensor")
    above = lax.ppermute(sends[0], "tensor", [(i, i + 1) for i in range(step)])
    below = lax.ppermute(sends[1], "tensor", [(i, i - 1) for i in range(count - step, count)])
    return lax.optimization_barrier((above, below))


def slots_sum(product):
    count = lax.axis_size("tensor")
    product = product.reshape(count, product.shape[0] // count, product.shape[1])
    total = product[0].astype(F32)
    for o in range(1, count):
        total = total + lax.ppermute(
            product[o], "tensor", [(i, (i + o) % count) for i in range(count)]
        ).astype(F32)
    return total


def half_columns(value, index):
    return lax.dynamic_slice_in_dim(value, index * (value.shape[1] // 2), value.shape[1] // 2, 1)


def in_order(own, other, section, axis):
    return jnp.where(
        section == 0, jnp.concatenate([own, other], axis), jnp.concatenate([other, own], axis)
    )


def gather_half(rows, section):
    own = half_columns(rows, section)
    other = swap(half_columns(rows, 1 - section), "section", 1)
    return jnp.concatenate(from_slots(in_order(own, other, section, 0)), 0)


def whole_rows(total, section):
    rows = total.shape[0] // 2
    own = lax.dynamic_slice_in_dim(total, section * rows, rows, 0)
    other = swap(lax.dynamic_slice_in_dim(total, (1 - section) * rows, rows, 0), "section", 1)
    return in_order(own, other, section, 1)


def both_halves(partial):
    return partial + swap(partial, "section", 1)


def gelu(x):
    return 0.5 * x * (1.0 + jnp.tanh(0.7978845608028654 * (x + 0.044715 * x * x * x)))


def ffn_kernel(hidden_steps, order, x_ref, gate_ref, up_ref, down_ref, ya_ref, yb_ref, x, hidden):
    step = pl.program_id(0)
    rows = ya_ref.shape[0]
    width = gate_ref.shape[1]
    blocks = order.shape[0]
    block = 2 * rows // blocks

    @pl.when(step == 0)
    def _():
        for slot in range(blocks):
            at = pl.multiple_of(order[slot] * block, block)
            x[slot * block : (slot + 1) * block, :] = x_ref[pl.ds(at, block), :]

    @pl.when(step < hidden_steps)
    def _():
        gate = jnp.dot(x[...], gate_ref[...], preferred_element_type=F32)
        up = jnp.dot(x[...], up_ref[...], preferred_element_type=F32)
        hidden[step] = (gelu(gate) * up).astype(BF16)

    @pl.when(step >= hidden_steps)
    def _():
        total = jnp.zeros((2 * rows, ya_ref.shape[1]), F32)
        for k in range(hidden.shape[0]):
            total += jnp.dot(
                hidden[k], down_ref[k * width : (k + 1) * width, :], preferred_element_type=F32
            )
        ya_ref[...] = total[:rows].astype(BF16)
        yb_ref[...] = total[rows:].astype(BF16)


def ffn(x, order, w_gate, w_up, w_down):
    rows, features = x.shape
    units = w_gate.shape[1]
    width = min(256, units)
    tile = 512
    first, last = units // width, features // tile
    return pl.pallas_call(
        functools.partial(ffn_kernel, first),
        grid_spec=pltpu.PrefetchScalarGridSpec(
            num_scalar_prefetch=1,
            grid=(first + last,),
            in_specs=[
                pl.BlockSpec((rows, features), lambda i, t: (0, 0), pipeline_mode=pl.Buffered(1)),
                pl.BlockSpec((features, width), lambda i, t: (0, jnp.minimum(i, first - 1))),
                pl.BlockSpec((features, width), lambda i, t: (0, jnp.minimum(i, first - 1))),
                pl.BlockSpec((units, tile), lambda i, t: (0, jnp.maximum(i - first, 0))),
            ],
            out_specs=[pl.BlockSpec((rows // 2, tile), lambda i, t: (0, jnp.maximum(i - first, 0)))] * 2,
            scratch_shapes=[
                pltpu.VMEM((rows, features), BF16),
                pltpu.VMEM((first, rows, width), BF16),
            ],
        ),
        out_shape=[jax.ShapeDtypeStruct((rows // 2, features), BF16)] * 2,
        compiler_params=pltpu.CompilerParams(vmem_limit_bytes=48 * 2**20),
        cost_estimate=pl.CostEstimate(
            flops=1024, bytes_accessed=1024, transcendentals=0
        ),
        name="ffn",
    )(order, x, w_gate, w_up, w_down)


def per_device(
    source,
    enc_gain,
    w_gate,
    w_up,
    w_down,
    enc_keep,
    final_gain,
    target,
    self_gain,
    self_qkv,
    self_out,
    cross_gain,
    cross_q,
    cross_kv,
    cross_out,
    dec_keep,
):
    section = lax.axis_index("section")
    count, tensor = lax.axis_size("tensor"), lax.axis_index("tensor")
    rows = target.shape[0]
    slot_chip = lax.rem(tensor + jnp.arange(count, dtype=jnp.int32), count)
    order = jnp.concatenate([section * count + slot_chip, (1 - section) * count + slot_chip])

    selfin = gather_half(norm_rows(target, self_gain).astype(BF16), section)

    normed = norm_rows(source, enc_gain).astype(BF16)
    block = normed.shape[0] // 2
    near = [
        lax.all_gather(normed[c * block : (c + 1) * block], ("section", "tensor"), axis=0, tiled=True)
        for c in range(2)
    ]
    kv = jnp.transpose(cross_kv, (1, 0, 2))
    kv = in_order(kv, swap(kv, "section", 1), section, 1)

    qkv_w = jnp.transpose(self_qkv, (1, 0, 2))
    q, k, v = [jnp.dot(selfin, qkv_w[i], preferred_element_type=F32) for i in range(3)]
    q, k, v = [y.astype(BF16) for y in both_halves(jnp.stack([q, k, v]))]
    positions = (
        (jnp.arange(2, dtype=jnp.int32)[None, :] * count + slot_chip[:, None])[:, :, None] * rows
        + jnp.arange(rows, dtype=jnp.int32)
    ).reshape(-1)
    scores = lax.dot_general(q, k, (((1,), (1,)), ((), ())), preferred_element_type=F32) * (1.0 / 16.0)
    scores = jnp.where(positions[None, :] <= positions[:, None], scores, F32(-1e30))
    expo = jnp.exp(scores - jnp.max(scores, axis=-1, keepdims=True))
    probs = (expo / jnp.sum(expo, axis=-1, keepdims=True)).astype(BF16)
    context = jnp.dot(probs, v, preferred_element_type=F32).astype(BF16)
    product = jnp.dot(context, self_out, preferred_element_type=F32).astype(BF16)
    total = slots_sum(product)

    mine, theirs = ffn(gated(near[0], product), order, w_gate, w_up, w_down)
    got = swap(theirs, "section", 1)
    came = sum_step(sum_sends(mine, got, None, 1), 1)
    total = gated(total, *came)
    mid = (target.astype(F32) + whole_rows(total, section)).astype(BF16)
    crossin = gather_half(norm_rows(mid, cross_gain).astype(BF16), section)
    for step in range(2, count - 1):
        came = sum_step(sum_sends(mine, got, came, step), step)
    sends = sum_sends(mine, got, came, count - 1)
    came = sum_step(sends, count - 1)
    mine_b, theirs_b = ffn(gated(near[1], *sends), order, w_gate, w_up, w_down)

    def finish_rows(c, mine, got, came):
        at = slice(c * block, (c + 1) * block)
        total = slot_sum(mine, got, 0) + came[0].astype(F32) + came[1].astype(F32)
        out = (source[at].astype(F32) + keep_factor(enc_keep[at]) * total).astype(BF16)
        memory = norm_rows(out, final_gain).astype(BF16)
        return out, memory

    def to_heads(memory):
        return lax.all_gather(memory, "tensor", axis=0, tiled=True)

    def keys_values(memory):
        return [jnp.dot(memory, kv[i], preferred_element_type=F32).astype(BF16) for i in range(2)]

    out_a, memory_a = finish_rows(0, mine, got, came)
    memory_a, mine_b = lax.optimization_barrier((memory_a, mine_b))
    memory_a = to_heads(memory_a)
    got = swap(theirs_b, "section", 1)
    came = sum_step(sum_sends(mine_b, got, None, 1), 1)
    crossin = gated(crossin, *came)
    cq = both_halves(jnp.dot(crossin, cross_q, preferred_element_type=F32)).astype(BF16)
    for step in range(2, count):
        sends = sum_sends(mine_b, got, came, step)
        if step == count - 1:
            sends = lax.optimization_barrier(sends + (memory_a,))[:2]
        came = sum_step(sends, step)
    out_b, memory_b = finish_rows(1, mine_b, got, came)
    memory_b = to_heads(memory_b)
    memory_a = gated(memory_a, out_b)
    keys_a, values_a = keys_values(memory_a)
    keys_b, values_b = keys_values(memory_b)
    enc_out = jnp.concatenate([out_a, out_b], 0)
    keys, values = jnp.concatenate([keys_a, keys_b], 0), jnp.concatenate([values_a, values_b], 0)

    scores = lax.dot_general(cq, keys, (((1,), (1,)), ((), ())), preferred_element_type=F32) * (1.0 / 16.0)
    top = jnp.max(scores, axis=-1, keepdims=True)
    expo = jnp.exp(scores - top)
    whole = jnp.sum(expo, axis=-1, keepdims=True)
    context = jnp.dot(expo.astype(BF16), values, preferred_element_type=F32)
    ours = jnp.concatenate(
        [context, jnp.broadcast_to(top, (top.shape[0], 128)), jnp.broadcast_to(whole, (top.shape[0], 128))], 1
    )
    theirs = swap(ours, "section", 1)
    their_top, their_whole = theirs[:, HD : HD + 1], theirs[:, HD + 128 : HD + 129]
    most = jnp.maximum(top, their_top)
    mine, other = jnp.exp(top - most), jnp.exp(their_top - most)
    context = (context * mine + theirs[:, :HD] * other) / (whole * mine + their_whole * other)
    product = jnp.dot(context.astype(BF16), cross_out, preferred_element_type=F32).astype(BF16)
    crosssum = whole_rows(slots_sum(product), section)
    dec_out = (mid.astype(F32) + keep_factor(dec_keep) * crosssum).astype(BF16)
    return (enc_out, dec_out)


def solution(mesh):
    return jax.shard_map(
        per_device,
        mesh=mesh,
        in_specs=(
            P(("dp", "section", "tensor"), None),
            P(),
            P(None, ("section", "tensor")),
            P(None, ("section", "tensor")),
            P(("section", "tensor"), None),
            P(("dp", "section", "tensor"), None),
            P(),
            P(("dp", "section", "tensor"), None),
            P(),
            P("section", None, "tensor"),
            P("tensor", "section"),
            P(),
            P("section", "tensor"),
            P("section", None, "tensor"),
            P("tensor", "section"),
            P(("dp", "section", "tensor"), None),
        ),
        out_specs=(P(("dp", "section", "tensor"), None), P(("dp", "section", "tensor"), None)),
        check_vma=False,
    )
```

```python
import functools

import jax
import jax.numpy as jnp
from jax import lax
from jax.experimental import pallas as pl
from jax.experimental.pallas import tpu as pltpu
from jax.sharding import PartitionSpec as P

HD = 256
F32 = jnp.float32
BF16 = jnp.bfloat16
STATS = 5


def norm_rows(x, gain):
    values = x.astype(F32)
    power = jnp.mean(values * values, axis=-1, keepdims=True)
    return values * lax.rsqrt(power + 1e-06) * gain


def keep_factor(words):
    shifts = jnp.arange(4, dtype=jnp.int32) * 3
    bits = jnp.right_shift(words[:, None, :], shifts[None, :, None]) & 7
    kept = jnp.where(bits == 7, 0.0, 8.0 / 7.0).astype(F32)
    return kept.reshape(words.shape[0], 4 * words.shape[1])


def swap(value, axis, distance):
    return lax.ppermute(value, axis, [(i, i ^ distance) for i in range(lax.axis_size(axis))])


def from_slots(value):
    count = lax.axis_size("tensor")
    return [value] + [
        lax.ppermute(value, "tensor", [(i, (i - o) % count) for i in range(count)]) for o in range(1, count)
    ]


def gated(value, *others):
    return lax.optimization_barrier((value,) + others)[0]


def slot_sum(mine, got, slot):
    block = mine.shape[0] // lax.axis_size("tensor")
    at = slice(slot * block, (slot + 1) * block)
    return mine[at].astype(F32) + got[at].astype(F32)


def sum_sends(mine, got, came, step):
    up, down = slot_sum(mine, got, lax.axis_size("tensor") - step), slot_sum(mine, got, step)
    if came is not None:
        up, down = up + came[0].astype(F32), down + came[1].astype(F32)
    return up.astype(BF16), down.astype(BF16)


def sum_step(sends, step):
    count = lax.axis_size("tensor")
    above = lax.ppermute(sends[0], "tensor", [(i, i + 1) for i in range(step)])
    below = lax.ppermute(sends[1], "tensor", [(i, i - 1) for i in range(count - step, count)])
    return lax.optimization_barrier((above, below))


def slots_sum(product):
    count = lax.axis_size("tensor")
    product = product.reshape(count, product.shape[0] // count, product.shape[1])
    total = product[0].astype(F32)
    for o in range(1, count):
        total = total + lax.ppermute(
            product[o], "tensor", [(i, (i + o) % count) for i in range(count)]
        ).astype(F32)
    return total


def half_columns(value, index):
    return lax.dynamic_slice_in_dim(value, index * (value.shape[1] // 2), value.shape[1] // 2, 1)


def in_order(own, other, section, axis):
    return jnp.where(
        section == 0, jnp.concatenate([own, other], axis), jnp.concatenate([other, own], axis)
    )


def gather_half(rows, section):
    own = half_columns(rows, section)
    other = swap(half_columns(rows, 1 - section), "section", 1)
    return jnp.concatenate(from_slots(in_order(own, other, section, 0)), 0)


def whole_rows(total, section):
    rows = total.shape[0] // 2
    own = lax.dynamic_slice_in_dim(total, section * rows, rows, 0)
    other = swap(lax.dynamic_slice_in_dim(total, (1 - section) * rows, rows, 0), "section", 1)
    return in_order(own, other, section, 1)


def both_halves(partial):
    return partial + swap(partial, "section", 1)


def gelu(x):
    return 0.5 * x * (1.0 + jnp.tanh(0.7978845608028654 * (x + 0.044715 * x * x * x)))


def ffn_kernel(ins, order, x_ref, gate_ref, up_ref, down_ref, y_ref, gate, up, hidden):
    step = pl.program_id(0)
    _, blocks, block, _ = x_ref.shape
    rows, depth = blocks * block, gate_ref.shape[0]

    for k in range(ins):

        @pl.when(step == k)
        def _():
            part = x_ref[0, :, :, k * depth : (k + 1) * depth].reshape(rows, depth)
            one = jnp.dot(part, gate_ref[...], preferred_element_type=F32)
            two = jnp.dot(part, up_ref[...], preferred_element_type=F32)
            if k == 0:
                gate[...] = one
                up[...] = two
            else:
                gate[...] += one
                up[...] += two

    @pl.when(step == ins)
    def _():
        for slot in range(blocks):
            at = pl.ds(pl.multiple_of(order[1 + slot] * block, block), block)
            hidden[slot * block : (slot + 1) * block, :] = (gelu(gate[at, :]) * up[at, :]).astype(BF16)

    @pl.when(step >= ins)
    def _():
        y_ref[...] = jnp.dot(hidden[...], down_ref[...], preferred_element_type=F32).astype(BF16)


def ffn(x, order, w_gate, w_up, w_down):
    _, blocks, block, features = x.shape
    units = w_gate.shape[1]
    rows, depth, tile = blocks * block, 512, 1024
    ins, outs = features // depth, features // tile
    return pl.pallas_call(
        functools.partial(ffn_kernel, ins),
        grid_spec=pltpu.PrefetchScalarGridSpec(
            num_scalar_prefetch=1,
            grid=(ins + outs,),
            in_specs=[
                pl.BlockSpec(
                    (1, blocks, block, features), lambda i, t: (t[0], 0, 0, 0), pipeline_mode=pl.Buffered(1)
                ),
                pl.BlockSpec((depth, units), lambda i, t: (jnp.minimum(i, ins - 1), 0)),
                pl.BlockSpec((depth, units), lambda i, t: (jnp.minimum(i, ins - 1), 0)),
                pl.BlockSpec((units, tile), lambda i, t: (0, jnp.maximum(i - ins, 0))),
            ],
            out_specs=pl.BlockSpec((rows, tile), lambda i, t: (0, jnp.maximum(i - ins, 0))),
            scratch_shapes=[
                pltpu.VMEM((rows, units), F32),
                pltpu.VMEM((rows, units), F32),
                pltpu.VMEM((rows, units), BF16),
            ],
        ),
        out_shape=jax.ShapeDtypeStruct((rows, features), BF16),
        compiler_params=pltpu.CompilerParams(vmem_limit_bytes=44 * 2**20),
        cost_estimate=pl.CostEstimate(flops=1024, bytes_accessed=1024, transcendentals=0),
        name="ffn",
    )(order, x, w_gate, w_up, w_down)


def attend_kernel(groups, table, mem_ref, cq_ref, *refs):
    locals_, shares, out_ref = refs[:2], refs[2:-1], refs[-1]
    slot = pl.program_id(0)
    depth = shares[0].shape[2]

    def attend(pieces):
        keys = jnp.zeros((mem_ref.shape[0], HD), F32)
        values = jnp.zeros((mem_ref.shape[0], HD), F32)
        for index, k, v in pieces:
            x = mem_ref[:, pl.ds(pl.multiple_of(table[index] * depth, depth), depth)]
            keys += jnp.dot(x, k, preferred_element_type=F32)
            values += jnp.dot(x, v, preferred_element_type=F32)
        k, v = keys.astype(BF16), values.astype(BF16)
        scores = lax.dot_general(cq_ref[0], k, (((1,), (1,)), ((), ())), preferred_element_type=F32)
        scores = scores * (1.0 / 16.0)
        top = jnp.max(scores, axis=-1, keepdims=True)
        expo = jnp.exp(scores - top)
        total = jnp.sum(expo, axis=-1, keepdims=True)
        context = jnp.dot(expo.astype(BF16), v, preferred_element_type=F32)
        out_ref[0, :, :HD] = context.astype(BF16)
        lanes = lax.broadcasted_iota(jnp.int32, (scores.shape[0], 128), 1)
        high = top.astype(BF16).astype(F32)
        rest = top - high
        middle = rest.astype(BF16).astype(F32)
        sum_high = total.astype(BF16).astype(F32)
        stats = jnp.zeros(lanes.shape, F32)
        for index, piece in enumerate((high, middle, rest - middle, sum_high, total - sum_high)):
            stats = jnp.where(lanes == index, piece, stats)
        out_ref[0, :, HD:] = stats.astype(BF16)

    @pl.when(slot == 0)
    def _():
        attend(
            [
                (2 * groups + place * groups + g, ref[0, g * depth : (g + 1) * depth, :], ref[1, g * depth : (g + 1) * depth, :])
                for place, ref in enumerate(locals_)
                for g in range(groups)
            ]
        )

    @pl.when(slot > 0)
    def _():
        attend([(i, ref[0, 0], ref[0, 1]) for i, ref in enumerate(shares)])


def attend_own_keys(memory, queries, own_head, shares, table):
    rows, features = memory.shape
    heads, count, width = queries.shape
    _, two, depth, _ = shares[0].shape
    share = pl.BlockSpec((1, two, depth, width), lambda h, t: (jnp.maximum(h - 1, 0), 0, 0, 0))
    whole = pl.BlockSpec(own_head[0].shape, lambda h, t: (0, 0, 0), pipeline_mode=pl.Buffered(1))
    return pl.pallas_call(
        functools.partial(attend_kernel, len(shares) // 2),
        grid_spec=pltpu.PrefetchScalarGridSpec(
            num_scalar_prefetch=1,
            grid=(heads,),
            in_specs=[
                pl.BlockSpec((rows, features), lambda h, t: (0, 0)),
                pl.BlockSpec((1, count, width), lambda h, t: (h, 0, 0)),
                whole,
                whole,
            ]
            + [share] * len(shares),
            out_specs=pl.BlockSpec((1, count, width + 128), lambda h, t: (h, 0, 0)),
        ),
        out_shape=jax.ShapeDtypeStruct((heads, count, width + 128), BF16),
        compiler_params=pltpu.CompilerParams(vmem_limit_bytes=40 * 2**20),
        cost_estimate=pl.CostEstimate(flops=1024, bytes_accessed=1024, transcendentals=0),
        name="attend_own_keys",
    )(table, memory, queries, *own_head, *shares)


def merged(contexts, tops, wholes):
    most = functools.reduce(jnp.maximum, tops)
    weights = [jnp.exp(top - most) for top in tops]
    context = sum(c * w for c, w in zip(contexts, weights))
    return context, most, sum(s * w for s, w in zip(wholes, weights))


def per_device(
    source,
    enc_gain,
    w_gate,
    w_up,
    w_down,
    enc_keep,
    final_gain,
    target,
    self_gain,
    self_qkv,
    self_out,
    cross_gain,
    cross_q,
    cross_kv,
    cross_out,
    dec_keep,
):
    section, group = lax.axis_index("section"), lax.axis_index("dp")
    count, tensor = lax.axis_size("tensor"), lax.axis_index("tensor")
    groups = lax.axis_size("dp")
    rows = target.shape[0]
    slot_chip = lax.rem(tensor + jnp.arange(count, dtype=jnp.int32), count)

    selfin = gather_half(norm_rows(target, self_gain).astype(BF16), section)

    normed = norm_rows(source, enc_gain).astype(BF16)
    x = lax.all_gather(normed, ("section", "tensor"), axis=0, tiled=False)
    x = x.reshape((2, count) + normed.shape)
    own_head = [jnp.transpose(cross_kv, (1, 0, 2))]
    own_head.append(swap(own_head[0], "section", 1))

    qkv_w = jnp.transpose(self_qkv, (1, 0, 2))
    q, k, v = [jnp.dot(selfin, qkv_w[i], preferred_element_type=F32) for i in range(3)]
    q, k, v = [y.astype(BF16) for y in both_halves(jnp.stack([q, k, v]))]
    positions = (
        (jnp.arange(2, dtype=jnp.int32)[None, :] * count + slot_chip[:, None])[:, :, None] * rows
        + jnp.arange(rows, dtype=jnp.int32)
    ).reshape(-1)
    scores = lax.dot_general(q, k, (((1,), (1,)), ((), ())), preferred_element_type=F32) * (1.0 / 16.0)
    scores = jnp.where(positions[None, :] <= positions[:, None], scores, F32(-1e30))
    expo = jnp.exp(scores - jnp.max(scores, axis=-1, keepdims=True))
    probs = (expo / jnp.sum(expo, axis=-1, keepdims=True)).astype(BF16)
    context = jnp.dot(probs, v, preferred_element_type=F32).astype(BF16)
    product = jnp.dot(context, self_out, preferred_element_type=F32).astype(BF16)
    total = slots_sum(product)

    x, product, other_head = lax.optimization_barrier((x, product, own_head[1]))
    own_head[1] = other_head
    depth = cross_kv.shape[0] // groups
    share = gated(lax.dynamic_slice_in_dim(own_head[0], group * depth, depth, 1), x)
    shares = [jnp.stack(from_slots(share)[1:])]

    theirs = ffn(x, jnp.concatenate([(1 - section)[None], slot_chip]), w_gate, w_up, w_down)
    got = swap(theirs, "section", 1)
    x = gated(x, theirs)
    mine = ffn(x, jnp.concatenate([section[None], slot_chip]), w_gate, w_up, w_down)
    mine, shares[0] = lax.optimization_barrier((mine, shares[0]))
    shares += [swap(shares[0], "dp", j) for j in range(1, groups)]

    came = sum_step(sum_sends(mine, got, None, 1), 1)
    total = gated(total, mine)
    mid = (target.astype(F32) + whole_rows(total, section)).astype(BF16)
    crossin = gather_half(norm_rows(mid, cross_gain).astype(BF16), section)
    for step in range(2, count):
        sends = sum_sends(mine, got, came, step)
        if step == 2:
            near = tuple(shares[1 : 1 + groups // 2])
            held = lax.optimization_barrier(sends + near + (crossin,))
            sends, shares[1 : 1 + groups // 2], crossin = held[:2], list(held[2:-1]), held[-1]
            cq = both_halves(jnp.dot(crossin, cross_q, preferred_element_type=F32)).astype(BF16)
            cq = jnp.roll(cq.reshape(count, 2, rows, HD), tensor, axis=0)
            cq = jnp.transpose(cq, (1, 0, 2, 3)).reshape(2 * count * rows, HD)
            queries = jnp.stack(from_slots(cq))
        elif step == count - 1:
            rest = tuple(shares[1 + groups // 2 :])
            held = lax.optimization_barrier(sends + rest)
            sends, shares[1 + groups // 2 :] = held[:2], list(held[2:])
        came = sum_step(sends, step)
    total = slot_sum(mine, got, 0) + came[0].astype(F32) + came[1].astype(F32)
    enc_out = (source.astype(F32) + keep_factor(enc_keep) * total).astype(BF16)
    memory = norm_rows(enc_out, final_gain).astype(BF16)

    at = jnp.stack([group ^ j for j in range(groups)])
    places = [section * groups, (1 - section) * groups]
    table = jnp.concatenate(
        [p + at for p in places] + [p + jnp.arange(groups, dtype=jnp.int32) for p in places]
    ).astype(jnp.int32)
    shares += [swap(s, "section", 1) for s in shares]
    parts = attend_own_keys(memory, queries, own_head, shares, table)
    parts = [parts[0]] + [
        lax.ppermute(parts[o], "tensor", [(i, (i + o) % count) for i in range(count)]) for o in range(1, count)
    ]
    parts = [p.astype(F32) for p in parts]
    context, top, whole = merged(
        [p[:, :HD] for p in parts],
        [p[:, HD : HD + 1] + p[:, HD + 1 : HD + 2] + p[:, HD + 2 : HD + 3] for p in parts],
        [p[:, HD + 3 : HD + 4] + p[:, HD + 4 : HD + 5] for p in parts],
    )
    pad = [jnp.broadcast_to(y, (y.shape[0], 128)) for y in (top, whole)]
    other = swap(jnp.concatenate([context] + pad, 1), "section", 1)
    context, top, whole = merged(
        [context, other[:, :HD]], [top, other[:, HD : HD + 1]], [whole, other[:, HD + 128 : HD + 129]]
    )
    context = (context / whole).astype(BF16).reshape(2, count, rows, HD)
    context = jnp.roll(jnp.transpose(context, (1, 0, 2, 3)), -tensor, axis=0).reshape(2 * count * rows, HD)
    product = jnp.dot(context, cross_out, preferred_element_type=F32).astype(BF16)
    crosssum = whole_rows(slots_sum(product), section)
    dec_out = (mid.astype(F32) + keep_factor(dec_keep) * crosssum).astype(BF16)
    return (enc_out, dec_out)


def solution(mesh):
    return jax.shard_map(
        per_device,
        mesh=mesh,
        in_specs=(
            P(("dp", "section", "tensor"), None),
            P(),
            P(None, ("section", "tensor")),
            P(None, ("section", "tensor")),
            P(("section", "tensor"), None),
            P(("dp", "section", "tensor"), None),
            P(),
            P(("dp", "section", "tensor"), None),
            P(),
            P("section", None, "tensor"),
            P("tensor", "section"),
            P(),
            P("section", "tensor"),
            P("section", None, "tensor"),
            P("tensor", "section"),
            P(("dp", "section", "tensor"), None),
        ),
        out_specs=(P(("dp", "section", "tensor"), None), P(("dp", "section", "tensor"), None)),
        check_vma=False,
    )
```

```python
import functools

import jax
import jax.numpy as jnp
from jax import lax
from jax.experimental import pallas as pl
from jax.experimental.pallas import tpu as pltpu
from jax.sharding import PartitionSpec as P

HD = 256
F32 = jnp.float32
BF16 = jnp.bfloat16
STATS = 5


def norm_rows(x, gain):
    values = x.astype(F32)
    power = jnp.mean(values * values, axis=-1, keepdims=True)
    return values * lax.rsqrt(power + 1e-06) * gain


def keep_factor(words):
    shifts = jnp.arange(4, dtype=jnp.int32) * 3
    bits = jnp.right_shift(words[:, None, :], shifts[None, :, None]) & 7
    kept = jnp.where(bits == 7, 0.0, 8.0 / 7.0).astype(F32)
    return kept.reshape(words.shape[0], 4 * words.shape[1])


def swap(value, axis, distance):
    return lax.ppermute(value, axis, [(i, i ^ distance) for i in range(lax.axis_size(axis))])


def from_slots(value):
    count = lax.axis_size("tensor")
    return [value] + [
        lax.ppermute(value, "tensor", [(i, (i - o) % count) for i in range(count)]) for o in range(1, count)
    ]


def gated(value, *others):
    return lax.optimization_barrier((value,) + others)[0]


def slot_sum(mine, got, slot):
    block = mine.shape[0] // lax.axis_size("tensor")
    at = slice(slot * block, (slot + 1) * block)
    return mine[at].astype(F32) + got[at].astype(F32)


def sum_sends(mine, got, came, step):
    up, down = slot_sum(mine, got, lax.axis_size("tensor") - step), slot_sum(mine, got, step)
    if came is not None:
        up, down = up + came[0].astype(F32), down + came[1].astype(F32)
    return up.astype(BF16), down.astype(BF16)


def sum_step(sends, step):
    count = lax.axis_size("tensor")
    above = lax.ppermute(sends[0], "tensor", [(i, i + 1) for i in range(step)])
    below = lax.ppermute(sends[1], "tensor", [(i, i - 1) for i in range(count - step, count)])
    return lax.optimization_barrier((above, below))


def slots_sum(product):
    count = lax.axis_size("tensor")
    product = product.reshape(count, product.shape[0] // count, product.shape[1])
    total = product[0].astype(F32)
    for o in range(1, count):
        total = total + lax.ppermute(
            product[o], "tensor", [(i, (i + o) % count) for i in range(count)]
        ).astype(F32)
    return total


def half_columns(value, index):
    return lax.dynamic_slice_in_dim(value, index * (value.shape[1] // 2), value.shape[1] // 2, 1)


def in_order(own, other, section, axis):
    return jnp.where(
        section == 0, jnp.concatenate([own, other], axis), jnp.concatenate([other, own], axis)
    )


def gather_half(rows, section):
    own = half_columns(rows, section)
    other = swap(half_columns(rows, 1 - section), "section", 1)
    return jnp.concatenate(from_slots(in_order(own, other, section, 0)), 0)


def whole_rows(total, section):
    rows = total.shape[0] // 2
    own = lax.dynamic_slice_in_dim(total, section * rows, rows, 0)
    other = swap(lax.dynamic_slice_in_dim(total, (1 - section) * rows, rows, 0), "section", 1)
    return in_order(own, other, section, 1)


def both_halves(partial):
    return partial + swap(partial, "section", 1)


def gelu(x):
    return 0.5 * x * (1.0 + jnp.tanh(0.7978845608028654 * (x + 0.044715 * x * x * x)))


def ffn_kernel(ins, order, x_ref, gate_ref, up_ref, down_ref, y_ref, gate, up, hidden):
    step = pl.program_id(0)
    _, blocks, block, _ = x_ref.shape
    rows, depth = blocks * block, gate_ref.shape[0]

    for k in range(ins):

        @pl.when(step == k)
        def _():
            part = x_ref[0, :, :, k * depth : (k + 1) * depth].reshape(rows, depth)
            one = jnp.dot(part, gate_ref[...], preferred_element_type=F32)
            two = jnp.dot(part, up_ref[...], preferred_element_type=F32)
            if k == 0:
                gate[...] = one
                up[...] = two
            else:
                gate[...] += one
                up[...] += two

    @pl.when(step == ins)
    def _():
        for slot in range(blocks):
            at = pl.ds(pl.multiple_of(order[1 + slot] * block, block), block)
            hidden[slot * block : (slot + 1) * block, :] = (gelu(gate[at, :]) * up[at, :]).astype(BF16)

    @pl.when(step >= ins)
    def _():
        y_ref[...] = jnp.dot(hidden[...], down_ref[...], preferred_element_type=F32).astype(BF16)


def ffn(x, order, w_gate, w_up, w_down):
    _, blocks, block, features = x.shape
    units = w_gate.shape[1]
    rows, depth, tile = blocks * block, 512, 1024
    ins, outs = features // depth, features // tile
    return pl.pallas_call(
        functools.partial(ffn_kernel, ins),
        grid_spec=pltpu.PrefetchScalarGridSpec(
            num_scalar_prefetch=1,
            grid=(ins + outs,),
            in_specs=[
                pl.BlockSpec(
                    (1, blocks, block, features), lambda i, t: (t[0], 0, 0, 0), pipeline_mode=pl.Buffered(1)
                ),
                pl.BlockSpec((depth, units), lambda i, t: (jnp.minimum(i, ins - 1), 0)),
                pl.BlockSpec((depth, units), lambda i, t: (jnp.minimum(i, ins - 1), 0)),
                pl.BlockSpec((units, tile), lambda i, t: (0, jnp.maximum(i - ins, 0))),
            ],
            out_specs=pl.BlockSpec((rows, tile), lambda i, t: (0, jnp.maximum(i - ins, 0))),
            scratch_shapes=[
                pltpu.VMEM((rows, units), F32),
                pltpu.VMEM((rows, units), F32),
                pltpu.VMEM((rows, units), BF16),
            ],
        ),
        out_shape=jax.ShapeDtypeStruct((rows, features), BF16),
        compiler_params=pltpu.CompilerParams(vmem_limit_bytes=44 * 2**20),
        cost_estimate=pl.CostEstimate(flops=1024, bytes_accessed=1024, transcendentals=0),
        name="ffn",
    )(order, x, w_gate, w_up, w_down)


def attend_kernel(groups, table, mem_ref, cq_ref, *refs):
    locals_, shares, out_ref = refs[:2], refs[2:-1], refs[-1]
    slot = pl.program_id(0)
    depth = shares[0].shape[2]

    def attend(pieces):
        keys = jnp.zeros((mem_ref.shape[0], HD), F32)
        values = jnp.zeros((mem_ref.shape[0], HD), F32)
        for index, k, v in pieces:
            x = mem_ref[:, pl.ds(pl.multiple_of(table[index] * depth, depth), depth)]
            keys += jnp.dot(x, k, preferred_element_type=F32)
            values += jnp.dot(x, v, preferred_element_type=F32)
        k, v = keys.astype(BF16), values.astype(BF16)
        scores = lax.dot_general(cq_ref[0], k, (((1,), (1,)), ((), ())), preferred_element_type=F32)
        scores = scores * (1.0 / 16.0)
        top = jnp.max(scores, axis=-1, keepdims=True)
        expo = jnp.exp(scores - top)
        total = jnp.sum(expo, axis=-1, keepdims=True)
        context = jnp.dot(expo.astype(BF16), v, preferred_element_type=F32)
        out_ref[0, :, :HD] = context.astype(BF16)
        lanes = lax.broadcasted_iota(jnp.int32, (scores.shape[0], 128), 1)
        high = top.astype(BF16).astype(F32)
        rest = top - high
        middle = rest.astype(BF16).astype(F32)
        sum_high = total.astype(BF16).astype(F32)
        stats = jnp.zeros(lanes.shape, F32)
        for index, piece in enumerate((high, middle, rest - middle, sum_high, total - sum_high)):
            stats = jnp.where(lanes == index, piece, stats)
        out_ref[0, :, HD:] = stats.astype(BF16)

    @pl.when(slot == 0)
    def _():
        attend(
            [
                (2 * groups + place * groups + g, ref[0, g * depth : (g + 1) * depth, :], ref[1, g * depth : (g + 1) * depth, :])
                for place, ref in enumerate(locals_)
                for g in range(groups)
            ]
        )

    @pl.when(slot > 0)
    def _():
        attend([(i, ref[0, 0], ref[0, 1]) for i, ref in enumerate(shares)])


def attend_own_keys(memory, queries, own_head, shares, table):
    rows, features = memory.shape
    heads, count, width = queries.shape
    _, two, depth, _ = shares[0].shape
    share = pl.BlockSpec((1, two, depth, width), lambda h, t: (jnp.maximum(h - 1, 0), 0, 0, 0))
    whole = pl.BlockSpec(own_head[0].shape, lambda h, t: (0, 0, 0), pipeline_mode=pl.Buffered(1))
    return pl.pallas_call(
        functools.partial(attend_kernel, len(shares) // 2),
        grid_spec=pltpu.PrefetchScalarGridSpec(
            num_scalar_prefetch=1,
            grid=(heads,),
            in_specs=[
                pl.BlockSpec((rows, features), lambda h, t: (0, 0)),
                pl.BlockSpec((1, count, width), lambda h, t: (h, 0, 0)),
                whole,
                whole,
            ]
            + [share] * len(shares),
            out_specs=pl.BlockSpec((1, count, width + 128), lambda h, t: (h, 0, 0)),
        ),
        out_shape=jax.ShapeDtypeStruct((heads, count, width + 128), BF16),
        compiler_params=pltpu.CompilerParams(vmem_limit_bytes=40 * 2**20),
        cost_estimate=pl.CostEstimate(flops=1024, bytes_accessed=1024, transcendentals=0),
        name="attend_own_keys",
    )(table, memory, queries, *own_head, *shares)


def merged(contexts, tops, wholes):
    most = functools.reduce(jnp.maximum, tops)
    weights = [jnp.exp(top - most) for top in tops]
    context = sum(c * w for c, w in zip(contexts, weights))
    return context, most, sum(s * w for s, w in zip(wholes, weights))


def per_device(
    source,
    enc_gain,
    w_gate,
    w_up,
    w_down,
    enc_keep,
    final_gain,
    target,
    self_gain,
    self_qkv,
    self_out,
    cross_gain,
    cross_q,
    cross_kv,
    cross_out,
    dec_keep,
):
    section, group = lax.axis_index("section"), lax.axis_index("dp")
    count, tensor = lax.axis_size("tensor"), lax.axis_index("tensor")
    groups = lax.axis_size("dp")
    rows = target.shape[0]
    slot_chip = lax.rem(tensor + jnp.arange(count, dtype=jnp.int32), count)

    selfin = gather_half(norm_rows(target, self_gain).astype(BF16), section)

    normed = norm_rows(source, enc_gain).astype(BF16)
    x = lax.all_gather(normed, ("section", "tensor"), axis=0, tiled=False)
    x = x.reshape((2, count) + normed.shape)
    own_head = [jnp.transpose(cross_kv, (1, 0, 2))]
    own_head.append(swap(own_head[0], "section", 1))

    qkv_w = jnp.transpose(self_qkv, (1, 0, 2))
    q, k, v = [jnp.dot(selfin, qkv_w[i], preferred_element_type=F32) for i in range(3)]
    q, k, v = [y.astype(BF16) for y in both_halves(jnp.stack([q, k, v]))]
    positions = (
        (jnp.arange(2, dtype=jnp.int32)[None, :] * count + slot_chip[:, None])[:, :, None] * rows
        + jnp.arange(rows, dtype=jnp.int32)
    ).reshape(-1)
    scores = lax.dot_general(q, k, (((1,), (1,)), ((), ())), preferred_element_type=F32) * (1.0 / 16.0)
    scores = jnp.where(positions[None, :] <= positions[:, None], scores, F32(-1e30))
    expo = jnp.exp(scores - jnp.max(scores, axis=-1, keepdims=True))
    probs = (expo / jnp.sum(expo, axis=-1, keepdims=True)).astype(BF16)
    context = jnp.dot(probs, v, preferred_element_type=F32).astype(BF16)
    product = jnp.dot(context, self_out, preferred_element_type=F32).astype(BF16)
    total = slots_sum(product)

    mid = (target.astype(F32) + whole_rows(total, section)).astype(BF16)
    crossin = norm_rows(mid, cross_gain).astype(BF16)
    x, crossin, other_head = lax.optimization_barrier((x, crossin, own_head[1]))
    own_head[1] = other_head
    crossin = gather_half(crossin, section)

    depth = cross_kv.shape[0] // groups
    share = gated(lax.dynamic_slice_in_dim(own_head[0], group * depth, depth, 1), x)
    share = lax.all_gather(share, "tensor", axis=0, tiled=False)
    shares = [jnp.roll(share, -tensor, axis=0)[1:]]

    theirs = ffn(x, jnp.concatenate([(1 - section)[None], slot_chip]), w_gate, w_up, w_down)
    theirs, crossin = lax.optimization_barrier((theirs, crossin))
    got = swap(theirs, "section", 1)
    cq = both_halves(jnp.dot(crossin, cross_q, preferred_element_type=F32)).astype(BF16)
    cq = jnp.roll(cq.reshape(count, 2, rows, HD), tensor, axis=0)
    cq = jnp.transpose(cq, (1, 0, 2, 3)).reshape(2 * count * rows, HD)
    x, cq, shares[0] = lax.optimization_barrier((x, cq, shares[0]))
    queries = jnp.stack(from_slots(cq))
    mine = ffn(x, jnp.concatenate([section[None], slot_chip]), w_gate, w_up, w_down)
    shares += [swap(shares[0], "dp", j) for j in range(1, groups)]

    mine, queries = lax.optimization_barrier((mine, queries))
    came = sum_step(sum_sends(mine, got, None, 1), 1)
    for step in range(2, count):
        sends = sum_sends(mine, got, came, step)
        if step == 2:
            near = tuple(shares[1 : 1 + groups // 2])
            held = lax.optimization_barrier(sends + near)
            sends, shares[1 : 1 + groups // 2] = held[:2], list(held[2:])
        elif step == count - 1:
            rest = tuple(shares[1 + groups // 2 :])
            held = lax.optimization_barrier(sends + rest)
            sends, shares[1 + groups // 2 :] = held[:2], list(held[2:])
        came = sum_step(sends, step)
    total = slot_sum(mine, got, 0) + came[0].astype(F32) + came[1].astype(F32)
    enc_out = (source.astype(F32) + keep_factor(enc_keep) * total).astype(BF16)
    memory = norm_rows(enc_out, final_gain).astype(BF16)

    at = jnp.stack([group ^ j for j in range(groups)])
    places = [section * groups, (1 - section) * groups]
    table = jnp.concatenate(
        [p + at for p in places] + [p + jnp.arange(groups, dtype=jnp.int32) for p in places]
    ).astype(jnp.int32)
    shares += [swap(s, "section", 1) for s in shares]
    parts = attend_own_keys(memory, queries, own_head, shares, table)
    parts = [parts[0]] + [
        lax.ppermute(parts[o], "tensor", [(i, (i + o) % count) for i in range(count)]) for o in range(1, count)
    ]
    parts = [p.astype(F32) for p in parts]
    context, top, whole = merged(
        [p[:, :HD] for p in parts],
        [p[:, HD : HD + 1] + p[:, HD + 1 : HD + 2] + p[:, HD + 2 : HD + 3] for p in parts],
        [p[:, HD + 3 : HD + 4] + p[:, HD + 4 : HD + 5] for p in parts],
    )
    pad = [jnp.broadcast_to(y, (y.shape[0], 128)) for y in (top, whole)]
    other = swap(jnp.concatenate([context] + pad, 1), "section", 1)
    context, top, whole = merged(
        [context, other[:, :HD]], [top, other[:, HD : HD + 1]], [whole, other[:, HD + 128 : HD + 129]]
    )
    context = (context / whole).astype(BF16).reshape(2, count, rows, HD)
    context = jnp.roll(jnp.transpose(context, (1, 0, 2, 3)), -tensor, axis=0).reshape(2 * count * rows, HD)
    product = jnp.dot(context, cross_out, preferred_element_type=F32).astype(BF16)
    crosssum = whole_rows(slots_sum(product), section)
    dec_out = (mid.astype(F32) + keep_factor(dec_keep) * crosssum).astype(BF16)
    return (enc_out, dec_out)


def solution(mesh):
    return jax.shard_map(
        per_device,
        mesh=mesh,
        in_specs=(
            P(("dp", "section", "tensor"), None),
            P(),
            P(None, ("section", "tensor")),
            P(None, ("section", "tensor")),
            P(("section", "tensor"), None),
            P(("dp", "section", "tensor"), None),
            P(),
            P(("dp", "section", "tensor"), None),
            P(),
            P("section", None, "tensor"),
            P("tensor", "section"),
            P(),
            P("section", "tensor"),
            P("section", None, "tensor"),
            P("tensor", "section"),
            P(("dp", "section", "tensor"), None),
        ),
        out_specs=(P(("dp", "section", "tensor"), None), P(("dp", "section", "tensor"), None)),
        check_vma=False,
    )
```

```python
import functools

import jax
import jax.numpy as jnp
from jax import lax
from jax.experimental import pallas as pl
from jax.experimental.pallas import tpu as pltpu
from jax.sharding import PartitionSpec as P

HD = 256
F32 = jnp.float32
BF16 = jnp.bfloat16
STATS = 5


def norm_rows(x, gain):
    values = x.astype(F32)
    power = jnp.mean(values * values, axis=-1, keepdims=True)
    return values * lax.rsqrt(power + 1e-06) * gain


def keep_factor(words):
    shifts = jnp.arange(4, dtype=jnp.int32) * 3
    bits = jnp.right_shift(words[:, None, :], shifts[None, :, None]) & 7
    kept = jnp.where(bits == 7, 0.0, 8.0 / 7.0).astype(F32)
    return kept.reshape(words.shape[0], 4 * words.shape[1])


def swap(value, axis, distance):
    return lax.ppermute(value, axis, [(i, i ^ distance) for i in range(lax.axis_size(axis))])


def from_slots(value):
    count = lax.axis_size("tensor")
    return [value] + [
        lax.ppermute(value, "tensor", [(i, (i - o) % count) for i in range(count)]) for o in range(1, count)
    ]


def gated(value, *others):
    return lax.optimization_barrier((value,) + others)[0]


def slot_sum(mine, got, slot):
    block = mine.shape[0] // lax.axis_size("tensor")
    at = slice(slot * block, (slot + 1) * block)
    return mine[at].astype(F32) + got[at].astype(F32)


def sum_sends(mine, got, came, step):
    up, down = slot_sum(mine, got, lax.axis_size("tensor") - step), slot_sum(mine, got, step)
    if came is not None:
        up, down = up + came[0].astype(F32), down + came[1].astype(F32)
    return up.astype(BF16), down.astype(BF16)


def sum_step(sends, step):
    count = lax.axis_size("tensor")
    above = lax.ppermute(sends[0], "tensor", [(i, i + 1) for i in range(step)])
    below = lax.ppermute(sends[1], "tensor", [(i, i - 1) for i in range(count - step, count)])
    return lax.optimization_barrier((above, below))


def slots_sum(product):
    count = lax.axis_size("tensor")
    product = product.reshape(count, product.shape[0] // count, product.shape[1])
    total = product[0].astype(F32)
    for o in range(1, count):
        total = total + lax.ppermute(
            product[o], "tensor", [(i, (i + o) % count) for i in range(count)]
        ).astype(F32)
    return total


def near_bits(axis):
    bits, bit = [], 1
    while bit < lax.axis_size(axis):
        bits.append(bit)
        bit *= 2
    return bits


def half_columns(value, index):
    return lax.dynamic_slice_in_dim(value, index * (value.shape[1] // 2), value.shape[1] // 2, 1)


def in_order(own, other, section, axis):
    return jnp.where(
        section == 0, jnp.concatenate([own, other], axis), jnp.concatenate([other, own], axis)
    )


def gather_half(rows, section):
    own = half_columns(rows, section)
    other = swap(half_columns(rows, 1 - section), "section", 1)
    return jnp.concatenate(from_slots(in_order(own, other, section, 0)), 0)


def whole_rows(total, section):
    rows = total.shape[0] // 2
    own = lax.dynamic_slice_in_dim(total, section * rows, rows, 0)
    other = swap(lax.dynamic_slice_in_dim(total, (1 - section) * rows, rows, 0), "section", 1)
    return in_order(own, other, section, 1)


def both_halves(partial):
    return partial + swap(partial, "section", 1)


def gelu(x):
    return 0.5 * x * (1.0 + jnp.tanh(0.7978845608028654 * (x + 0.044715 * x * x * x)))


def ffn_kernel(ins, order, x_ref, gate_ref, up_ref, down_ref, y_ref, gate, up, hidden):
    step = pl.program_id(0)
    _, blocks, block, _ = x_ref.shape
    rows, depth = blocks * block, gate_ref.shape[0]

    for k in range(ins):

        @pl.when(step == k)
        def _():
            part = x_ref[0, :, :, k * depth : (k + 1) * depth].reshape(rows, depth)
            one = jnp.dot(part, gate_ref[...], preferred_element_type=F32)
            two = jnp.dot(part, up_ref[...], preferred_element_type=F32)
            if k == 0:
                gate[...] = one
                up[...] = two
            else:
                gate[...] += one
                up[...] += two

    @pl.when(step == ins)
    def _():
        for slot in range(blocks):
            at = pl.ds(pl.multiple_of(order[1 + slot] * block, block), block)
            hidden[slot * block : (slot + 1) * block, :] = (gelu(gate[at, :]) * up[at, :]).astype(BF16)

    @pl.when(step >= ins)
    def _():
        y_ref[...] = jnp.dot(hidden[...], down_ref[...], preferred_element_type=F32).astype(BF16)


def ffn(x, order, w_gate, w_up, w_down):
    _, blocks, block, features = x.shape
    units = w_gate.shape[1]
    rows, depth, tile = blocks * block, 512, 1024
    ins, outs = features // depth, features // tile
    return pl.pallas_call(
        functools.partial(ffn_kernel, ins),
        grid_spec=pltpu.PrefetchScalarGridSpec(
            num_scalar_prefetch=1,
            grid=(ins + outs,),
            in_specs=[
                pl.BlockSpec(
                    (1, blocks, block, features), lambda i, t: (t[0], 0, 0, 0), pipeline_mode=pl.Buffered(1)
                ),
                pl.BlockSpec((depth, units), lambda i, t: (jnp.minimum(i, ins - 1), 0)),
                pl.BlockSpec((depth, units), lambda i, t: (jnp.minimum(i, ins - 1), 0)),
                pl.BlockSpec((units, tile), lambda i, t: (0, jnp.maximum(i - ins, 0))),
            ],
            out_specs=pl.BlockSpec((rows, tile), lambda i, t: (0, jnp.maximum(i - ins, 0))),
            scratch_shapes=[
                pltpu.VMEM((rows, units), F32),
                pltpu.VMEM((rows, units), F32),
                pltpu.VMEM((rows, units), BF16),
            ],
        ),
        out_shape=jax.ShapeDtypeStruct((rows, features), BF16),
        compiler_params=pltpu.CompilerParams(vmem_limit_bytes=28 * 2**20),
        cost_estimate=pl.CostEstimate(flops=1024, bytes_accessed=1024, transcendentals=0),
        name="ffn",
    )(order, x, w_gate, w_up, w_down)


def attend_kernel(plan, depth, table, mem_ref, cq_ref, *refs):
    locals_, shares, out_ref = refs[:2], refs[2:-1], refs[-1]
    slot = pl.program_id(0)
    groups = len(plan) // 2

    def attend(pieces):
        keys = jnp.zeros((mem_ref.shape[0], HD), F32)
        values = jnp.zeros((mem_ref.shape[0], HD), F32)
        for index, k, v in pieces:
            x = mem_ref[:, pl.ds(pl.multiple_of(table[index] * depth, depth), depth)]
            keys += jnp.dot(x, k, preferred_element_type=F32)
            values += jnp.dot(x, v, preferred_element_type=F32)
        k, v = keys.astype(BF16), values.astype(BF16)
        scores = lax.dot_general(cq_ref[0], k, (((1,), (1,)), ((), ())), preferred_element_type=F32)
        scores = scores * (1.0 / 16.0)
        top = jnp.max(scores, axis=-1, keepdims=True)
        expo = jnp.exp(scores - top)
        total = jnp.sum(expo, axis=-1, keepdims=True)
        context = jnp.dot(expo.astype(BF16), v, preferred_element_type=F32)
        out_ref[0, :, :HD] = context.astype(BF16)
        lanes = lax.broadcasted_iota(jnp.int32, (scores.shape[0], 128), 1)
        high = top.astype(BF16).astype(F32)
        rest = top - high
        middle = rest.astype(BF16).astype(F32)
        sum_high = total.astype(BF16).astype(F32)
        stats = jnp.zeros(lanes.shape, F32)
        for index, piece in enumerate((high, middle, rest - middle, sum_high, total - sum_high)):
            stats = jnp.where(lanes == index, piece, stats)
        out_ref[0, :, HD:] = stats.astype(BF16)

    @pl.when(slot == 0)
    def _():
        attend(
            [
                (2 * groups + place * groups + g, ref[0, g * depth : (g + 1) * depth, :], ref[1, g * depth : (g + 1) * depth, :])
                for place, ref in enumerate(locals_)
                for g in range(groups)
            ]
        )

    @pl.when(slot > 0)
    def _():
        attend([(i, shares[k][0, a], shares[v][0, b]) for i, (k, a, v, b) in enumerate(plan)])


def attend_own_keys(memory, queries, own_head, shares, plan, table):
    rows, features = memory.shape
    heads, count, width = queries.shape
    depth = shares[0].shape[2]
    whole = pl.BlockSpec(own_head[0].shape, lambda h, t: (0, 0, 0), pipeline_mode=pl.Buffered(1))
    return pl.pallas_call(
        functools.partial(attend_kernel, plan, depth),
        grid_spec=pltpu.PrefetchScalarGridSpec(
            num_scalar_prefetch=1,
            grid=(heads,),
            in_specs=[
                pl.BlockSpec((rows, features), lambda h, t: (0, 0)),
                pl.BlockSpec((1, count, width), lambda h, t: (h, 0, 0)),
                whole,
                whole,
            ]
            + [
                pl.BlockSpec((1,) + share.shape[1:], lambda h, t: (jnp.maximum(h - 1, 0), 0, 0, 0))
                for share in shares
            ],
            out_specs=pl.BlockSpec((1, count, width + 128), lambda h, t: (h, 0, 0)),
        ),
        out_shape=jax.ShapeDtypeStruct((heads, count, width + 128), BF16),
        compiler_params=pltpu.CompilerParams(vmem_limit_bytes=30 * 2**20),
        cost_estimate=pl.CostEstimate(flops=1024, bytes_accessed=1024, transcendentals=0),
        name="attend_own_keys",
    )(table, memory, queries, *own_head, *shares)


def merged(contexts, tops, wholes):
    most = functools.reduce(jnp.maximum, tops)
    weights = [jnp.exp(top - most) for top in tops]
    context = sum(c * w for c, w in zip(contexts, weights))
    return context, most, sum(s * w for s, w in zip(wholes, weights))


def per_device(
    source,
    enc_gain,
    w_gate,
    w_up,
    w_down,
    enc_keep,
    final_gain,
    target,
    self_gain,
    self_qkv,
    self_out,
    cross_gain,
    cross_q,
    cross_kv,
    cross_out,
    dec_keep,
):
    section, group = lax.axis_index("section"), lax.axis_index("dp")
    count, tensor = lax.axis_size("tensor"), lax.axis_index("tensor")
    groups = lax.axis_size("dp")
    rows = target.shape[0]
    slot_chip = lax.rem(tensor + jnp.arange(count, dtype=jnp.int32), count)

    selfin = gather_half(norm_rows(target, self_gain).astype(BF16), section)

    normed = norm_rows(source, enc_gain).astype(BF16)
    x = lax.all_gather(normed, ("section", "tensor"), axis=0, tiled=False)
    x = x.reshape((2, count) + normed.shape)
    own_head = [jnp.transpose(cross_kv, (1, 0, 2))]
    own_head.append(swap(own_head[0], "section", 1))

    qkv_w = jnp.transpose(self_qkv, (1, 0, 2))
    q, k, v = [jnp.dot(selfin, qkv_w[i], preferred_element_type=F32) for i in range(3)]
    q, k, v = [y.astype(BF16) for y in both_halves(jnp.stack([q, k, v]))]
    positions = (
        (jnp.arange(2, dtype=jnp.int32)[None, :] * count + slot_chip[:, None])[:, :, None] * rows
        + jnp.arange(rows, dtype=jnp.int32)
    ).reshape(-1)
    scores = lax.dot_general(q, k, (((1,), (1,)), ((), ())), preferred_element_type=F32) * (1.0 / 16.0)
    scores = jnp.where(positions[None, :] <= positions[:, None], scores, F32(-1e30))
    expo = jnp.exp(scores - jnp.max(scores, axis=-1, keepdims=True))
    probs = (expo / jnp.sum(expo, axis=-1, keepdims=True)).astype(BF16)
    context = jnp.dot(probs, v, preferred_element_type=F32).astype(BF16)
    product = jnp.dot(context, self_out, preferred_element_type=F32).astype(BF16)
    total = slots_sum(product)

    mid = (target.astype(F32) + whole_rows(total, section)).astype(BF16)
    crossin = norm_rows(mid, cross_gain).astype(BF16)
    crossin = gather_half(crossin, section)

    cq = both_halves(jnp.dot(crossin, cross_q, preferred_element_type=F32)).astype(BF16)
    cq = jnp.roll(cq.reshape(count, 2, rows, HD), tensor, axis=0)
    cq = jnp.transpose(cq, (1, 0, 2, 3)).reshape(2 * count * rows, HD)
    x, cq, other_head = lax.optimization_barrier((x, cq, own_head[1]))
    own_head[1] = other_head
    heads = [0]
    for bit in near_bits("tensor")[::-1]:
        heads += [m ^ bit for m in heads]
    queries = jnp.stack([cq] + [swap(cq, "tensor", m) for m in heads[1:]])

    depth = cross_kv.shape[0] // groups
    share = lax.dynamic_slice_in_dim(own_head[0], group * depth, depth, 1)[None]
    share, x = lax.optimization_barrier((share, x))
    bits = near_bits("tensor")[::-1]
    for bit in bits[:-1]:
        share = jnp.concatenate([share, swap(share, "tensor", bit)], 0)

    theirs = ffn(x, jnp.concatenate([(1 - section)[None], slot_chip]), w_gate, w_up, w_down)
    theirs, queries, share = lax.optimization_barrier((theirs, queries, share))
    got = swap(theirs, "section", 1)
    x = gated(x, share)
    last = swap(share, "tensor", bits[-1])
    mine = ffn(x, jnp.concatenate([section[None], slot_chip]), w_gate, w_up, w_down)
    mine, last = lax.optimization_barrier((mine, last))
    shares = [jnp.concatenate([share[1:], last], 0)]

    far = [j for j in range(1, groups) if groups != 4 or j < 3]
    shares += [swap(shares[0], "dp", j) for j in far]
    plan = [(j, 0, j, 1) for j in range(len(shares))]
    came = sum_step(sum_sends(mine, got, None, 1), 1)
    for step in range(2, count):
        sends = sum_sends(mine, got, came, step)
        if step == count - 1:
            held = lax.optimization_barrier(sends + tuple(shares[1:]))
            sends, shares[1:] = held[:2], list(held[2:])
        came = sum_step(sends, step)
    if groups == 4:
        passed = [swap(shares[2][:, :1], "dp", 1), swap(shares[1][:, 1:], "dp", 2)]
        held = lax.optimization_barrier(came + tuple(passed))
        came, shares = held[:2], shares + list(held[2:])
        plan.append((3, 0, 4, 0))
    total = slot_sum(mine, got, 0) + came[0].astype(F32) + came[1].astype(F32)
    enc_out = (source.astype(F32) + keep_factor(enc_keep) * total).astype(BF16)
    memory = norm_rows(enc_out, final_gain).astype(BF16)

    at = jnp.stack([group ^ j for j in range(groups)])
    places = [section * groups, (1 - section) * groups]
    table = jnp.concatenate(
        [p + at for p in places] + [p + jnp.arange(groups, dtype=jnp.int32) for p in places]
    ).astype(jnp.int32)
    plan += [(k + len(shares), a, v + len(shares), b) for k, a, v, b in plan]
    shares += [swap(s, "section", 1) for s in shares]
    parts = attend_own_keys(memory, queries, own_head, shares, tuple(plan), table)
    parts = [parts[0]] + [
        swap(parts[o], "tensor", heads[o]) for o in range(1, count)
    ]
    parts = [p.astype(F32) for p in parts]
    context, top, whole = merged(
        [p[:, :HD] for p in parts],
        [p[:, HD : HD + 1] + p[:, HD + 1 : HD + 2] + p[:, HD + 2 : HD + 3] for p in parts],
        [p[:, HD + 3 : HD + 4] + p[:, HD + 4 : HD + 5] for p in parts],
    )
    pad = [jnp.broadcast_to(y, (y.shape[0], 128)) for y in (top, whole)]
    other = swap(jnp.concatenate([context] + pad, 1), "section", 1)
    context, top, whole = merged(
        [context, other[:, :HD]], [top, other[:, HD : HD + 1]], [whole, other[:, HD + 128 : HD + 129]]
    )
    context = (context / whole).astype(BF16).reshape(2, count, rows, HD)
    context = jnp.roll(jnp.transpose(context, (1, 0, 2, 3)), -tensor, axis=0).reshape(2 * count * rows, HD)
    product = jnp.dot(context, cross_out, preferred_element_type=F32).astype(BF16)
    crosssum = whole_rows(slots_sum(product), section)
    dec_out = (mid.astype(F32) + keep_factor(dec_keep) * crosssum).astype(BF16)
    return (enc_out, dec_out)


def solution(mesh):
    return jax.shard_map(
        per_device,
        mesh=mesh,
        in_specs=(
            P(("dp", "section", "tensor"), None),
            P(),
            P(None, ("section", "tensor")),
            P(None, ("section", "tensor")),
            P(("section", "tensor"), None),
            P(("dp", "section", "tensor"), None),
            P(),
            P(("dp", "section", "tensor"), None),
            P(),
            P("section", None, "tensor"),
            P("tensor", "section"),
            P(),
            P("section", "tensor"),
            P("section", None, "tensor"),
            P("tensor", "section"),
            P(("dp", "section", "tensor"), None),
        ),
        out_specs=(P(("dp", "section", "tensor"), None), P(("dp", "section", "tensor"), None)),
        check_vma=False,
    )
```

```python
import functools

import jax
import jax.numpy as jnp
from jax import lax
from jax.experimental import pallas as pl
from jax.experimental.pallas import tpu as pltpu
from jax.sharding import PartitionSpec as P

HD = 256
F32 = jnp.float32
BF16 = jnp.bfloat16
STATS = 5


def norm_rows(x, gain):
    values = x.astype(F32)
    power = jnp.mean(values * values, axis=-1, keepdims=True)
    return values * lax.rsqrt(power + 1e-06) * gain


def keep_factor(words):
    shifts = jnp.arange(4, dtype=jnp.int32) * 3
    bits = jnp.right_shift(words[:, None, :], shifts[None, :, None]) & 7
    kept = jnp.where(bits == 7, 0.0, 8.0 / 7.0).astype(F32)
    return kept.reshape(words.shape[0], 4 * words.shape[1])


def swap(value, axis, distance):
    return lax.ppermute(value, axis, [(i, i ^ distance) for i in range(lax.axis_size(axis))])


def from_slots(value):
    count = lax.axis_size("tensor")
    return [value] + [
        lax.ppermute(value, "tensor", [(i, (i - o) % count) for i in range(count)]) for o in range(1, count)
    ]


def gated(value, *others):
    return lax.optimization_barrier((value,) + others)[0]


def slot_sum(mine, got, slot):
    block = mine.shape[0] // lax.axis_size("tensor")
    at = slice(slot * block, (slot + 1) * block)
    return mine[at].astype(F32) + got[at].astype(F32)


def sum_sends(mine, got, came, step):
    up, down = slot_sum(mine, got, lax.axis_size("tensor") - step), slot_sum(mine, got, step)
    if came is not None:
        up, down = up + came[0].astype(F32), down + came[1].astype(F32)
    return up.astype(BF16), down.astype(BF16)


def sum_step(sends, step):
    count = lax.axis_size("tensor")
    above = lax.ppermute(sends[0], "tensor", [(i, i + 1) for i in range(step)])
    below = lax.ppermute(sends[1], "tensor", [(i, i - 1) for i in range(count - step, count)])
    return lax.optimization_barrier((above, below))


def slots_sum(product):
    count = lax.axis_size("tensor")
    product = product.reshape(count, product.shape[0] // count, product.shape[1])
    total = product[0].astype(F32)
    for o in range(1, count):
        total = total + lax.ppermute(
            product[o], "tensor", [(i, (i + o) % count) for i in range(count)]
        ).astype(F32)
    return total


def near_bits(axis):
    bits, bit = [], 1
    while bit < lax.axis_size(axis):
        bits.append(bit)
        bit *= 2
    return bits


def half_columns(value, index):
    return lax.dynamic_slice_in_dim(value, index * (value.shape[1] // 2), value.shape[1] // 2, 1)


def in_order(own, other, section, axis):
    return jnp.where(
        section == 0, jnp.concatenate([own, other], axis), jnp.concatenate([other, own], axis)
    )


def gather_half(rows, section):
    own = half_columns(rows, section)
    other = swap(half_columns(rows, 1 - section), "section", 1)
    return jnp.concatenate(from_slots(in_order(own, other, section, 0)), 0)


def whole_rows(total, section):
    rows = total.shape[0] // 2
    own = lax.dynamic_slice_in_dim(total, section * rows, rows, 0)
    other = swap(lax.dynamic_slice_in_dim(total, (1 - section) * rows, rows, 0), "section", 1)
    return in_order(own, other, section, 1)


def both_halves(partial):
    return partial + swap(partial, "section", 1)


def gelu(x):
    return 0.5 * x * (1.0 + jnp.tanh(0.7978845608028654 * (x + 0.044715 * x * x * x)))


def ffn_kernel(ins, order, x_ref, gate_ref, up_ref, down_ref, y_ref, gate, up, hidden):
    step = pl.program_id(0)
    _, blocks, block, _ = x_ref.shape
    rows, depth = blocks * block, gate_ref.shape[0]

    for k in range(ins):

        @pl.when(step == k)
        def _():
            part = x_ref[0, :, :, k * depth : (k + 1) * depth].reshape(rows, depth)
            one = jnp.dot(part, gate_ref[...], preferred_element_type=F32)
            two = jnp.dot(part, up_ref[...], preferred_element_type=F32)
            if k == 0:
                gate[...] = one
                up[...] = two
            else:
                gate[...] += one
                up[...] += two

    @pl.when(step == ins)
    def _():
        for slot in range(blocks):
            at = pl.ds(pl.multiple_of(order[1 + slot] * block, block), block)
            hidden[slot * block : (slot + 1) * block, :] = (gelu(gate[at, :]) * up[at, :]).astype(BF16)

    @pl.when(step >= ins)
    def _():
        y_ref[...] = jnp.dot(hidden[...], down_ref[...], preferred_element_type=F32).astype(BF16)


def ffn(x, order, w_gate, w_up, w_down):
    _, blocks, block, features = x.shape
    units = w_gate.shape[1]
    rows, depth, tile = blocks * block, 512, 1024
    ins, outs = features // depth, features // tile
    return pl.pallas_call(
        functools.partial(ffn_kernel, ins),
        grid_spec=pltpu.PrefetchScalarGridSpec(
            num_scalar_prefetch=1,
            grid=(ins + outs,),
            in_specs=[
                pl.BlockSpec(
                    (1, blocks, block, features), lambda i, t: (t[0], 0, 0, 0), pipeline_mode=pl.Buffered(1)
                ),
                pl.BlockSpec(
                    (depth, units), lambda i, t: (jnp.minimum(i, ins - 1), 0)
                ),
                pl.BlockSpec(
                    (depth, units), lambda i, t: (jnp.minimum(i, ins - 1), 0)
                ),
                pl.BlockSpec(
                    (units, tile), lambda i, t: (0, jnp.maximum(i - ins, 0))
                ),
            ],
            out_specs=pl.BlockSpec((rows, tile), lambda i, t: (0, jnp.maximum(i - ins, 0))),
            scratch_shapes=[
                pltpu.VMEM((rows, units), F32),
                pltpu.VMEM((rows, units), F32),
                pltpu.VMEM((rows, units), BF16),
            ],
        ),
        out_shape=jax.ShapeDtypeStruct((rows, features), BF16),
        compiler_params=pltpu.CompilerParams(vmem_limit_bytes=48 * 2**20),
        cost_estimate=pl.CostEstimate(flops=1024, bytes_accessed=1024, transcendentals=0),
        name="ffn",
    )(order, x, w_gate, w_up, w_down)


def attend_kernel(plan, depth, table, mem_ref, cq_ref, *refs):
    locals_, shares, out_ref = refs[:2], refs[2:-1], refs[-1]
    slot = pl.program_id(0)
    groups = len(plan) // 2

    def attend(pieces):
        keys = jnp.zeros((mem_ref.shape[0], HD), F32)
        values = jnp.zeros((mem_ref.shape[0], HD), F32)
        for index, k, v in pieces:
            x = mem_ref[:, pl.ds(pl.multiple_of(table[index] * depth, depth), depth)]
            keys += jnp.dot(x, k, preferred_element_type=F32)
            values += jnp.dot(x, v, preferred_element_type=F32)
        k, v = keys.astype(BF16), values.astype(BF16)
        scores = lax.dot_general(cq_ref[0], k, (((1,), (1,)), ((), ())), preferred_element_type=F32)
        scores = scores * (1.0 / 16.0)
        top = jnp.max(scores, axis=-1, keepdims=True)
        expo = jnp.exp(scores - top)
        total = jnp.sum(expo, axis=-1, keepdims=True)
        context = jnp.dot(expo.astype(BF16), v, preferred_element_type=F32)
        out_ref[0, :, :HD] = context.astype(BF16)
        lanes = lax.broadcasted_iota(jnp.int32, (scores.shape[0], 128), 1)
        high = top.astype(BF16).astype(F32)
        rest = top - high
        middle = rest.astype(BF16).astype(F32)
        sum_high = total.astype(BF16).astype(F32)
        stats = jnp.zeros(lanes.shape, F32)
        for index, piece in enumerate((high, middle, rest - middle, sum_high, total - sum_high)):
            stats = jnp.where(lanes == index, piece, stats)
        out_ref[0, :, HD:] = stats.astype(BF16)

    @pl.when(slot == 0)
    def _():
        attend(
            [
                (2 * groups + place * groups + g, ref[0, g * depth : (g + 1) * depth, :], ref[1, g * depth : (g + 1) * depth, :])
                for place, ref in enumerate(locals_)
                for g in range(groups)
            ]
        )

    @pl.when(slot > 0)
    def _():
        attend([(i, shares[k][0, a], shares[v][0, b]) for i, (k, a, v, b) in enumerate(plan)])


def attend_own_keys(memory, queries, own_head, shares, plan, table):
    rows, features = memory.shape
    heads, count, width = queries.shape
    depth = shares[0].shape[2]
    whole = pl.BlockSpec(own_head[0].shape, lambda h, t: (0, 0, 0), pipeline_mode=pl.Buffered(1))
    return pl.pallas_call(
        functools.partial(attend_kernel, plan, depth),
        grid_spec=pltpu.PrefetchScalarGridSpec(
            num_scalar_prefetch=1,
            grid=(heads,),
            in_specs=[
                pl.BlockSpec((rows, features), lambda h, t: (0, 0)),
                pl.BlockSpec((1, count, width), lambda h, t: (h, 0, 0)),
                whole,
                whole,
            ]
            + [
                pl.BlockSpec((1,) + share.shape[1:], lambda h, t: (jnp.maximum(h - 1, 0), 0, 0, 0))
                for share in shares
            ],
            out_specs=pl.BlockSpec((1, count, width + 128), lambda h, t: (h, 0, 0)),
        ),
        out_shape=jax.ShapeDtypeStruct((heads, count, width + 128), BF16),
        compiler_params=pltpu.CompilerParams(vmem_limit_bytes=30 * 2**20),
        cost_estimate=pl.CostEstimate(flops=1024, bytes_accessed=1024, transcendentals=0),
        name="attend_own_keys",
    )(table, memory, queries, *own_head, *shares)


def merged(contexts, tops, wholes):
    most = functools.reduce(jnp.maximum, tops)
    weights = [jnp.exp(top - most) for top in tops]
    context = sum(c * w for c, w in zip(contexts, weights))
    return context, most, sum(s * w for s, w in zip(wholes, weights))


def per_device(
    source,
    enc_gain,
    w_gate,
    w_up,
    w_down,
    enc_keep,
    final_gain,
    target,
    self_gain,
    self_qkv,
    self_out,
    cross_gain,
    cross_q,
    cross_kv,
    cross_out,
    dec_keep,
):
    section, group = lax.axis_index("section"), lax.axis_index("dp")
    count, tensor = lax.axis_size("tensor"), lax.axis_index("tensor")
    groups = lax.axis_size("dp")
    rows = target.shape[0]
    slot_chip = lax.rem(tensor + jnp.arange(count, dtype=jnp.int32), count)

    selfin = gather_half(norm_rows(target, self_gain).astype(BF16), section)

    normed = norm_rows(source, enc_gain).astype(BF16)
    x = lax.all_gather(normed, ("section", "tensor"), axis=0, tiled=False)
    x = x.reshape((2, count) + normed.shape)
    own_head = [jnp.transpose(cross_kv, (1, 0, 2))]
    own_head.append(swap(own_head[0], "section", 1))

    qkv_w = jnp.transpose(self_qkv, (1, 0, 2))
    q, k, v = [jnp.dot(selfin, qkv_w[i], preferred_element_type=F32) for i in range(3)]
    q, k, v = [y.astype(BF16) for y in both_halves(jnp.stack([q, k, v]))]
    positions = (
        (jnp.arange(2, dtype=jnp.int32)[None, :] * count + slot_chip[:, None])[:, :, None] * rows
        + jnp.arange(rows, dtype=jnp.int32)
    ).reshape(-1)
    scores = lax.dot_general(q, k, (((1,), (1,)), ((), ())), preferred_element_type=F32) * (1.0 / 16.0)
    scores = jnp.where(positions[None, :] <= positions[:, None], scores, F32(-1e30))
    expo = jnp.exp(scores - jnp.max(scores, axis=-1, keepdims=True))
    probs = (expo / jnp.sum(expo, axis=-1, keepdims=True)).astype(BF16)
    context = jnp.dot(probs, v, preferred_element_type=F32).astype(BF16)
    product = jnp.dot(context, self_out, preferred_element_type=F32).astype(BF16)
    total = slots_sum(product)

    mid = (target.astype(F32) + whole_rows(total, section)).astype(BF16)
    crossin = norm_rows(mid, cross_gain).astype(BF16)
    crossin = gather_half(crossin, section)

    cq = both_halves(jnp.dot(crossin, cross_q, preferred_element_type=F32)).astype(BF16)
    cq = jnp.roll(cq.reshape(count, 2, rows, HD), tensor, axis=0)
    cq = jnp.transpose(cq, (1, 0, 2, 3)).reshape(2 * count * rows, HD)
    x, cq, other_head = lax.optimization_barrier((x, cq, own_head[1]))
    own_head[1] = other_head
    heads = [0]
    for bit in near_bits("tensor")[::-1]:
        heads += [m ^ bit for m in heads]
    queries = jnp.stack([cq] + [swap(cq, "tensor", m) for m in heads[1:]])

    depth = cross_kv.shape[0] // groups
    share = lax.dynamic_slice_in_dim(own_head[0], group * depth, depth, 1)[None]
    share, x = lax.optimization_barrier((share, x))
    bits = near_bits("tensor")[::-1]
    for bit in bits[:-1]:
        share = jnp.concatenate([share, swap(share, "tensor", bit)], 0)

    theirs = ffn(x, jnp.concatenate([(1 - section)[None], slot_chip]), w_gate, w_up, w_down)
    theirs, queries, share = lax.optimization_barrier((theirs, queries, share))
    got = swap(theirs, "section", 1)
    x = gated(x, share)
    last = swap(share, "tensor", bits[-1])
    mine = ffn(x, jnp.concatenate([section[None], slot_chip]), w_gate, w_up, w_down)
    mine, last = lax.optimization_barrier((mine, last))
    shares = [jnp.concatenate([share[1:], last], 0)]

    far = [j for j in range(1, groups) if groups != 4 or j < 3]
    shares += [swap(shares[0], "dp", j) for j in far]
    plan = [(j, 0, j, 1) for j in range(len(shares))]
    came = sum_step(sum_sends(mine, got, None, 1), 1)
    for step in range(2, count):
        sends = sum_sends(mine, got, came, step)
        if step == 2:
            held = lax.optimization_barrier(sends + tuple(shares[1:]))
            sends, shares[1:] = held[:2], list(held[2:])
            if groups == 4:
                passed = [swap(shares[2][:, :1], "dp", 1), swap(shares[1][:, 1:], "dp", 2)]
                plan.append((3, 0, 4, 0))
        if step == count - 1 and groups == 4:
            held = lax.optimization_barrier(sends + tuple(passed))
            sends, shares = held[:2], shares + list(held[2:])
        came = sum_step(sends, step)
    total = slot_sum(mine, got, 0) + came[0].astype(F32) + came[1].astype(F32)
    enc_out = (source.astype(F32) + keep_factor(enc_keep) * total).astype(BF16)
    memory = norm_rows(enc_out, final_gain).astype(BF16)

    at = jnp.stack([group ^ j for j in range(groups)])
    places = [section * groups, (1 - section) * groups]
    table = jnp.concatenate(
        [p + at for p in places] + [p + jnp.arange(groups, dtype=jnp.int32) for p in places]
    ).astype(jnp.int32)
    plan += [(k + len(shares), a, v + len(shares), b) for k, a, v, b in plan]
    shares += [swap(s, "section", 1) for s in shares]
    parts = attend_own_keys(memory, queries, own_head, shares, tuple(plan), table)
    parts = [parts[0]] + [
        swap(parts[o], "tensor", heads[o]) for o in range(1, count)
    ]
    parts = [p.astype(F32) for p in parts]
    context, top, whole = merged(
        [p[:, :HD] for p in parts],
        [p[:, HD : HD + 1] + p[:, HD + 1 : HD + 2] + p[:, HD + 2 : HD + 3] for p in parts],
        [p[:, HD + 3 : HD + 4] + p[:, HD + 4 : HD + 5] for p in parts],
    )
    pad = [jnp.broadcast_to(y, (y.shape[0], 128)) for y in (top, whole)]
    other = swap(jnp.concatenate([context] + pad, 1), "section", 1)
    context, top, whole = merged(
        [context, other[:, :HD]], [top, other[:, HD : HD + 1]], [whole, other[:, HD + 128 : HD + 129]]
    )
    context = (context / whole).astype(BF16).reshape(2, count, rows, HD)
    context = jnp.roll(jnp.transpose(context, (1, 0, 2, 3)), -tensor, axis=0).reshape(2 * count * rows, HD)
    product = jnp.dot(context, cross_out, preferred_element_type=F32).astype(BF16)
    crosssum = whole_rows(slots_sum(product), section)
    dec_out = (mid.astype(F32) + keep_factor(dec_keep) * crosssum).astype(BF16)
    return (enc_out, dec_out)


def solution(mesh):
    return jax.shard_map(
        per_device,
        mesh=mesh,
        in_specs=(
            P(("dp", "section", "tensor"), None),
            P(),
            P(None, ("section", "tensor")),
            P(None, ("section", "tensor")),
            P(("section", "tensor"), None),
            P(("dp", "section", "tensor"), None),
            P(),
            P(("dp", "section", "tensor"), None),
            P(),
            P("section", None, "tensor"),
            P("tensor", "section"),
            P(),
            P("section", "tensor"),
            P("section", None, "tensor"),
            P("tensor", "section"),
            P(("dp", "section", "tensor"), None),
        ),
        out_specs=(P(("dp", "section", "tensor"), None), P(("dp", "section", "tensor"), None)),
        check_vma=False,
    )
```

```python
import functools

import jax
import jax.numpy as jnp
from jax import lax
from jax.experimental import pallas as pl
from jax.experimental.pallas import tpu as pltpu
from jax.sharding import PartitionSpec as P

HD = 256
F32 = jnp.float32
BF16 = jnp.bfloat16
STATS = 5


def norm_rows(x, gain):
    values = x.astype(F32)
    power = jnp.mean(values * values, axis=-1, keepdims=True)
    return values * lax.rsqrt(power + 1e-06) * gain


def keep_factor(words):
    shifts = jnp.arange(4, dtype=jnp.int32) * 3
    bits = jnp.right_shift(words[:, None, :], shifts[None, :, None]) & 7
    kept = jnp.where(bits == 7, 0.0, 8.0 / 7.0).astype(F32)
    return kept.reshape(words.shape[0], 4 * words.shape[1])


def swap(value, axis, distance):
    return lax.ppermute(value, axis, [(i, i ^ distance) for i in range(lax.axis_size(axis))])


def from_slots(value):
    count = lax.axis_size("tensor")
    return [value] + [
        lax.ppermute(value, "tensor", [(i, (i - o) % count) for i in range(count)]) for o in range(1, count)
    ]


def gated(value, *others):
    return lax.optimization_barrier((value,) + others)[0]


def slot_sum(mine, got, slot):
    block = mine.shape[0] // lax.axis_size("tensor")
    at = slice(slot * block, (slot + 1) * block)
    return mine[at].astype(F32) + got[at].astype(F32)


def sum_sends(mine, got, came, step):
    up, down = slot_sum(mine, got, lax.axis_size("tensor") - step), slot_sum(mine, got, step)
    if came is not None:
        up, down = up + came[0].astype(F32), down + came[1].astype(F32)
    return up.astype(BF16), down.astype(BF16)


def sum_step(sends, step):
    count = lax.axis_size("tensor")
    above = lax.ppermute(sends[0], "tensor", [(i, i + 1) for i in range(step)])
    below = lax.ppermute(sends[1], "tensor", [(i, i - 1) for i in range(count - step, count)])
    return lax.optimization_barrier((above, below))


def slots_sum(product):
    count = lax.axis_size("tensor")
    product = product.reshape(count, product.shape[0] // count, product.shape[1])
    total = product[0].astype(F32)
    for o in range(1, count):
        total = total + lax.ppermute(
            product[o], "tensor", [(i, (i + o) % count) for i in range(count)]
        ).astype(F32)
    return total


def near_bits(axis):
    bits, bit = [], 1
    while bit < lax.axis_size(axis):
        bits.append(bit)
        bit *= 2
    return bits


def half_columns(value, index):
    return lax.dynamic_slice_in_dim(value, index * (value.shape[1] // 2), value.shape[1] // 2, 1)


def in_order(own, other, section, axis):
    return jnp.where(
        section == 0, jnp.concatenate([own, other], axis), jnp.concatenate([other, own], axis)
    )


def gather_half(rows, section):
    own = half_columns(rows, section)
    other = swap(half_columns(rows, 1 - section), "section", 1)
    return jnp.concatenate(from_slots(in_order(own, other, section, 0)), 0)


def whole_rows(total, section):
    rows = total.shape[0] // 2
    own = lax.dynamic_slice_in_dim(total, section * rows, rows, 0)
    other = swap(lax.dynamic_slice_in_dim(total, (1 - section) * rows, rows, 0), "section", 1)
    return in_order(own, other, section, 1)


def both_halves(partial):
    return partial + swap(partial, "section", 1)


def gelu(x):
    return 0.5 * x * (1.0 + jnp.tanh(0.7978845608028654 * (x + 0.044715 * x * x * x)))


def ffn_kernel(ins, order, x_ref, gate_ref, up_ref, down_ref, y_ref, gate, up, hidden):
    step = pl.program_id(0)
    _, blocks, block, _ = x_ref.shape
    rows, depth = blocks * block, gate_ref.shape[0]

    for k in range(ins):

        @pl.when(step == k)
        def _():
            part = x_ref[0, :, :, k * depth : (k + 1) * depth].reshape(rows, depth)
            one = jnp.dot(part, gate_ref[...], preferred_element_type=F32)
            two = jnp.dot(part, up_ref[...], preferred_element_type=F32)
            if k == 0:
                gate[...] = one
                up[...] = two
            else:
                gate[...] += one
                up[...] += two

    @pl.when(step == ins)
    def _():
        for slot in range(blocks):
            at = pl.ds(pl.multiple_of(order[1 + slot] * block, block), block)
            hidden[slot * block : (slot + 1) * block, :] = (gelu(gate[at, :]) * up[at, :]).astype(BF16)

    @pl.when(step >= ins)
    def _():
        y_ref[...] = jnp.dot(hidden[...], down_ref[...], preferred_element_type=F32).astype(BF16)


def ffn(x, order, w_gate, w_up, w_down):
    _, blocks, block, features = x.shape
    units = w_gate.shape[1]
    rows, depth, tile = blocks * block, 512, 1024
    ins, outs = features // depth, features // tile
    return pl.pallas_call(
        functools.partial(ffn_kernel, ins),
        grid_spec=pltpu.PrefetchScalarGridSpec(
            num_scalar_prefetch=1,
            grid=(ins + outs,),
            in_specs=[
                pl.BlockSpec(
                    (1, blocks, block, features), lambda i, t: (t[0], 0, 0, 0), pipeline_mode=pl.Buffered(1)
                ),
                pl.BlockSpec(
                    (depth, units), lambda i, t: (jnp.minimum(i, ins - 1), 0)
                ),
                pl.BlockSpec(
                    (depth, units), lambda i, t: (jnp.minimum(i, ins - 1), 0)
                ),
                pl.BlockSpec(
                    (units, tile), lambda i, t: (0, jnp.maximum(i - ins, 0))
                ),
            ],
            out_specs=pl.BlockSpec((rows, tile), lambda i, t: (0, jnp.maximum(i - ins, 0))),
            scratch_shapes=[
                pltpu.VMEM((rows, units), F32),
                pltpu.VMEM((rows, units), F32),
                pltpu.VMEM((rows, units), BF16),
            ],
        ),
        out_shape=jax.ShapeDtypeStruct((rows, features), BF16),
        compiler_params=pltpu.CompilerParams(vmem_limit_bytes=48 * 2**20),
        cost_estimate=pl.CostEstimate(flops=1024, bytes_accessed=1024, transcendentals=0),
        name="ffn",
    )(order, x, w_gate, w_up, w_down)


def attend_kernel(plan, depth, table, mem_ref, cq_ref, *refs):
    locals_, shares, out_ref = refs[:2], refs[2:-1], refs[-1]
    slot = pl.program_id(0)
    groups = len(plan) // 2

    def attend(pieces):
        keys = jnp.zeros((mem_ref.shape[0], HD), F32)
        values = jnp.zeros((mem_ref.shape[0], HD), F32)
        for index, k, v in pieces:
            x = mem_ref[:, pl.ds(pl.multiple_of(table[index] * depth, depth), depth)]
            keys += jnp.dot(x, k, preferred_element_type=F32)
            values += jnp.dot(x, v, preferred_element_type=F32)
        k, v = keys.astype(BF16), values.astype(BF16)
        scores = lax.dot_general(cq_ref[0], k, (((1,), (1,)), ((), ())), preferred_element_type=F32)
        scores = scores * (1.0 / 16.0)
        top = jnp.max(scores, axis=-1, keepdims=True)
        expo = jnp.exp(scores - top)
        total = jnp.sum(expo, axis=-1, keepdims=True)
        context = jnp.dot(expo.astype(BF16), v, preferred_element_type=F32)
        out_ref[0, :, :HD] = context.astype(BF16)
        lanes = lax.broadcasted_iota(jnp.int32, (scores.shape[0], 128), 1)
        high = top.astype(BF16).astype(F32)
        rest = top - high
        middle = rest.astype(BF16).astype(F32)
        sum_high = total.astype(BF16).astype(F32)
        stats = jnp.zeros(lanes.shape, F32)
        for index, piece in enumerate((high, middle, rest - middle, sum_high, total - sum_high)):
            stats = jnp.where(lanes == index, piece, stats)
        out_ref[0, :, HD:] = stats.astype(BF16)

    @pl.when(slot == 0)
    def _():
        attend(
            [
                (2 * groups + place * groups + g, ref[0, g * depth : (g + 1) * depth, :], ref[1, g * depth : (g + 1) * depth, :])
                for place, ref in enumerate(locals_)
                for g in range(groups)
            ]
        )

    @pl.when(slot > 0)
    def _():
        attend([(i, shares[k][0, a], shares[v][0, b]) for i, (k, a, v, b) in enumerate(plan)])


def attend_own_keys(memory, queries, own_head, shares, plan, table):
    rows, features = memory.shape
    heads, count, width = queries.shape
    depth = shares[0].shape[2]
    whole = pl.BlockSpec(own_head[0].shape, lambda h, t: (0, 0, 0), pipeline_mode=pl.Buffered(1))
    return pl.pallas_call(
        functools.partial(attend_kernel, plan, depth),
        grid_spec=pltpu.PrefetchScalarGridSpec(
            num_scalar_prefetch=1,
            grid=(heads,),
            in_specs=[
                pl.BlockSpec((rows, features), lambda h, t: (0, 0)),
                pl.BlockSpec((1, count, width), lambda h, t: (h, 0, 0)),
                whole,
                whole,
            ]
            + [
                pl.BlockSpec((1,) + share.shape[1:], lambda h, t: (jnp.maximum(h - 1, 0), 0, 0, 0))
                for share in shares
            ],
            out_specs=pl.BlockSpec((1, count, width + 128), lambda h, t: (h, 0, 0)),
        ),
        out_shape=jax.ShapeDtypeStruct((heads, count, width + 128), BF16),
        compiler_params=pltpu.CompilerParams(vmem_limit_bytes=30 * 2**20),
        cost_estimate=pl.CostEstimate(flops=1024, bytes_accessed=1024, transcendentals=0),
        name="attend_own_keys",
    )(table, memory, queries, *own_head, *shares)


def merged(contexts, tops, wholes):
    most = functools.reduce(jnp.maximum, tops)
    weights = [jnp.exp(top - most) for top in tops]
    context = sum(c * w for c, w in zip(contexts, weights))
    return context, most, sum(s * w for s, w in zip(wholes, weights))


def per_device(
    source,
    enc_gain,
    w_gate,
    w_up,
    w_down,
    enc_keep,
    final_gain,
    target,
    self_gain,
    self_qkv,
    self_out,
    cross_gain,
    cross_q,
    cross_kv,
    cross_out,
    dec_keep,
):
    section, group = lax.axis_index("section"), lax.axis_index("dp")
    count, tensor = lax.axis_size("tensor"), lax.axis_index("tensor")
    groups = lax.axis_size("dp")
    rows = target.shape[0]
    slot_chip = lax.rem(tensor + jnp.arange(count, dtype=jnp.int32), count)

    selfin = gather_half(norm_rows(target, self_gain).astype(BF16), section)

    normed = norm_rows(source, enc_gain).astype(BF16)
    x = lax.all_gather(normed, ("section", "tensor"), axis=0, tiled=False)
    x = x.reshape((2, count) + normed.shape)
    own_head = [jnp.transpose(cross_kv, (1, 0, 2))]
    own_head.append(swap(own_head[0], "section", 1))

    qkv_w = jnp.transpose(self_qkv, (1, 0, 2))
    q, k, v = [jnp.dot(selfin, qkv_w[i], preferred_element_type=F32) for i in range(3)]
    q, k, v = [y.astype(BF16) for y in both_halves(jnp.stack([q, k, v]))]
    positions = (
        (jnp.arange(2, dtype=jnp.int32)[None, :] * count + slot_chip[:, None])[:, :, None] * rows
        + jnp.arange(rows, dtype=jnp.int32)
    ).reshape(-1)
    scores = lax.dot_general(q, k, (((1,), (1,)), ((), ())), preferred_element_type=F32) * (1.0 / 16.0)
    scores = jnp.where(positions[None, :] <= positions[:, None], scores, F32(-1e30))
    expo = jnp.exp(scores - jnp.max(scores, axis=-1, keepdims=True))
    probs = (expo / jnp.sum(expo, axis=-1, keepdims=True)).astype(BF16)
    context = jnp.dot(probs, v, preferred_element_type=F32).astype(BF16)
    product = jnp.dot(context, self_out, preferred_element_type=F32).astype(BF16)
    total = slots_sum(product)

    mid = (target.astype(F32) + whole_rows(total, section)).astype(BF16)
    crossin = norm_rows(mid, cross_gain).astype(BF16)
    crossin = gather_half(crossin, section)

    cq = both_halves(jnp.dot(crossin, cross_q, preferred_element_type=F32)).astype(BF16)
    cq = jnp.roll(cq.reshape(count, 2, rows, HD), tensor, axis=0)
    cq = jnp.transpose(cq, (1, 0, 2, 3)).reshape(2 * count * rows, HD)
    x, cq, other_head = lax.optimization_barrier((x, cq, own_head[1]))
    own_head[1] = other_head
    heads = [0]
    for bit in near_bits("tensor")[::-1]:
        heads += [m ^ bit for m in heads]
    queries = jnp.stack([cq] + [swap(cq, "tensor", m) for m in heads[1:]])

    depth = cross_kv.shape[0] // groups
    share = lax.dynamic_slice_in_dim(own_head[0], group * depth, depth, 1)[None]
    share, x = lax.optimization_barrier((share, x))
    bits = near_bits("tensor")[::-1]
    for bit in bits[:-1]:
        share = jnp.concatenate([share, swap(share, "tensor", bit)], 0)

    theirs = ffn(x, jnp.concatenate([(1 - section)[None], slot_chip]), w_gate, w_up, w_down)
    theirs, queries, share = lax.optimization_barrier((theirs, queries, share))
    got = swap(theirs, "section", 1)
    x = gated(x, share)
    last = swap(share, "tensor", bits[-1])
    mine = ffn(x, jnp.concatenate([section[None], slot_chip]), w_gate, w_up, w_down)
    mine, last = lax.optimization_barrier((mine, last))
    shares = [jnp.concatenate([share[1:], last], 0)]

    came = sum_step(sum_sends(mine, got, None, 1), 1)
    if groups == 4:
        k, v = shares[0][:, :1], shares[0][:, 1:]
        near = [swap(k, "dp", 1), swap(k, "dp", 2)]
        plan = [(0, 0, 0, 1), (1, 0, 3, 0), (2, 0, 4, 0), (5, 0, 6, 0)]
        swapped = []
    else:
        near = [swap(shares[0], "dp", j) for j in range(1, groups)]
        plan = [(j, 0, j, 1) for j in range(groups)]
    for step in range(2, count):
        sends = sum_sends(mine, got, came, step)
        if step == 2:
            held = lax.optimization_barrier(sends + tuple(near))
            sends, shares = held[:2], shares + list(held[2:])
            if groups == 4:
                near = [swap(v, "dp", 1), swap(v, "dp", 2)]
                swapped = [swap(y, "section", 1) for y in shares]
        if step == count - 1 and groups == 4:
            held = lax.optimization_barrier(sends + tuple(near) + tuple(swapped))
            sends, near, swapped = held[:2], list(held[2:4]), list(held[4:])
            shares = shares + near
            passed = [swap(shares[2], "dp", 1), swap(near[0], "dp", 2)]
            swapped += [swap(y, "section", 1) for y in near]
        came = sum_step(sends, step)
    if groups == 4:
        held = lax.optimization_barrier(came + tuple(passed))
        came, shares = held[:2], shares + list(held[2:])
        swapped += [swap(y, "section", 1) for y in held[2:]]
    else:
        swapped = [swap(y, "section", 1) for y in shares]
    total = slot_sum(mine, got, 0) + came[0].astype(F32) + came[1].astype(F32)
    enc_out = (source.astype(F32) + keep_factor(enc_keep) * total).astype(BF16)
    memory = norm_rows(enc_out, final_gain).astype(BF16)

    at = jnp.stack([group ^ j for j in range(groups)])
    places = [section * groups, (1 - section) * groups]
    table = jnp.concatenate(
        [p + at for p in places] + [p + jnp.arange(groups, dtype=jnp.int32) for p in places]
    ).astype(jnp.int32)
    plan += [(k + len(shares), a, v + len(shares), b) for k, a, v, b in plan]
    shares = shares + swapped
    parts = attend_own_keys(memory, queries, own_head, shares, tuple(plan), table)
    parts = [parts[0]] + [
        swap(parts[o], "tensor", heads[o]) for o in range(1, count)
    ]
    parts = [p.astype(F32) for p in parts]
    context, top, whole = merged(
        [p[:, :HD] for p in parts],
        [p[:, HD : HD + 1] + p[:, HD + 1 : HD + 2] + p[:, HD + 2 : HD + 3] for p in parts],
        [p[:, HD + 3 : HD + 4] + p[:, HD + 4 : HD + 5] for p in parts],
    )
    pad = [jnp.broadcast_to(y, (y.shape[0], 128)) for y in (top, whole)]
    other = swap(jnp.concatenate([context] + pad, 1), "section", 1)
    context, top, whole = merged(
        [context, other[:, :HD]], [top, other[:, HD : HD + 1]], [whole, other[:, HD + 128 : HD + 129]]
    )
    context = (context / whole).astype(BF16).reshape(2, count, rows, HD)
    context = jnp.roll(jnp.transpose(context, (1, 0, 2, 3)), -tensor, axis=0).reshape(2 * count * rows, HD)
    product = jnp.dot(context, cross_out, preferred_element_type=F32).astype(BF16)
    crosssum = whole_rows(slots_sum(product), section)
    dec_out = (mid.astype(F32) + keep_factor(dec_keep) * crosssum).astype(BF16)
    return (enc_out, dec_out)


def solution(mesh):
    return jax.shard_map(
        per_device,
        mesh=mesh,
        in_specs=(
            P(("dp", "section", "tensor"), None),
            P(),
            P(None, ("section", "tensor")),
            P(None, ("section", "tensor")),
            P(("section", "tensor"), None),
            P(("dp", "section", "tensor"), None),
            P(),
            P(("dp", "section", "tensor"), None),
            P(),
            P("section", None, "tensor"),
            P("tensor", "section"),
            P(),
            P("section", "tensor"),
            P("section", None, "tensor"),
            P("tensor", "section"),
            P(("dp", "section", "tensor"), None),
        ),
        out_specs=(P(("dp", "section", "tensor"), None), P(("dp", "section", "tensor"), None)),
        check_vma=False,
    )
```

```python
import functools

import jax
import jax.numpy as jnp
from jax import lax
from jax.experimental import pallas as pl
from jax.experimental.pallas import tpu as pltpu
from jax.sharding import PartitionSpec as P

HD = 256
F32 = jnp.float32
BF16 = jnp.bfloat16
STATS = 5


def norm_rows(x, gain):
    values = x.astype(F32)
    power = jnp.mean(values * values, axis=-1, keepdims=True)
    return values * lax.rsqrt(power + 1e-06) * gain


def keep_factor(words):
    shifts = jnp.arange(4, dtype=jnp.int32) * 3
    bits = jnp.right_shift(words[:, None, :], shifts[None, :, None]) & 7
    kept = jnp.where(bits == 7, 0.0, 8.0 / 7.0).astype(F32)
    return kept.reshape(words.shape[0], 4 * words.shape[1])


def swap(value, axis, distance):
    return lax.ppermute(value, axis, [(i, i ^ distance) for i in range(lax.axis_size(axis))])


def from_slots(value):
    count = lax.axis_size("tensor")
    return [value] + [
        lax.ppermute(value, "tensor", [(i, (i - o) % count) for i in range(count)]) for o in range(1, count)
    ]


def gated(value, *others):
    return lax.optimization_barrier((value,) + others)[0]


def slot_sum(mine, got, slot):
    block = mine.shape[0] // lax.axis_size("tensor")
    at = slice(slot * block, (slot + 1) * block)
    return mine[at].astype(F32) + got[at].astype(F32)


def sum_sends(mine, got, came, step):
    up, down = slot_sum(mine, got, lax.axis_size("tensor") - step), slot_sum(mine, got, step)
    if came is not None:
        up, down = up + came[0].astype(F32), down + came[1].astype(F32)
    return up.astype(BF16), down.astype(BF16)


def sum_step(sends, step):
    count = lax.axis_size("tensor")
    above = lax.ppermute(sends[0], "tensor", [(i, i + 1) for i in range(step)])
    below = lax.ppermute(sends[1], "tensor", [(i, i - 1) for i in range(count - step, count)])
    return lax.optimization_barrier((above, below))


def slots_sum(product):
    count = lax.axis_size("tensor")
    product = product.reshape(count, product.shape[0] // count, product.shape[1])
    total = product[0].astype(F32)
    for o in range(1, count):
        total = total + lax.ppermute(
            product[o], "tensor", [(i, (i + o) % count) for i in range(count)]
        ).astype(F32)
    return total


def near_bits(axis):
    bits, bit = [], 1
    while bit < lax.axis_size(axis):
        bits.append(bit)
        bit *= 2
    return bits


def half_columns(value, index):
    return lax.dynamic_slice_in_dim(value, index * (value.shape[1] // 2), value.shape[1] // 2, 1)


def in_order(own, other, section, axis):
    return jnp.where(
        section == 0, jnp.concatenate([own, other], axis), jnp.concatenate([other, own], axis)
    )


def gather_half(rows, section):
    own = half_columns(rows, section)
    other = swap(half_columns(rows, 1 - section), "section", 1)
    return jnp.concatenate(from_slots(in_order(own, other, section, 0)), 0)


def whole_rows(total, section):
    rows = total.shape[0] // 2
    own = lax.dynamic_slice_in_dim(total, section * rows, rows, 0)
    other = swap(lax.dynamic_slice_in_dim(total, (1 - section) * rows, rows, 0), "section", 1)
    return in_order(own, other, section, 1)


def both_halves(partial):
    return partial + swap(partial, "section", 1)


def gelu(x):
    return 0.5 * x * (1.0 + jnp.tanh(0.7978845608028654 * (x + 0.044715 * x * x * x)))


def ffn_kernel(ins, order, x_ref, gate_ref, up_ref, down_ref, y_ref, gate, up, hidden):
    step = pl.program_id(0)
    _, blocks, block, _ = x_ref.shape
    rows, depth = blocks * block, gate_ref.shape[0]

    @pl.when(step < ins)
    def _():
        part = x_ref[0].reshape(rows, depth)
        one = jnp.dot(part, gate_ref[...], preferred_element_type=F32)
        two = jnp.dot(part, up_ref[...], preferred_element_type=F32)

        @pl.when(step == 0)
        def _():
            gate[...] = one
            up[...] = two

        @pl.when(step > 0)
        def _():
            gate[...] += one
            up[...] += two

    @pl.when(step == ins)
    def _():
        for slot in range(blocks):
            at = pl.ds(pl.multiple_of(order[1 + slot] * block, block), block)
            hidden[slot * block : (slot + 1) * block, :] = (gelu(gate[at, :]) * up[at, :]).astype(BF16)

    @pl.when(step >= ins)
    def _():
        y_ref[...] = jnp.dot(hidden[...], down_ref[...], preferred_element_type=F32).astype(BF16)


def ffn(x, order, w_gate, w_up, w_down):
    _, blocks, block, features = x.shape
    units = w_gate.shape[1]
    rows, depth, tile = blocks * block, 512, 1024
    ins, outs = features // depth, features // tile
    return pl.pallas_call(
        functools.partial(ffn_kernel, ins),
        grid_spec=pltpu.PrefetchScalarGridSpec(
            num_scalar_prefetch=1,
            grid=(ins + outs,),
            in_specs=[
                pl.BlockSpec(
                    (1, blocks, block, depth), lambda i, t: (t[0], 0, 0, jnp.minimum(i, ins - 1))
                ),
                pl.BlockSpec(
                    (depth, units), lambda i, t: (jnp.minimum(i, ins - 1), 0)
                ),
                pl.BlockSpec(
                    (depth, units), lambda i, t: (jnp.minimum(i, ins - 1), 0)
                ),
                pl.BlockSpec(
                    (units, tile), lambda i, t: (0, jnp.maximum(i - ins, 0))
                ),
            ],
            out_specs=pl.BlockSpec((rows, tile), lambda i, t: (0, jnp.maximum(i - ins, 0))),
            scratch_shapes=[
                pltpu.VMEM((rows, units), F32),
                pltpu.VMEM((rows, units), F32),
                pltpu.VMEM((rows, units), BF16),
            ],
        ),
        out_shape=jax.ShapeDtypeStruct((rows, features), BF16),
        compiler_params=pltpu.CompilerParams(vmem_limit_bytes=48 * 2**20),
        cost_estimate=pl.CostEstimate(flops=1024, bytes_accessed=1024, transcendentals=0),
        name="ffn",
    )(order, x, w_gate, w_up, w_down)


def attend_kernel(plan, depth, table, mem_ref, cq_ref, *refs):
    locals_, shares, out_ref = refs[:2], refs[2:-1], refs[-1]
    slot = pl.program_id(0)
    groups = len(plan) // 2

    def attend(pieces):
        keys = jnp.zeros((mem_ref.shape[0], HD), F32)
        values = jnp.zeros((mem_ref.shape[0], HD), F32)
        for index, k, v in pieces:
            x = mem_ref[:, pl.ds(pl.multiple_of(table[index] * depth, depth), depth)]
            keys += jnp.dot(x, k, preferred_element_type=F32)
            values += jnp.dot(x, v, preferred_element_type=F32)
        k, v = keys.astype(BF16), values.astype(BF16)
        scores = lax.dot_general(cq_ref[0], k, (((1,), (1,)), ((), ())), preferred_element_type=F32)
        scores = scores * (1.0 / 16.0)
        top = jnp.max(scores, axis=-1, keepdims=True)
        expo = jnp.exp(scores - top)
        total = jnp.sum(expo, axis=-1, keepdims=True)
        context = jnp.dot(expo.astype(BF16), v, preferred_element_type=F32)
        out_ref[0, :, :HD] = context.astype(BF16)
        lanes = lax.broadcasted_iota(jnp.int32, (scores.shape[0], 128), 1)
        high = top.astype(BF16).astype(F32)
        rest = top - high
        middle = rest.astype(BF16).astype(F32)
        sum_high = total.astype(BF16).astype(F32)
        stats = jnp.zeros(lanes.shape, F32)
        for index, piece in enumerate((high, middle, rest - middle, sum_high, total - sum_high)):
            stats = jnp.where(lanes == index, piece, stats)
        out_ref[0, :, HD:] = stats.astype(BF16)

    @pl.when(slot == 0)
    def _():
        attend(
            [
                (2 * groups + place * groups + g, ref[0, g * depth : (g + 1) * depth, :], ref[1, g * depth : (g + 1) * depth, :])
                for place, ref in enumerate(locals_)
                for g in range(groups)
            ]
        )

    @pl.when(slot > 0)
    def _():
        attend([(i, shares[k][0, a], shares[v][0, b]) for i, (k, a, v, b) in enumerate(plan)])


def attend_own_keys(memory, queries, own_head, shares, plan, table):
    rows, features = memory.shape
    heads, count, width = queries.shape
    depth = shares[0].shape[2]
    whole = pl.BlockSpec(own_head[0].shape, lambda h, t: (0, 0, 0), pipeline_mode=pl.Buffered(1))
    return pl.pallas_call(
        functools.partial(attend_kernel, plan, depth),
        grid_spec=pltpu.PrefetchScalarGridSpec(
            num_scalar_prefetch=1,
            grid=(heads,),
            in_specs=[
                pl.BlockSpec((rows, features), lambda h, t: (0, 0)),
                pl.BlockSpec((1, count, width), lambda h, t: (h, 0, 0)),
                whole,
                whole,
            ]
            + [
                pl.BlockSpec((1,) + share.shape[1:], lambda h, t: (jnp.maximum(h - 1, 0), 0, 0, 0))
                for share in shares
            ],
            out_specs=pl.BlockSpec((1, count, width + 128), lambda h, t: (h, 0, 0)),
        ),
        out_shape=jax.ShapeDtypeStruct((heads, count, width + 128), BF16),
        compiler_params=pltpu.CompilerParams(vmem_limit_bytes=30 * 2**20),
        cost_estimate=pl.CostEstimate(flops=1024, bytes_accessed=1024, transcendentals=0),
        name="attend_own_keys",
    )(table, memory, queries, *own_head, *shares)


def merged(contexts, tops, wholes):
    most = functools.reduce(jnp.maximum, tops)
    weights = [jnp.exp(top - most) for top in tops]
    context = sum(c * w for c, w in zip(contexts, weights))
    return context, most, sum(s * w for s, w in zip(wholes, weights))


def per_device(
    source,
    enc_gain,
    w_gate,
    w_up,
    w_down,
    enc_keep,
    final_gain,
    target,
    self_gain,
    self_qkv,
    self_out,
    cross_gain,
    cross_q,
    cross_kv,
    cross_out,
    dec_keep,
):
    section, group = lax.axis_index("section"), lax.axis_index("dp")
    count, tensor = lax.axis_size("tensor"), lax.axis_index("tensor")
    groups = lax.axis_size("dp")
    rows = target.shape[0]
    slot_chip = lax.rem(tensor + jnp.arange(count, dtype=jnp.int32), count)

    selfin = gather_half(norm_rows(target, self_gain).astype(BF16), section)

    normed = norm_rows(source, enc_gain).astype(BF16)
    x = lax.all_gather(normed, ("section", "tensor"), axis=0, tiled=False)
    x = x.reshape((2, count) + normed.shape)
    own_head = [jnp.transpose(cross_kv, (1, 0, 2))]
    own_head.append(swap(own_head[0], "section", 1))

    qkv_w = jnp.transpose(self_qkv, (1, 0, 2))
    q, k, v = [jnp.dot(selfin, qkv_w[i], preferred_element_type=F32) for i in range(3)]
    q, k, v = [y.astype(BF16) for y in both_halves(jnp.stack([q, k, v]))]
    positions = (
        (jnp.arange(2, dtype=jnp.int32)[None, :] * count + slot_chip[:, None])[:, :, None] * rows
        + jnp.arange(rows, dtype=jnp.int32)
    ).reshape(-1)
    scores = lax.dot_general(q, k, (((1,), (1,)), ((), ())), preferred_element_type=F32) * (1.0 / 16.0)
    scores = jnp.where(positions[None, :] <= positions[:, None], scores, F32(-1e30))
    expo = jnp.exp(scores - jnp.max(scores, axis=-1, keepdims=True))
    probs = (expo / jnp.sum(expo, axis=-1, keepdims=True)).astype(BF16)
    context = jnp.dot(probs, v, preferred_element_type=F32).astype(BF16)
    product = jnp.dot(context, self_out, preferred_element_type=F32).astype(BF16)
    total = slots_sum(product)

    mid = (target.astype(F32) + whole_rows(total, section)).astype(BF16)
    crossin = norm_rows(mid, cross_gain).astype(BF16)
    crossin = gather_half(crossin, section)

    cq = both_halves(jnp.dot(crossin, cross_q, preferred_element_type=F32)).astype(BF16)
    cq = jnp.roll(cq.reshape(count, 2, rows, HD), tensor, axis=0)
    cq = jnp.transpose(cq, (1, 0, 2, 3)).reshape(2 * count * rows, HD)
    heads = [0]
    for bit in near_bits("tensor")[::-1]:
        heads += [m ^ bit for m in heads]
    queries = jnp.stack([cq] + [swap(cq, "tensor", m) for m in heads[1:]])
    x, queries, other_head = lax.optimization_barrier((x, queries, own_head[1]))
    own_head[1] = other_head

    depth = cross_kv.shape[0] // groups
    share = lax.dynamic_slice_in_dim(own_head[0], group * depth, depth, 1)[None]
    share, x = lax.optimization_barrier((share, x))
    bits = near_bits("tensor")[::-1]
    for bit in bits[:-1]:
        share = jnp.concatenate([share, swap(share, "tensor", bit)], 0)

    theirs = ffn(x, jnp.concatenate([(1 - section)[None], slot_chip]), w_gate, w_up, w_down)
    theirs, share = lax.optimization_barrier((theirs, share))
    got = swap(theirs, "section", 1)
    x = gated(x, share)
    last = swap(share, "tensor", bits[-1])
    mine = ffn(x, jnp.concatenate([section[None], slot_chip]), w_gate, w_up, w_down)
    mine, last = lax.optimization_barrier((mine, last))
    shares = [jnp.concatenate([share[1:], last], 0)]

    came = sum_step(sum_sends(mine, got, None, 1), 1)
    if groups == 4:
        k, v = shares[0][:, :1], shares[0][:, 1:]
        near = [swap(k, "dp", 1), swap(k, "dp", 2)]
        plan = [(0, 0, 0, 1), (1, 0, 3, 0), (2, 0, 4, 0), (5, 0, 6, 0)]
        swapped = []
    else:
        near = [swap(shares[0], "dp", j) for j in range(1, groups)]
        plan = [(j, 0, j, 1) for j in range(groups)]
    for step in range(2, count):
        sends = sum_sends(mine, got, came, step)
        if step == 2:
            held = lax.optimization_barrier(sends + tuple(near))
            sends, shares = held[:2], shares + list(held[2:])
            if groups == 4:
                near = [swap(v, "dp", 1), swap(v, "dp", 2)]
                swapped = [swap(y, "section", 1) for y in shares]
        if step == count - 1 and groups == 4:
            held = lax.optimization_barrier(sends + tuple(near) + tuple(swapped))
            sends, near, swapped = held[:2], list(held[2:4]), list(held[4:])
            shares = shares + near
            passed = [swap(shares[2], "dp", 1), swap(near[0], "dp", 2)]
            swapped += [swap(y, "section", 1) for y in near]
        came = sum_step(sends, step)
    if groups == 4:
        held = lax.optimization_barrier(came + tuple(passed))
        came, shares = held[:2], shares + list(held[2:])
        swapped += [swap(y, "section", 1) for y in held[2:]]
    else:
        swapped = [swap(y, "section", 1) for y in shares]
    total = slot_sum(mine, got, 0) + came[0].astype(F32) + came[1].astype(F32)
    enc_out = (source.astype(F32) + keep_factor(enc_keep) * total).astype(BF16)
    memory = norm_rows(enc_out, final_gain).astype(BF16)

    at = jnp.stack([group ^ j for j in range(groups)])
    places = [section * groups, (1 - section) * groups]
    table = jnp.concatenate(
        [p + at for p in places] + [p + jnp.arange(groups, dtype=jnp.int32) for p in places]
    ).astype(jnp.int32)
    plan += [(k + len(shares), a, v + len(shares), b) for k, a, v, b in plan]
    shares = shares + swapped
    parts = attend_own_keys(memory, queries, own_head, shares, tuple(plan), table)
    parts = [parts[0]] + [
        swap(parts[o], "tensor", heads[o]) for o in range(1, count)
    ]
    parts = [p.astype(F32) for p in parts]
    context, top, whole = merged(
        [p[:, :HD] for p in parts],
        [p[:, HD : HD + 1] + p[:, HD + 1 : HD + 2] + p[:, HD + 2 : HD + 3] for p in parts],
        [p[:, HD + 3 : HD + 4] + p[:, HD + 4 : HD + 5] for p in parts],
    )
    pad = [jnp.broadcast_to(y, (y.shape[0], 128)) for y in (top, whole)]
    other = swap(jnp.concatenate([context] + pad, 1), "section", 1)
    context, top, whole = merged(
        [context, other[:, :HD]], [top, other[:, HD : HD + 1]], [whole, other[:, HD + 128 : HD + 129]]
    )
    context = (context / whole).astype(BF16).reshape(2, count, rows, HD)
    context = jnp.roll(jnp.transpose(context, (1, 0, 2, 3)), -tensor, axis=0).reshape(2 * count * rows, HD)
    product = jnp.dot(context, cross_out, preferred_element_type=F32).astype(BF16)
    crosssum = whole_rows(slots_sum(product), section)
    dec_out = (mid.astype(F32) + keep_factor(dec_keep) * crosssum).astype(BF16)
    return (enc_out, dec_out)


def solution(mesh):
    return jax.shard_map(
        per_device,
        mesh=mesh,
        in_specs=(
            P(("dp", "section", "tensor"), None),
            P(),
            P(None, ("section", "tensor")),
            P(None, ("section", "tensor")),
            P(("section", "tensor"), None),
            P(("dp", "section", "tensor"), None),
            P(),
            P(("dp", "section", "tensor"), None),
            P(),
            P("section", None, "tensor"),
            P("tensor", "section"),
            P(),
            P("section", "tensor"),
            P("section", None, "tensor"),
            P("tensor", "section"),
            P(("dp", "section", "tensor"), None),
        ),
        out_specs=(P(("dp", "section", "tensor"), None), P(("dp", "section", "tensor"), None)),
        check_vma=False,
    )
```

```python
import functools

import jax
import jax.numpy as jnp
from jax import lax
from jax.experimental import pallas as pl
from jax.experimental.pallas import tpu as pltpu
from jax.sharding import PartitionSpec as P

HD = 256
F32 = jnp.float32
BF16 = jnp.bfloat16
STATS = 5


def norm_rows(x, gain):
    values = x.astype(F32)
    power = jnp.mean(values * values, axis=-1, keepdims=True)
    return values * lax.rsqrt(power + 1e-06) * gain


def keep_factor(words):
    shifts = jnp.arange(4, dtype=jnp.int32) * 3
    bits = jnp.right_shift(words[:, None, :], shifts[None, :, None]) & 7
    kept = jnp.where(bits == 7, 0.0, 8.0 / 7.0).astype(F32)
    return kept.reshape(words.shape[0], 4 * words.shape[1])


def swap(value, axis, distance):
    return lax.ppermute(value, axis, [(i, i ^ distance) for i in range(lax.axis_size(axis))])


def from_slots(value):
    count = lax.axis_size("tensor")
    return [value] + [
        lax.ppermute(value, "tensor", [(i, (i - o) % count) for i in range(count)]) for o in range(1, count)
    ]


def gated(value, *others):
    return lax.optimization_barrier((value,) + others)[0]


def slot_sum(mine, got, slot):
    block = mine.shape[0] // lax.axis_size("tensor")
    at = slice(slot * block, (slot + 1) * block)
    return mine[at].astype(F32) + got[at].astype(F32)


def sum_sends(mine, got, came, step):
    up, down = slot_sum(mine, got, lax.axis_size("tensor") - step), slot_sum(mine, got, step)
    if came is not None:
        up, down = up + came[0].astype(F32), down + came[1].astype(F32)
    return up.astype(BF16), down.astype(BF16)


def sum_step(sends, step):
    count = lax.axis_size("tensor")
    above = lax.ppermute(sends[0], "tensor", [(i, i + 1) for i in range(step)])
    below = lax.ppermute(sends[1], "tensor", [(i, i - 1) for i in range(count - step, count)])
    return lax.optimization_barrier((above, below))


def slots_sum(product):
    count = lax.axis_size("tensor")
    product = product.reshape(count, product.shape[0] // count, product.shape[1])
    total = product[0].astype(F32)
    for o in range(1, count):
        total = total + lax.ppermute(
            product[o], "tensor", [(i, (i + o) % count) for i in range(count)]
        ).astype(F32)
    return total


def near_bits(axis):
    bits, bit = [], 1
    while bit < lax.axis_size(axis):
        bits.append(bit)
        bit *= 2
    return bits


def half_columns(value, index):
    return lax.dynamic_slice_in_dim(value, index * (value.shape[1] // 2), value.shape[1] // 2, 1)


def in_order(own, other, section, axis):
    return jnp.where(
        section == 0, jnp.concatenate([own, other], axis), jnp.concatenate([other, own], axis)
    )


def gather_half(rows, section):
    own = half_columns(rows, section)
    other = swap(half_columns(rows, 1 - section), "section", 1)
    return jnp.concatenate(from_slots(in_order(own, other, section, 0)), 0)


def whole_rows(total, section):
    rows = total.shape[0] // 2
    own = lax.dynamic_slice_in_dim(total, section * rows, rows, 0)
    other = swap(lax.dynamic_slice_in_dim(total, (1 - section) * rows, rows, 0), "section", 1)
    return in_order(own, other, section, 1)


def both_halves(partial):
    return partial + swap(partial, "section", 1)


def gelu(x):
    return 0.5 * x * (1.0 + jnp.tanh(0.7978845608028654 * (x + 0.044715 * x * x * x)))


def ffn_kernel(ins, order, x_ref, gate_ref, up_ref, down_ref, y_ref, gate, up, hidden):
    step = pl.program_id(0)
    _, blocks, block, _ = x_ref.shape
    rows, depth = blocks * block, gate_ref.shape[0]

    @pl.when(step < ins)
    def _():
        part = x_ref[0].reshape(rows, depth)
        one = jnp.dot(part, gate_ref[...], preferred_element_type=F32)
        two = jnp.dot(part, up_ref[...], preferred_element_type=F32)

        @pl.when(step == 0)
        def _():
            gate[...] = one
            up[...] = two

        @pl.when(step > 0)
        def _():
            gate[...] += one
            up[...] += two

    @pl.when(step == ins)
    def _():
        for slot in range(blocks):
            at = pl.ds(pl.multiple_of(order[1 + slot] * block, block), block)
            hidden[slot * block : (slot + 1) * block, :] = (gelu(gate[at, :]) * up[at, :]).astype(BF16)

    @pl.when(step >= ins)
    def _():
        y_ref[...] = jnp.dot(hidden[...], down_ref[...], preferred_element_type=F32).astype(BF16)


def ffn(x, order, w_gate, w_up, w_down):
    _, blocks, block, features = x.shape
    units = w_gate.shape[1]
    rows, depth, tile = blocks * block, 1024, 1024
    ins, outs = features // depth, features // tile
    return pl.pallas_call(
        functools.partial(ffn_kernel, ins),
        grid_spec=pltpu.PrefetchScalarGridSpec(
            num_scalar_prefetch=1,
            grid=(ins + outs,),
            in_specs=[
                pl.BlockSpec(
                    (1, blocks, block, depth), lambda i, t: (t[0], 0, 0, jnp.minimum(i, ins - 1))
                ),
                pl.BlockSpec(
                    (depth, units), lambda i, t: (jnp.minimum(i, ins - 1), 0)
                ),
                pl.BlockSpec(
                    (depth, units), lambda i, t: (jnp.minimum(i, ins - 1), 0)
                ),
                pl.BlockSpec(
                    (units, tile), lambda i, t: (0, jnp.maximum(i - ins, 0))
                ),
            ],
            out_specs=pl.BlockSpec((rows, tile), lambda i, t: (0, jnp.maximum(i - ins, 0))),
            scratch_shapes=[
                pltpu.VMEM((rows, units), F32),
                pltpu.VMEM((rows, units), F32),
                pltpu.VMEM((rows, units), BF16),
            ],
        ),
        out_shape=jax.ShapeDtypeStruct((rows, features), BF16),
        compiler_params=pltpu.CompilerParams(vmem_limit_bytes=48 * 2**20),
        cost_estimate=pl.CostEstimate(flops=1024, bytes_accessed=1024, transcendentals=0),
        name="ffn",
    )(order, x, w_gate, w_up, w_down)


def attend_kernel(plan, depth, table, mem_ref, cq_ref, *refs):
    locals_, shares, out_ref = refs[:2], refs[2:-1], refs[-1]
    slot = pl.program_id(0)
    groups = len(plan) // 2

    def attend(pieces):
        keys = jnp.zeros((mem_ref.shape[0], HD), F32)
        values = jnp.zeros((mem_ref.shape[0], HD), F32)
        for index, k, v in pieces:
            x = mem_ref[:, pl.ds(pl.multiple_of(table[index] * depth, depth), depth)]
            keys += jnp.dot(x, k, preferred_element_type=F32)
            values += jnp.dot(x, v, preferred_element_type=F32)
        k, v = keys.astype(BF16), values.astype(BF16)
        scores = lax.dot_general(cq_ref[0], k, (((1,), (1,)), ((), ())), preferred_element_type=F32)
        scores = scores * (1.0 / 16.0)
        top = jnp.max(scores, axis=-1, keepdims=True)
        expo = jnp.exp(scores - top)
        total = jnp.sum(expo, axis=-1, keepdims=True)
        context = jnp.dot(expo.astype(BF16), v, preferred_element_type=F32)
        out_ref[0, :, :HD] = context.astype(BF16)
        lanes = lax.broadcasted_iota(jnp.int32, (scores.shape[0], 128), 1)
        high = top.astype(BF16).astype(F32)
        rest = top - high
        middle = rest.astype(BF16).astype(F32)
        sum_high = total.astype(BF16).astype(F32)
        stats = jnp.zeros(lanes.shape, F32)
        for index, piece in enumerate((high, middle, rest - middle, sum_high, total - sum_high)):
            stats = jnp.where(lanes == index, piece, stats)
        out_ref[0, :, HD:] = stats.astype(BF16)

    @pl.when(slot == 0)
    def _():
        attend(
            [
                (2 * groups + place * groups + g, ref[0, g * depth : (g + 1) * depth, :], ref[1, g * depth : (g + 1) * depth, :])
                for place, ref in enumerate(locals_)
                for g in range(groups)
            ]
        )

    @pl.when(slot > 0)
    def _():
        attend([(i, shares[k][0, a], shares[v][0, b]) for i, (k, a, v, b) in enumerate(plan)])


def attend_own_keys(memory, queries, own_head, shares, plan, table):
    rows, features = memory.shape
    heads, count, width = queries.shape
    depth = shares[0].shape[2]
    whole = pl.BlockSpec(own_head[0].shape, lambda h, t: (0, 0, 0), pipeline_mode=pl.Buffered(1))
    return pl.pallas_call(
        functools.partial(attend_kernel, plan, depth),
        grid_spec=pltpu.PrefetchScalarGridSpec(
            num_scalar_prefetch=1,
            grid=(heads,),
            in_specs=[
                pl.BlockSpec((rows, features), lambda h, t: (0, 0)),
                pl.BlockSpec((1, count, width), lambda h, t: (h, 0, 0)),
                whole,
                whole,
            ]
            + [
                pl.BlockSpec((1,) + share.shape[1:], lambda h, t: (jnp.maximum(h - 1, 0), 0, 0, 0))
                for share in shares
            ],
            out_specs=pl.BlockSpec((1, count, width + 128), lambda h, t: (h, 0, 0)),
        ),
        out_shape=jax.ShapeDtypeStruct((heads, count, width + 128), BF16),
        compiler_params=pltpu.CompilerParams(vmem_limit_bytes=30 * 2**20),
        cost_estimate=pl.CostEstimate(flops=1024, bytes_accessed=1024, transcendentals=0),
        name="attend_own_keys",
    )(table, memory, queries, *own_head, *shares)


def merged(contexts, tops, wholes):
    most = functools.reduce(jnp.maximum, tops)
    weights = [jnp.exp(top - most) for top in tops]
    context = sum(c * w for c, w in zip(contexts, weights))
    return context, most, sum(s * w for s, w in zip(wholes, weights))


def per_device(
    source,
    enc_gain,
    w_gate,
    w_up,
    w_down,
    enc_keep,
    final_gain,
    target,
    self_gain,
    self_qkv,
    self_out,
    cross_gain,
    cross_q,
    cross_kv,
    cross_out,
    dec_keep,
):
    section, group = lax.axis_index("section"), lax.axis_index("dp")
    count, tensor = lax.axis_size("tensor"), lax.axis_index("tensor")
    groups = lax.axis_size("dp")
    rows = target.shape[0]
    slot_chip = lax.rem(tensor + jnp.arange(count, dtype=jnp.int32), count)

    selfin = gather_half(norm_rows(target, self_gain).astype(BF16), section)

    normed = norm_rows(source, enc_gain).astype(BF16)
    x = lax.all_gather(normed, ("section", "tensor"), axis=0, tiled=False)
    x = x.reshape((2, count) + normed.shape)
    own_head = [jnp.transpose(cross_kv, (1, 0, 2))]
    own_head.append(swap(own_head[0], "section", 1))

    qkv_w = jnp.transpose(self_qkv, (1, 0, 2))
    q, k, v = [jnp.dot(selfin, qkv_w[i], preferred_element_type=F32) for i in range(3)]
    q, k, v = [y.astype(BF16) for y in both_halves(jnp.stack([q, k, v]))]
    positions = (
        (jnp.arange(2, dtype=jnp.int32)[None, :] * count + slot_chip[:, None])[:, :, None] * rows
        + jnp.arange(rows, dtype=jnp.int32)
    ).reshape(-1)
    scores = lax.dot_general(q, k, (((1,), (1,)), ((), ())), preferred_element_type=F32) * (1.0 / 16.0)
    scores = jnp.where(positions[None, :] <= positions[:, None], scores, F32(-1e30))
    expo = jnp.exp(scores - jnp.max(scores, axis=-1, keepdims=True))
    probs = (expo / jnp.sum(expo, axis=-1, keepdims=True)).astype(BF16)
    context = jnp.dot(probs, v, preferred_element_type=F32).astype(BF16)
    product = jnp.dot(context, self_out, preferred_element_type=F32).astype(BF16)
    total = slots_sum(product)

    mid = (target.astype(F32) + whole_rows(total, section)).astype(BF16)
    crossin = norm_rows(mid, cross_gain).astype(BF16)
    crossin = gather_half(crossin, section)

    cq = both_halves(jnp.dot(crossin, cross_q, preferred_element_type=F32)).astype(BF16)
    cq = jnp.roll(cq.reshape(count, 2, rows, HD), tensor, axis=0)
    cq = jnp.transpose(cq, (1, 0, 2, 3)).reshape(2 * count * rows, HD)
    heads = [0]
    for bit in near_bits("tensor")[::-1]:
        heads += [m ^ bit for m in heads]
    queries = jnp.stack([cq] + [swap(cq, "tensor", m) for m in heads[1:]])
    x, queries, other_head = lax.optimization_barrier((x, queries, own_head[1]))
    own_head[1] = other_head

    depth = cross_kv.shape[0] // groups
    share = lax.dynamic_slice_in_dim(own_head[0], group * depth, depth, 1)[None]
    share, x = lax.optimization_barrier((share, x))
    bits = near_bits("tensor")[::-1]
    for bit in bits[:-1]:
        share = jnp.concatenate([share, swap(share, "tensor", bit)], 0)

    theirs = ffn(x, jnp.concatenate([(1 - section)[None], slot_chip]), w_gate, w_up, w_down)
    theirs, share = lax.optimization_barrier((theirs, share))
    got = swap(theirs, "section", 1)
    x = gated(x, share)
    last = swap(share, "tensor", bits[-1])
    mine = ffn(x, jnp.concatenate([section[None], slot_chip]), w_gate, w_up, w_down)
    mine, last = lax.optimization_barrier((mine, last))
    shares = [jnp.concatenate([share[1:], last], 0)]

    came = sum_step(sum_sends(mine, got, None, 1), 1)
    if groups == 4:
        k, v = shares[0][:, :1], shares[0][:, 1:]
        near = [swap(k, "dp", 1), swap(k, "dp", 2), swap(shares[0], "section", 1)]
        plan = [(0, 0, 0, 1), (1, 0, 3, 0), (2, 0, 4, 0), (5, 0, 6, 0)]
        swapped = []
    else:
        near = [swap(shares[0], "dp", j) for j in range(1, groups)]
        plan = [(j, 0, j, 1) for j in range(groups)]
    for step in range(2, count):
        sends = sum_sends(mine, got, came, step)
        if step == 2:
            held = lax.optimization_barrier(sends + tuple(near))
            if groups == 4:
                sends, shares = held[:2], shares + list(held[2:4])
                near = [swap(v, "dp", 1), swap(v, "dp", 2)]
                swapped = [held[4]] + [swap(y, "section", 1) for y in shares[1:]]
            else:
                sends, shares = held[:2], shares + list(held[2:])
        if step == count - 1 and groups == 4:
            held = lax.optimization_barrier(sends + tuple(near) + tuple(swapped))
            sends, near, swapped = held[:2], list(held[2:4]), list(held[4:])
            shares = shares + near
            passed = [swap(shares[2], "dp", 1), swap(near[0], "dp", 2)]
            swapped += [swap(y, "section", 1) for y in near]
        came = sum_step(sends, step)
    if groups == 4:
        held = lax.optimization_barrier(came + tuple(passed))
        came, shares = held[:2], shares + list(held[2:])
        swapped += [swap(y, "section", 1) for y in held[2:]]
    else:
        swapped = [swap(y, "section", 1) for y in shares]
    total = slot_sum(mine, got, 0) + came[0].astype(F32) + came[1].astype(F32)
    enc_out = (source.astype(F32) + keep_factor(enc_keep) * total).astype(BF16)
    memory = norm_rows(enc_out, final_gain).astype(BF16)

    at = jnp.stack([group ^ j for j in range(groups)])
    places = [section * groups, (1 - section) * groups]
    table = jnp.concatenate(
        [p + at for p in places] + [p + jnp.arange(groups, dtype=jnp.int32) for p in places]
    ).astype(jnp.int32)
    plan += [(k + len(shares), a, v + len(shares), b) for k, a, v, b in plan]
    shares = shares + swapped
    parts = attend_own_keys(memory, queries, own_head, shares, tuple(plan), table)
    parts = [parts[0]] + [
        swap(parts[o], "tensor", heads[o]) for o in range(1, count)
    ]
    parts = [p.astype(F32) for p in parts]
    context, top, whole = merged(
        [p[:, :HD] for p in parts],
        [p[:, HD : HD + 1] + p[:, HD + 1 : HD + 2] + p[:, HD + 2 : HD + 3] for p in parts],
        [p[:, HD + 3 : HD + 4] + p[:, HD + 4 : HD + 5] for p in parts],
    )
    pad = [jnp.broadcast_to(y, (y.shape[0], 128)) for y in (top, whole)]
    other = swap(jnp.concatenate([context] + pad, 1), "section", 1)
    context, top, whole = merged(
        [context, other[:, :HD]], [top, other[:, HD : HD + 1]], [whole, other[:, HD + 128 : HD + 129]]
    )
    context = (context / whole).astype(BF16).reshape(2, count, rows, HD)
    context = jnp.roll(jnp.transpose(context, (1, 0, 2, 3)), -tensor, axis=0).reshape(2 * count * rows, HD)
    product = jnp.dot(context, cross_out, preferred_element_type=F32).astype(BF16)
    crosssum = whole_rows(slots_sum(product), section)
    dec_out = (mid.astype(F32) + keep_factor(dec_keep) * crosssum).astype(BF16)
    return (enc_out, dec_out)


def solution(mesh):
    return jax.shard_map(
        per_device,
        mesh=mesh,
        in_specs=(
            P(("dp", "section", "tensor"), None),
            P(),
            P(None, ("section", "tensor")),
            P(None, ("section", "tensor")),
            P(("section", "tensor"), None),
            P(("dp", "section", "tensor"), None),
            P(),
            P(("dp", "section", "tensor"), None),
            P(),
            P("section", None, "tensor"),
            P("tensor", "section"),
            P(),
            P("section", "tensor"),
            P("section", None, "tensor"),
            P("tensor", "section"),
            P(("dp", "section", "tensor"), None),
        ),
        out_specs=(P(("dp", "section", "tensor"), None), P(("dp", "section", "tensor"), None)),
        check_vma=False,
    )
```

```python
import functools

import jax
import jax.numpy as jnp
from jax import lax
from jax.experimental import pallas as pl
from jax.experimental.pallas import tpu as pltpu
from jax.sharding import PartitionSpec as P

HD = 256
F32 = jnp.float32
BF16 = jnp.bfloat16
STATS = 5


def norm_rows(x, gain):
    values = x.astype(F32)
    power = jnp.mean(values * values, axis=-1, keepdims=True)
    return values * lax.rsqrt(power + 1e-06) * gain


def keep_factor(words):
    shifts = jnp.arange(4, dtype=jnp.int32) * 3
    bits = jnp.right_shift(words[:, None, :], shifts[None, :, None]) & 7
    kept = jnp.where(bits == 7, 0.0, 8.0 / 7.0).astype(F32)
    return kept.reshape(words.shape[0], 4 * words.shape[1])


def swap(value, axis, distance):
    return lax.ppermute(value, axis, [(i, i ^ distance) for i in range(lax.axis_size(axis))])


def from_slots(value):
    count = lax.axis_size("tensor")
    return [value] + [
        lax.ppermute(value, "tensor", [(i, (i - o) % count) for i in range(count)]) for o in range(1, count)
    ]


def gated(value, *others):
    return lax.optimization_barrier((value,) + others)[0]


def slot_sum(mine, got, slot):
    block = mine.shape[0] // lax.axis_size("tensor")
    at = slice(slot * block, (slot + 1) * block)
    return mine[at].astype(F32) + got[at].astype(F32)


def sum_sends(mine, got, came, step):
    up, down = slot_sum(mine, got, lax.axis_size("tensor") - step), slot_sum(mine, got, step)
    if came is not None:
        up, down = up + came[0].astype(F32), down + came[1].astype(F32)
    return up.astype(BF16), down.astype(BF16)


def sum_step(sends, step):
    count = lax.axis_size("tensor")
    above = lax.ppermute(sends[0], "tensor", [(i, i + 1) for i in range(step)])
    below = lax.ppermute(sends[1], "tensor", [(i, i - 1) for i in range(count - step, count)])
    return lax.optimization_barrier((above, below))


def slots_sum(product):
    count = lax.axis_size("tensor")
    product = product.reshape(count, product.shape[0] // count, product.shape[1])
    total = product[0].astype(F32)
    for o in range(1, count):
        total = total + lax.ppermute(
            product[o], "tensor", [(i, (i + o) % count) for i in range(count)]
        ).astype(F32)
    return total


def near_bits(axis):
    bits, bit = [], 1
    while bit < lax.axis_size(axis):
        bits.append(bit)
        bit *= 2
    return bits


def half_columns(value, index):
    return lax.dynamic_slice_in_dim(value, index * (value.shape[1] // 2), value.shape[1] // 2, 1)


def in_order(own, other, section, axis):
    return jnp.where(
        section == 0, jnp.concatenate([own, other], axis), jnp.concatenate([other, own], axis)
    )


def gather_half(rows, section):
    own = half_columns(rows, section)
    other = swap(half_columns(rows, 1 - section), "section", 1)
    return jnp.concatenate(from_slots(in_order(own, other, section, 0)), 0)


def whole_rows(total, section):
    rows = total.shape[0] // 2
    own = lax.dynamic_slice_in_dim(total, section * rows, rows, 0)
    other = swap(lax.dynamic_slice_in_dim(total, (1 - section) * rows, rows, 0), "section", 1)
    return in_order(own, other, section, 1)


def both_halves(partial):
    return partial + swap(partial, "section", 1)


def gelu(x):
    return 0.5 * x * (1.0 + jnp.tanh(0.7978845608028654 * (x + 0.044715 * x * x * x)))


def ffn_kernel(ins, order, x_ref, gate_ref, up_ref, down_ref, y_ref, gate, up, hidden):
    step = pl.program_id(0)
    _, blocks, block, _ = x_ref.shape
    rows, depth = blocks * block, gate_ref.shape[0]

    @pl.when(step < ins)
    def _():
        part = x_ref[0].reshape(rows, depth)
        one = jnp.dot(part, gate_ref[...], preferred_element_type=F32)
        two = jnp.dot(part, up_ref[...], preferred_element_type=F32)

        @pl.when(step == 0)
        def _():
            gate[...] = one
            up[...] = two

        @pl.when(step > 0)
        def _():
            gate[...] += one
            up[...] += two

    @pl.when(step == ins)
    def _():
        for slot in range(blocks):
            at = pl.ds(pl.multiple_of(order[1 + slot] * block, block), block)
            hidden[slot * block : (slot + 1) * block, :] = (gelu(gate[at, :]) * up[at, :]).astype(BF16)

    @pl.when(step >= ins)
    def _():
        y_ref[...] = jnp.dot(hidden[...], down_ref[...], preferred_element_type=F32).astype(BF16)


def ffn(x, order, w_gate, w_up, w_down):
    _, blocks, block, features = x.shape
    units = w_gate.shape[1]
    rows, depth, tile = blocks * block, 1024, 1024
    ins, outs = features // depth, features // tile
    return pl.pallas_call(
        functools.partial(ffn_kernel, ins),
        grid_spec=pltpu.PrefetchScalarGridSpec(
            num_scalar_prefetch=1,
            grid=(ins + outs,),
            in_specs=[
                pl.BlockSpec(
                    (1, blocks, block, depth), lambda i, t: (t[0], 0, 0, jnp.minimum(i, ins - 1))
                ),
                pl.BlockSpec(
                    (depth, units), lambda i, t: (jnp.minimum(i, ins - 1), 0)
                ),
                pl.BlockSpec(
                    (depth, units), lambda i, t: (jnp.minimum(i, ins - 1), 0)
                ),
                pl.BlockSpec(
                    (units, tile), lambda i, t: (0, jnp.maximum(i - ins, 0))
                ),
            ],
            out_specs=pl.BlockSpec((rows, tile), lambda i, t: (0, jnp.maximum(i - ins, 0))),
            scratch_shapes=[
                pltpu.VMEM((rows, units), F32),
                pltpu.VMEM((rows, units), F32),
                pltpu.VMEM((rows, units), BF16),
            ],
        ),
        out_shape=jax.ShapeDtypeStruct((rows, features), BF16),
        compiler_params=pltpu.CompilerParams(vmem_limit_bytes=48 * 2**20),
        cost_estimate=pl.CostEstimate(flops=1024, bytes_accessed=1024, transcendentals=0),
        name="ffn",
    )(order, x, w_gate, w_up, w_down)


def attend_kernel(plan, depth, table, mem_ref, cq_ref, *refs):
    locals_, shares, out_ref = refs[:2], refs[2:-1], refs[-1]
    slot = pl.program_id(0)
    groups = len(plan) // 2

    def attend(pieces):
        keys = jnp.zeros((mem_ref.shape[0], HD), F32)
        values = jnp.zeros((mem_ref.shape[0], HD), F32)
        for index, k, v in pieces:
            x = mem_ref[:, pl.ds(pl.multiple_of(table[index] * depth, depth), depth)]
            keys += jnp.dot(x, k, preferred_element_type=F32)
            values += jnp.dot(x, v, preferred_element_type=F32)
        k, v = keys.astype(BF16), values.astype(BF16)
        scores = lax.dot_general(cq_ref[0], k, (((1,), (1,)), ((), ())), preferred_element_type=F32)
        scores = scores * (1.0 / 16.0)
        top = jnp.max(scores, axis=-1, keepdims=True)
        expo = jnp.exp(scores - top)
        total = jnp.sum(expo, axis=-1, keepdims=True)
        context = jnp.dot(expo.astype(BF16), v, preferred_element_type=F32)
        out_ref[0, :, :HD] = context.astype(BF16)
        lanes = lax.broadcasted_iota(jnp.int32, (scores.shape[0], 128), 1)
        high = top.astype(BF16).astype(F32)
        rest = top - high
        middle = rest.astype(BF16).astype(F32)
        sum_high = total.astype(BF16).astype(F32)
        stats = jnp.zeros(lanes.shape, F32)
        for index, piece in enumerate((high, middle, rest - middle, sum_high, total - sum_high)):
            stats = jnp.where(lanes == index, piece, stats)
        out_ref[0, :, HD:] = stats.astype(BF16)

    @pl.when(slot == 0)
    def _():
        attend(
            [
                (2 * groups + place * groups + g, ref[0, g * depth : (g + 1) * depth, :], ref[1, g * depth : (g + 1) * depth, :])
                for place, ref in enumerate(locals_)
                for g in range(groups)
            ]
        )

    @pl.when(slot > 0)
    def _():
        attend([(i, shares[k][0, a], shares[v][0, b]) for i, (k, a, v, b) in enumerate(plan)])


def attend_own_keys(memory, queries, own_head, shares, plan, table):
    rows, features = memory.shape
    heads, count, width = queries.shape
    depth = shares[0].shape[2]
    whole = pl.BlockSpec(own_head[0].shape, lambda h, t: (0, 0, 0), pipeline_mode=pl.Buffered(1))
    return pl.pallas_call(
        functools.partial(attend_kernel, plan, depth),
        grid_spec=pltpu.PrefetchScalarGridSpec(
            num_scalar_prefetch=1,
            grid=(heads,),
            in_specs=[
                pl.BlockSpec((rows, features), lambda h, t: (0, 0)),
                pl.BlockSpec((1, count, width), lambda h, t: (h, 0, 0)),
                whole,
                whole,
            ]
            + [
                pl.BlockSpec((1,) + share.shape[1:], lambda h, t: (jnp.maximum(h - 1, 0), 0, 0, 0))
                for share in shares
            ],
            out_specs=pl.BlockSpec((1, count, width + 128), lambda h, t: (h, 0, 0)),
        ),
        out_shape=jax.ShapeDtypeStruct((heads, count, width + 128), BF16),
        compiler_params=pltpu.CompilerParams(vmem_limit_bytes=56 * 2**20),
        cost_estimate=pl.CostEstimate(flops=1024, bytes_accessed=1024, transcendentals=0),
        name="attend_own_keys",
    )(table, memory, queries, *own_head, *shares)


def merged(contexts, tops, wholes):
    most = functools.reduce(jnp.maximum, tops)
    weights = [jnp.exp(top - most) for top in tops]
    context = sum(c * w for c, w in zip(contexts, weights))
    return context, most, sum(s * w for s, w in zip(wholes, weights))


def per_device(
    source,
    enc_gain,
    w_gate,
    w_up,
    w_down,
    enc_keep,
    final_gain,
    target,
    self_gain,
    self_qkv,
    self_out,
    cross_gain,
    cross_q,
    cross_kv,
    cross_out,
    dec_keep,
):
    section, group = lax.axis_index("section"), lax.axis_index("dp")
    count, tensor = lax.axis_size("tensor"), lax.axis_index("tensor")
    groups = lax.axis_size("dp")
    rows = target.shape[0]
    slot_chip = lax.rem(tensor + jnp.arange(count, dtype=jnp.int32), count)

    selfin = gather_half(norm_rows(target, self_gain).astype(BF16), section)

    normed = norm_rows(source, enc_gain).astype(BF16)
    x = lax.all_gather(normed, ("section", "tensor"), axis=0, tiled=False)
    x = x.reshape((2, count) + normed.shape)
    own_head = [jnp.transpose(cross_kv, (1, 0, 2))]
    own_head.append(swap(own_head[0], "section", 1))

    qkv_w = jnp.transpose(self_qkv, (1, 0, 2))
    q, k, v = [jnp.dot(selfin, qkv_w[i], preferred_element_type=F32) for i in range(3)]
    q, k, v = [y.astype(BF16) for y in both_halves(jnp.stack([q, k, v]))]
    positions = (
        (jnp.arange(2, dtype=jnp.int32)[None, :] * count + slot_chip[:, None])[:, :, None] * rows
        + jnp.arange(rows, dtype=jnp.int32)
    ).reshape(-1)
    scores = lax.dot_general(q, k, (((1,), (1,)), ((), ())), preferred_element_type=F32) * (1.0 / 16.0)
    scores = jnp.where(positions[None, :] <= positions[:, None], scores, F32(-1e30))
    expo = jnp.exp(scores - jnp.max(scores, axis=-1, keepdims=True))
    probs = (expo / jnp.sum(expo, axis=-1, keepdims=True)).astype(BF16)
    context = jnp.dot(probs, v, preferred_element_type=F32).astype(BF16)
    product = jnp.dot(context, self_out, preferred_element_type=F32).astype(BF16)
    total = slots_sum(product)

    mid = (target.astype(F32) + whole_rows(total, section)).astype(BF16)
    crossin = norm_rows(mid, cross_gain).astype(BF16)
    crossin = gather_half(crossin, section)

    cq = both_halves(jnp.dot(crossin, cross_q, preferred_element_type=F32)).astype(BF16)
    cq = jnp.roll(cq.reshape(count, 2, rows, HD), tensor, axis=0)
    cq = jnp.transpose(cq, (1, 0, 2, 3)).reshape(2 * count * rows, HD)
    heads = [0]
    for bit in near_bits("tensor")[::-1]:
        heads += [m ^ bit for m in heads]
    queries = jnp.stack([cq] + [swap(cq, "tensor", m) for m in heads[1:]])
    x, queries, other_head = lax.optimization_barrier((x, queries, own_head[1]))
    own_head[1] = other_head

    depth = cross_kv.shape[0] // groups
    share = lax.dynamic_slice_in_dim(own_head[0], group * depth, depth, 1)[None]
    share, x = lax.optimization_barrier((share, x))
    bits = near_bits("tensor")[::-1]
    for bit in bits[:-1]:
        share = jnp.concatenate([share, swap(share, "tensor", bit)], 0)

    theirs = ffn(x, jnp.concatenate([(1 - section)[None], slot_chip]), w_gate, w_up, w_down)
    theirs, share = lax.optimization_barrier((theirs, share))
    got = swap(theirs, "section", 1)
    x = gated(x, share)
    last = swap(share, "tensor", bits[-1])
    mine = ffn(x, jnp.concatenate([section[None], slot_chip]), w_gate, w_up, w_down)
    mine, last = lax.optimization_barrier((mine, last))
    shares = [jnp.concatenate([share[1:], last], 0)]

    came = sum_step(sum_sends(mine, got, None, 1), 1)
    if groups == 4:
        k, v = shares[0][:, :1], shares[0][:, 1:]
        near = [swap(k, "dp", 1), swap(k, "dp", 2), swap(shares[0], "section", 1)]
        plan = [(0, 0, 0, 1), (1, 0, 3, 0), (2, 0, 4, 0), (5, 0, 6, 0)]
        swapped = []
    else:
        near = [swap(shares[0], "dp", j) for j in range(1, groups)]
        plan = [(j, 0, j, 1) for j in range(groups)]
    for step in range(2, count):
        sends = sum_sends(mine, got, came, step)
        if step == 2:
            held = lax.optimization_barrier(sends + tuple(near))
            if groups == 4:
                sends, shares = held[:2], shares + list(held[2:4])
                near = [swap(v, "dp", 1), swap(v, "dp", 2)]
                swapped = [held[4]] + [swap(y, "section", 1) for y in shares[1:]]
            else:
                sends, shares = held[:2], shares + list(held[2:])
        if step == count - 1 and groups == 4:
            held = lax.optimization_barrier(sends + tuple(near) + tuple(swapped))
            sends, near, swapped = held[:2], list(held[2:4]), list(held[4:])
            shares = shares + near
            passed = [swap(shares[2], "dp", 1), swap(near[0], "dp", 2)]
            swapped += [swap(y, "section", 1) for y in near]
        came = sum_step(sends, step)
    if groups == 4:
        held = lax.optimization_barrier(came + tuple(passed))
        came, shares = held[:2], shares + list(held[2:])
        swapped += [swap(y, "section", 1) for y in held[2:]]
    else:
        swapped = [swap(y, "section", 1) for y in shares]
    total = slot_sum(mine, got, 0) + came[0].astype(F32) + came[1].astype(F32)
    enc_out = (source.astype(F32) + keep_factor(enc_keep) * total).astype(BF16)
    memory = norm_rows(enc_out, final_gain).astype(BF16)

    at = jnp.stack([group ^ j for j in range(groups)])
    places = [section * groups, (1 - section) * groups]
    table = jnp.concatenate(
        [p + at for p in places] + [p + jnp.arange(groups, dtype=jnp.int32) for p in places]
    ).astype(jnp.int32)
    plan += [(k + len(shares), a, v + len(shares), b) for k, a, v, b in plan]
    shares = shares + swapped
    parts = attend_own_keys(memory, queries, own_head, shares, tuple(plan), table)
    parts = [parts[0]] + [
        swap(parts[o], "tensor", heads[o]) for o in range(1, count)
    ]
    parts = [p.astype(F32) for p in parts]
    context, top, whole = merged(
        [p[:, :HD] for p in parts],
        [p[:, HD : HD + 1] + p[:, HD + 1 : HD + 2] + p[:, HD + 2 : HD + 3] for p in parts],
        [p[:, HD + 3 : HD + 4] + p[:, HD + 4 : HD + 5] for p in parts],
    )
    pad = [jnp.broadcast_to(y, (y.shape[0], 128)) for y in (top, whole)]
    other = swap(jnp.concatenate([context] + pad, 1), "section", 1)
    context, top, whole = merged(
        [context, other[:, :HD]], [top, other[:, HD : HD + 1]], [whole, other[:, HD + 128 : HD + 129]]
    )
    context = (context / whole).astype(BF16).reshape(2, count, rows, HD)
    context = jnp.roll(jnp.transpose(context, (1, 0, 2, 3)), -tensor, axis=0).reshape(2 * count * rows, HD)
    product = jnp.dot(context, cross_out, preferred_element_type=F32).astype(BF16)
    crosssum = whole_rows(slots_sum(product), section)
    dec_out = (mid.astype(F32) + keep_factor(dec_keep) * crosssum).astype(BF16)
    return (enc_out, dec_out)


def solution(mesh):
    return jax.shard_map(
        per_device,
        mesh=mesh,
        in_specs=(
            P(("dp", "section", "tensor"), None),
            P(),
            P(None, ("section", "tensor")),
            P(None, ("section", "tensor")),
            P(("section", "tensor"), None),
            P(("dp", "section", "tensor"), None),
            P(),
            P(("dp", "section", "tensor"), None),
            P(),
            P("section", None, "tensor"),
            P("tensor", "section"),
            P(),
            P("section", "tensor"),
            P("section", None, "tensor"),
            P("tensor", "section"),
            P(("dp", "section", "tensor"), None),
        ),
        out_specs=(P(("dp", "section", "tensor"), None), P(("dp", "section", "tensor"), None)),
        check_vma=False,
    )
```
